32 devices in a mesh: row: 4 (over y, x), col: 8 (over z, core).
Axes of the slice: x: 2, y: 2, z: 4, core: 2. Of those that a mesh axis runs over, the one named last changes fastest.
Arguments:
- latent: bfloat16 [8192, 1408], P(('row', 'col')), may hold values from -6 to 6
- skips: bfloat16 [2, 8192, 1408], P(None, ('row', 'col')), may hold values from -6 to 6
- cond: bfloat16 [8, 1408], P('row'), may hold values from -6 to 6
- text: bfloat16 [8, 333, 1024], P('row', None, 'col'), may hold values from -6 to 6
- skip_gain: float32 [2, 2816], replicated, may hold values from 0.1 to 1.9
- attn_gain: float32 [2, 2, 1408], replicated, may hold values from 0.1 to 1.9
- ffn_gain: float32 [2, 1408], replicated, may hold values from 0.1 to 1.9
- skip_w: bfloat16 [2, 2816, 1408], P(None, 'row', 'col'), may hold values from -0.109375 to 0.109375
- mod_w: bfloat16 [2, 1408, 1408], P(None, 'row', 'col'), may hold values from -0.15625 to 0.15625
- qkv_w: bfloat16 [2, 3, 1408, 1408], P(None, None, 'row', 'col'), may hold values from -0.15625 to 0.15625
- out_w: bfloat16 [2, 1408, 1408], P(None, 'col', 'row'), may hold values from -2.5 to 2.5
- cq_w: bfloat16 [2, 1408, 1408], P(None, 'row', 'col'), may hold values from -0.15625 to 0.15625
- ckv_w: bfloat16 [2, 2, 1024, 1408], P(None, None, 'row', 'col'), may hold values from -0.1875 to 0.1875
- cout_w: bfloat16 [2, 1408, 1408], P(None, 'col', 'row'), may hold values from -1.75 to 1.75
- fc1_w: bfloat16 [2, 1408, 6144], P(None, 'row', 'col'), may hold values from -0.15625 to 0.15625
- fc2_w: bfloat16 [2, 6144, 1408], P(None, 'col', 'row'), may hold values from -0.078125 to 0.078125
- cotangent: bfloat16 [8192, 1408], P(('row', 'col')), may hold values from -6 to 6
Outputs:
- mixed: float32 [8192, 1408], P(('row', 'col'))
- latent_grad: float32 [8192, 1408], P(('row', 'col'))
- skip_grad: float32 [2, 8192, 1408], P(None, ('row', 'col'))
- text_grad: float32 [8, 333, 1024], P('row', None, 'col')
- skip_gain_grad: float32 [2, 2816], replicated
- attn_gain_grad: float32 [2, 2, 1408], replicated
- ffn_gain_grad: float32 [2, 1408], replicated
- skip_w_grad: float32 [2, 2816, 1408], P(None, 'row', 'col')
- mod_w_grad: float32 [2, 1408, 1408], P(None, 'row', 'col')
- qkv_w_grad: float32 [2, 3, 1408, 1408], P(None, None, 'row', 'col')
- out_w_grad: float32 [2, 1408, 1408], P(None, 'col', 'row')
- cq_w_grad: float32 [2, 1408, 1408], P(None, 'row', 'col')
- ckv_w_grad: float32 [2, 2, 1024, 1408], P(None, None, 'row', 'col')
- cout_w_grad: float32 [2, 1408, 1408], P(None, 'col', 'row')
- fc1_w_grad: float32 [2, 1408, 6144], P(None, 'row', 'col')
- fc2_w_grad: float32 [2, 6144, 1408], P(None, 'col', 'row')
The draws below stay inside these ranges and needn't reach their ends.
All inputs are finite; a program needn't handle non-finite values.
Results may differ from the reference program's by a relative error of at most 0.025.
Values may be sent and summed in bfloat16 or wider, within the bound.
A program may use at most 384 MiB of HBM per device.

```python
import jax
import jax.numpy as jnp
from jax import lax

D = 1408
HEADS = 16
HD = 88
FF = 6144
TD = 1024
TXT = 333
SIDE = 32
LAYERS = 2
SEQS_ROW = 2
SEQ = 1024
SEQS = 8
TOKENS = 8192
N_ROW = 4


def block_scale(rng, dims, shards, smallest, largest):
    factor_of, own = 1.0, jax.random.fold_in(rng, 6)
    for position, blocks in shards:
        heights = jnp.exp(jax.random.uniform(jax.random.fold_in(own, position), (blocks,), jnp.float32, smallest / len(shards), largest / len(shards)))
        factor_of = factor_of * jnp.repeat(heights, dims[position] // blocks).reshape([-1 if axis == position else 1 for axis in range(len(dims))])
    return factor_of


def bell_draw(rng, dims, deviation, most, split=(), kind=jnp.bfloat16):
    entries = jax.random.normal(rng, dims, jnp.float32) * deviation
    if len(split) > 0:
        entries = block_scale(rng, dims, split, -0.22, 0.18) * entries
    return jnp.clip(entries, min=-most, max=most).astype(kind)


def setup_inputs(seed: int = 0) -> dict:
    splits = jax.random.split(jax.random.key(seed), 18)
    latent = bell_draw(splits[0], (TOKENS, D), 1.0, 6.0, ((0, 32),))
    skips = bell_draw(splits[1], (LAYERS, TOKENS, D), 1.0, 6.0, ((1, 32),))
    cond = bell_draw(splits[2], (SEQS, D), 1.0, 6.0, ((0, 4),))
    text = bell_draw(splits[3], (SEQS, TXT, TD), 1.0, 6.0, ((0, 4), (2, 8)))
    skip_gain = jnp.clip(1.0 + 0.18 * jax.random.normal(splits[4], (LAYERS, 2 * D), jnp.float32), 0.1, 1.9)
    attn_gain = jnp.clip(1.0 + 0.18 * jax.random.normal(splits[5], (LAYERS, 2, D), jnp.float32), 0.1, 1.9)
    ffn_gain = jnp.clip(1.0 + 0.18 * jax.random.normal(splits[6], (LAYERS, D), jnp.float32), 0.1, 1.9)
    skip_w = bell_draw(splits[7], (LAYERS, 2 * D, D), (2 * D) ** -0.5, 0.109375, ((1, 4), (2, 8)))
    mod_w = bell_draw(splits[8], (LAYERS, D, D), D ** -0.5, 0.15625, ((1, 4), (2, 8)))
    qkv_w = bell_draw(splits[9], (LAYERS, 3, D, D), D ** -0.5, 0.15625, ((2, 4), (3, 8)))
    out_w = bell_draw(splits[10], (LAYERS, D, D), (max(D // 256, 1)) ** -0.5, 2.5, ((1, 8), (2, 4)))
    cq_w = bell_draw(splits[11], (LAYERS, D, D), D ** -0.5, 0.15625, ((1, 4), (2, 8)))
    ckv_w = bell_draw(splits[12], (LAYERS, 2, TD, D), TD ** -0.5, 0.1875, ((2, 4), (3, 8)))
    cout_w = bell_draw(splits[13], (LAYERS, D, D), (max(D // 128, 1)) ** -0.5, 1.75, ((1, 8), (2, 4)))
    fc1_w = bell_draw(splits[14], (LAYERS, D, FF), D ** -0.5, 0.15625, ((1, 4), (2, 8)))
    fc2_w = bell_draw(splits[15], (LAYERS, FF, D), FF ** -0.5, 0.078125, ((1, 8), (2, 4)))
    cotangent = bell_draw(splits[16], (TOKENS, D), 1.0, 6.0, ((0, 32),))
    return dict(latent=latent, skips=skips, cond=cond, text=text, skip_gain=skip_gain, attn_gain=attn_gain, ffn_gain=ffn_gain, skip_w=skip_w, mod_w=mod_w, qkv_w=qkv_w, out_w=out_w, cq_w=cq_w, ckv_w=ckv_w, cout_w=cout_w, fc1_w=fc1_w, fc2_w=fc2_w, cotangent=cotangent)


HIGHEST = lax.Precision.HIGHEST
EPSILON = 1e-06

@jax.custom_vjp
def low(v):
    return lax.optimization_barrier(v.astype(jnp.bfloat16)).astype(jnp.float32)

@jax.custom_vjp
def low_back(v):
    return v

def low_keep(v):
    return (low(v), None)

def low_pass(kept, grad):
    return (grad,)

def back_keep(v):
    return (v, None)

def back_low(kept, grad):
    return (low(grad),)
low.defvjp(low_keep, low_pass)
low_back.defvjp(back_keep, back_low)

def norm_rows(value):
    center = value - lax.optimization_barrier(jnp.mean(value, axis=-1, keepdims=True))
    spread = lax.optimization_barrier(jnp.mean(center * center, axis=-1, keepdims=True))
    return center * lax.rsqrt(spread + EPSILON)

def silu(value):
    return value * jax.nn.sigmoid(value)

def gelu_tanh(value):
    inner = 0.7978845608028654 * (value + 0.044715 * value * value * value)
    return 0.5 * value * (1.0 + jnp.tanh(inner))

def rotary_tables():
    place = jnp.arange(SEQ, dtype=jnp.int32)
    grid_row = (place // SIDE).astype(jnp.float32)
    grid_col = (place % SIDE).astype(jnp.float32)
    pair = jnp.arange(HD // 2, dtype=jnp.int32)
    quarter = HD // 4
    power = (pair % quarter).astype(jnp.float32) * (4.0 / HD)
    freq = jnp.exp(-power * jnp.log(10000.0))
    coordinate = jnp.where(pair[None, :] < quarter, grid_row[:, None], grid_col[:, None])
    angle = coordinate * freq[None, :]
    return (jnp.cos(angle), jnp.sin(angle))

def rotate(value, cos_table, sin_table):
    pairs = value.reshape(value.shape[:-1] + (value.shape[-1] // 2, 2))
    even = pairs[..., 0]
    odd = pairs[..., 1]
    cosine = cos_table[:, None, :]
    sine = sin_table[:, None, :]
    turned = jnp.stack([even * cosine - odd * sine, even * sine + odd * cosine], axis=-1)
    return turned.reshape(value.shape)

def attend(query, keys, values):
    scores = low_back(jnp.einsum('qhe,khe->hqk', query, keys, precision=HIGHEST) * HD ** (-0.5))
    shifted = scores - lax.optimization_barrier(jnp.max(scores, axis=-1, keepdims=True))
    expo = jnp.exp(shifted)
    probs = expo / lax.optimization_barrier(jnp.sum(expo, axis=-1, keepdims=True))
    result = jnp.einsum('hqk,khe->qhe', low(probs), values, precision=HIGHEST)
    return low(low_back(result))

def self_branch(inputs):
    query, keys, values = inputs
    cos_table, sin_table = rotary_tables()
    query_low = low(rotate(norm_rows(query.reshape(SEQ, HEADS, HD)), cos_table, sin_table))
    keys_low = low(rotate(norm_rows(keys.reshape(SEQ, HEADS, HD)), cos_table, sin_table))
    values_low = low(values.reshape(SEQ, HEADS, HD))
    return attend(query_low, keys_low, values_low).reshape(SEQ, D)

def cross_branch(inputs):
    query, keys, values = inputs
    cos_table, sin_table = rotary_tables()
    query_low = low(rotate(norm_rows(query.reshape(SEQ, HEADS, HD)), cos_table, sin_table))
    keys_low = low(norm_rows(keys.reshape(TXT, HEADS, HD)))
    values_low = low(values.reshape(TXT, HEADS, HD))
    return attend(query_low, keys_low, values_low).reshape(SEQ, D)

def block(params, resid, skip_rows, cond, text):
    skip_gain, attn_gain, ffn_gain, skip_w, mod_w, qkv_w, out_w, cq_w, ckv_w, cout_w, fc1_w, fc2_w = params
    groups = cond.shape[0]
    cond_low = low(silu(cond))
    for layer_idx in range(LAYERS):
        joined = jnp.concatenate([resid, skip_rows[layer_idx]], axis=-1)
        skip_low = low(norm_rows(joined) * skip_gain[layer_idx])
        resid_one = low_back(jnp.dot(skip_low, skip_w[layer_idx], precision=HIGHEST))
        shift = low_back(jnp.dot(cond_low, mod_w[layer_idx], precision=HIGHEST))
        first = norm_rows(resid_one) * attn_gain[layer_idx, 0]
        first = (first.reshape(groups, SEQ, D) + shift[:, None, :]).reshape(-1, D)
        first_low = low(first)
        query = low_back(jnp.dot(first_low, qkv_w[layer_idx, 0], precision=HIGHEST))
        keys = low_back(jnp.dot(first_low, qkv_w[layer_idx, 1], precision=HIGHEST))
        values = low_back(jnp.dot(first_low, qkv_w[layer_idx, 2], precision=HIGHEST))
        attended = lax.map(jax.checkpoint(self_branch), (query.reshape(groups, SEQ, D), keys.reshape(groups, SEQ, D), values.reshape(groups, SEQ, D)))
        resid_two = resid_one + low_back(jnp.dot(attended.reshape(-1, D), out_w[layer_idx], precision=HIGHEST))
        third_low = low(norm_rows(resid_two) * attn_gain[layer_idx, 1])
        cross_query = low_back(jnp.dot(third_low, cq_w[layer_idx], precision=HIGHEST))
        text_keys = low_back(jnp.einsum('gnt,tc->gnc', text, ckv_w[layer_idx, 0], precision=HIGHEST))
        text_values = low_back(jnp.einsum('gnt,tc->gnc', text, ckv_w[layer_idx, 1], precision=HIGHEST))
        crossed = lax.map(jax.checkpoint(cross_branch), (cross_query.reshape(groups, SEQ, D), text_keys, text_values))
        resid_three = resid_two + low_back(jnp.dot(crossed.reshape(-1, D), cout_w[layer_idx], precision=HIGHEST))
        second_low = low(norm_rows(resid_three) * ffn_gain[layer_idx])
        hidden = low_back(jnp.dot(second_low, fc1_w[layer_idx], precision=HIGHEST))
        resid = resid_three + low_back(jnp.dot(low(gelu_tanh(hidden)), fc2_w[layer_idx], precision=HIGHEST))
    return resid

def reference(latent, skips, cond, text, skip_gain, attn_gain, ffn_gain, skip_w, mod_w, qkv_w, out_w, cq_w, ckv_w, cout_w, fc1_w, fc2_w, cotangent):
    params = tuple((weight.astype(jnp.float32) for weight in (skip_gain, attn_gain, ffn_gain, skip_w, mod_w, qkv_w, out_w, cq_w, ckv_w, cout_w, fc1_w, fc2_w)))
    group_rows = SEQS_ROW * SEQ
    latent_groups = latent.astype(jnp.float32).reshape(N_ROW, group_rows, D)
    skip_groups = jnp.transpose(skips.astype(jnp.float32).reshape(LAYERS, N_ROW, group_rows, D), (1, 0, 2, 3))
    cond_groups = cond.astype(jnp.float32).reshape(N_ROW, SEQS_ROW, D)
    text_groups = text.astype(jnp.float32).reshape(N_ROW, SEQS_ROW, TXT, TD)
    seed_groups = cotangent.astype(jnp.float32).reshape(N_ROW, group_rows, D)

    def step(total, group):
        latent_part, skip_part, cond_part, text_part, seed_part = group

        def forward(weights, latent_in, skip_in, text_in):
            return block(weights, latent_in, skip_in, cond_part, text_in)
        result, pull = jax.vjp(forward, params, latent_part, skip_part, text_part)
        param_grads, latent_grad, skip_grad, text_grad = pull(seed_part)
        total = jax.tree.map(lambda left, right: left + right, total, param_grads)
        return (total, (result, latent_grad, skip_grad, text_grad))
    zeros = jax.tree.map(jnp.zeros_like, params)
    total, (result, latent_grad, skip_grad, text_grad) = lax.scan(step, zeros, (latent_groups, skip_groups, cond_groups, text_groups, seed_groups))
    mixed = result.reshape(TOKENS, D)
    latent_grad = latent_grad.reshape(TOKENS, D)
    skip_grad = jnp.transpose(skip_grad, (1, 0, 2, 3)).reshape(LAYERS, TOKENS, D)
    text_grad = text_grad.reshape(SEQS, TXT, TD)
    return (mixed, latent_grad, skip_grad, text_grad, total[0], total[1], total[2], total[3], total[4], total[5], total[6], total[7], total[8], total[9], total[10], total[11])
```

```python
import jax
import jax.numpy as jnp
from jax import lax
from jax.sharding import Mesh
from jax.sharding import PartitionSpec as P

HD = 88
SIDE = 32
SEQ = 1024
LATENTS = 2

HIGHEST = lax.Precision.HIGHEST
EPSILON = 1e-06
F32 = jnp.float32
B16 = jnp.bfloat16
SCALE = HD ** (-0.5)


def norm_stats(value):
    center = value - jnp.mean(value, axis=-1, keepdims=True)
    spread = jnp.mean(center * center, axis=-1, keepdims=True)
    rstd = lax.rsqrt(spread + EPSILON)
    return center * rstd, rstd


def norm_back(normed, rstd, grad):
    return rstd * (
        grad
        - jnp.mean(grad, axis=-1, keepdims=True)
        - normed * jnp.mean(grad * normed, axis=-1, keepdims=True)
    )


def silu(value):
    return value * jax.nn.sigmoid(value)


def gelu_tanh(value):
    inner = 0.7978845608028654 * (value + 0.044715 * value * value * value)
    return 0.5 * value * (1.0 + jnp.tanh(inner))


def gelu_grad(value):
    inner = 0.7978845608028654 * (value + 0.044715 * value * value * value)
    tanh = jnp.tanh(inner)
    slope = 0.7978845608028654 * (1.0 + 3.0 * 0.044715 * value * value)
    return 0.5 * (1.0 + tanh) + 0.5 * value * (1.0 - tanh * tanh) * slope


def rotary_tables():
    place = jnp.arange(SEQ, dtype=jnp.int32)
    grid_row = (place // SIDE).astype(F32)
    grid_col = (place % SIDE).astype(F32)
    feature = jnp.arange(HD, dtype=jnp.int32)
    pair = feature // 2
    quarter = HD // 4
    power = (pair % quarter).astype(F32) * (4.0 / HD)
    freq = jnp.exp(-power * jnp.log(10000.0))
    coordinate = jnp.where(pair[:, None] < quarter, grid_row[None, :], grid_col[None, :])
    angle = coordinate * freq[:, None]
    sign = jnp.where(feature % 2 == 0, -1.0, 1.0)[:, None]
    return (jnp.cos(angle), jnp.sin(angle) * sign)


def head_norm(value):
    center = value - jnp.mean(value, axis=1, keepdims=True)
    spread = jnp.mean(center * center, axis=1, keepdims=True)
    rstd = lax.rsqrt(spread + EPSILON)
    return center * rstd, rstd


def head_norm_back(normed, rstd, grad):
    return rstd * (
        grad
        - jnp.mean(grad, axis=1, keepdims=True)
        - normed * jnp.mean(grad * normed, axis=1, keepdims=True)
    )


def swapped(value):
    heads, _, tokens = value.shape
    pairs = value.reshape(heads, HD // 2, 2, tokens)
    return pairs[:, :, ::-1].reshape(value.shape)


def rotate(value, tables):
    return value * tables[0] + swapped(value) * tables[1]


def rotate_back(grad, tables):
    return grad * tables[0] - swapped(grad) * tables[1]


def attention(query, keys, values, tables, rotate_keys):
    query = query.reshape(-1, HD, query.shape[1])
    keys = keys.reshape(-1, HD, keys.shape[1])
    values_low = values.reshape(-1, HD, values.shape[1]).astype(B16)
    query_low = rotate(head_norm(query)[0], tables).astype(B16)
    keys_normed = head_norm(keys)[0]
    keys_low = (rotate(keys_normed, tables) if rotate_keys else keys_normed).astype(B16)
    scores = jnp.einsum("heq,hek->hqk", query_low, keys_low, preferred_element_type=F32) * SCALE
    highest = jnp.max(scores, axis=-1, keepdims=True)
    expo = jnp.exp(scores - highest)
    total = jnp.sum(expo, axis=-1, keepdims=True)
    probs_low = (expo / total).astype(B16)
    result = jnp.einsum("hqk,hek->heq", probs_low, values_low, preferred_element_type=F32)
    return result.astype(B16).reshape(-1, query.shape[2]), (highest + jnp.log(total))[..., 0]


def attention_back(query, keys, values, logsum, grad_low, tables, rotate_keys):
    query = query.reshape(-1, HD, query.shape[1])
    keys = keys.reshape(-1, HD, keys.shape[1])
    values_low = values.reshape(-1, HD, values.shape[1]).astype(B16)
    grad_low = grad_low.reshape(-1, HD, grad_low.shape[1])
    query_normed, query_rstd = head_norm(query)
    keys_normed, keys_rstd = head_norm(keys)
    query_low = rotate(query_normed, tables).astype(B16)
    keys_low = (rotate(keys_normed, tables) if rotate_keys else keys_normed).astype(B16)
    scores = jnp.einsum("heq,hek->hqk", query_low, keys_low, preferred_element_type=F32) * SCALE
    probs = jnp.exp(scores - logsum[..., None])
    probs_low = probs.astype(B16)
    values_grad = jnp.einsum("hqk,heq->hek", probs_low, grad_low, preferred_element_type=F32)
    probs_grad = jnp.einsum("heq,hek->hqk", grad_low, values_low, preferred_element_type=F32)
    scores_grad = probs * (probs_grad - jnp.sum(probs * probs_grad, axis=-1, keepdims=True))
    scores_low = scores_grad.astype(B16)
    query_grad = jnp.einsum("hqk,hek->heq", scores_low, keys_low, preferred_element_type=F32)
    keys_grad = jnp.einsum("hqk,heq->hek", scores_low, query_low, preferred_element_type=F32)
    query_grad = rotate_back(query_grad * SCALE, tables)
    keys_grad = keys_grad * SCALE
    if rotate_keys:
        keys_grad = rotate_back(keys_grad, tables)
    query_grad = head_norm_back(query_normed, query_rstd, query_grad)
    keys_grad = head_norm_back(keys_normed, keys_rstd, keys_grad)
    flat = lambda value: value.reshape(-1, value.shape[2]).astype(B16)
    return flat(query_grad), flat(keys_grad), flat(values_grad)


def dot(left, right, left_dim, right_dim):
    return lax.dot_general(
        left, right, (((left_dim,), (right_dim,)), ((), ())), preferred_element_type=F32
    )


def on_device(
    latent,
    skips,
    cond,
    text,
    skip_gain,
    attn_gain,
    ffn_gain,
    skip_w,
    mod_w,
    qkv_w,
    out_w,
    cq_w,
    ckv_w,
    cout_w,
    fc1_w,
    fc2_w,
    cotangent,
):
    rows = lax.axis_size("row")
    ranks = lax.axis_size("tp")
    row = lax.axis_index("row")
    lat = lax.axis_index("lat")
    rank = lax.axis_index("tp")
    width = latent.shape[1]
    depth = qkv_w.shape[2]
    local = qkv_w.shape[3]
    hidden_local = fc1_w.shape[2]
    layers = skip_w.shape[0]
    text_depth = ckv_w.shape[2]
    text_count = text.shape[1]
    tables = rotary_tables()
    everyone = ("row", "lat", "tp")
    owners = ("lat", "row")

    def gather_tokens(value):
        return lax.all_gather(value, "tp", axis=0, tiled=True)

    def sum_tokens(value):
        return lax.psum_scatter(
            value.astype(B16), "tp", scatter_dimension=0, tiled=True
        ).astype(F32)

    skip_full, attn_full, cross_full, text_full_w, ffn_full = [], [], [], [], []
    for layer in range(layers):
        skip_full.append(
            lax.all_gather(skip_w[layer].T, everyone, axis=0).reshape(rows, width, -1)
        )
        attn_pack = jnp.concatenate(
            [qkv_w[layer, 0], qkv_w[layer, 1], qkv_w[layer, 2], out_w[layer].T], axis=1
        )
        attn_full.append(
            lax.all_gather(attn_pack, owners, axis=0).reshape(LATENTS, width, 4 * local)
        )
        cross_pack = jnp.concatenate([cq_w[layer], cout_w[layer].T], axis=1)
        cross_full.append(
            lax.all_gather(cross_pack, owners, axis=0).reshape(LATENTS, width, 2 * local)
        )
        text_pack = jnp.concatenate([ckv_w[layer, 0], ckv_w[layer, 1]], axis=1)
        text_full_w.append(
            lax.all_gather(text_pack, owners, axis=0).reshape(LATENTS, rows * text_depth, 2 * local)
        )
        ffn_pack = jnp.concatenate([fc1_w[layer], fc2_w[layer].T], axis=1)
        ffn_full.append(
            lax.all_gather(ffn_pack, owners, axis=0).reshape(LATENTS, width, 2 * hidden_local)
        )

    cond_all = lax.all_gather(cond, "row", axis=0, tiled=True)
    cond_low = silu(cond_all.astype(F32)).astype(B16)
    cond_rows = lax.dynamic_slice_in_dim(cond_low, row * depth, depth, axis=1)
    shift_part = jnp.einsum("sd,ldc->lsc", cond_rows, mod_w, preferred_element_type=F32)
    shift_all = jnp.sum(
        lax.all_gather(shift_part, everyone, axis=0).reshape(
            (rows, LATENTS * ranks) + shift_part.shape
        ),
        axis=0,
    )
    own_latent = row * LATENTS + lat
    shift = lax.dynamic_index_in_dim(shift_all, own_latent, axis=2, keepdims=False)
    shift = jnp.transpose(shift, (1, 0, 2)).reshape(layers, width)

    text_parts = lax.all_gather(text, ("lat", "tp"), axis=0)
    text_own = lax.dynamic_index_in_dim(text_parts, lat, axis=1, keepdims=False)
    text_own = jnp.transpose(text_own, (1, 0, 2)).reshape(text_count, -1)

    def split_heads(stack, index):
        return jnp.concatenate(
            [stack[part][index * local : (index + 1) * local] for part in range(LATENTS)], axis=0
        )

    resid = latent.astype(F32)
    saved = []
    for layer in range(layers):
        keep = {}
        joined = jnp.concatenate([resid, skips[layer].astype(F32)], axis=1)
        normed, rstd = norm_stats(joined)
        keep["skip"] = (normed, rstd)
        skip_low = (normed * skip_gain[layer]).astype(B16)
        keep["skip_low"] = skip_low
        resid_one = jnp.einsum(
            "trc,rdc->td",
            skip_low.reshape(skip_low.shape[0], rows, -1),
            skip_full[layer],
            preferred_element_type=F32,
        )
        normed, rstd = norm_stats(resid_one)
        keep["first"] = (normed, rstd)
        first_low = (normed * attn_gain[layer, 0] + shift[layer]).astype(B16)
        first_all = gather_tokens(first_low)
        keep["first_all"] = first_all
        weight = attn_full[layer]
        raw = [dot(weight[part, :, : 3 * local], first_all, 0, 1) for part in range(LATENTS)]
        query, keys, values = (split_heads(raw, index) for index in range(3))
        self_low, self_lse = attention(query, keys, values, tables, True)
        keep["self"] = (query, keys, values, self_lse, self_low)
        out_t = jnp.concatenate([weight[part, :, 3 * local :] for part in range(LATENTS)], axis=1)
        keep["out_t"] = out_t
        resid_two = resid_one + sum_tokens(dot(self_low, out_t, 0, 1))

        normed, rstd = norm_stats(resid_two)
        keep["third"] = (normed, rstd)
        third_low = (normed * attn_gain[layer, 1]).astype(B16)
        third_all = gather_tokens(third_low)
        keep["third_all"] = third_all
        weight = cross_full[layer]
        query_w = jnp.concatenate([weight[part, :, :local] for part in range(LATENTS)], axis=1)
        cout_t = jnp.concatenate([weight[part, :, local:] for part in range(LATENTS)], axis=1)
        keep["cross_w"] = (query_w, cout_t)
        cross_query = dot(query_w, third_all, 0, 1)
        text_raw = [dot(text_full_w[layer][part], text_own, 0, 1) for part in range(LATENTS)]
        text_keys, text_values = (split_heads(text_raw, index) for index in range(2))
        cross_low, cross_lse = attention(cross_query, text_keys, text_values, tables, False)
        keep["cross"] = (cross_query, text_keys, text_values, cross_lse, cross_low)
        resid_three = resid_two + sum_tokens(dot(cross_low, cout_t, 0, 1))

        normed, rstd = norm_stats(resid_three)
        keep["second"] = (normed, rstd)
        second_low = (normed * ffn_gain[layer]).astype(B16)
        second_all = gather_tokens(second_low)
        keep["second_all"] = second_all
        weight = ffn_full[layer]
        hidden = [
            dot(second_all, weight[part, :, :hidden_local], 1, 0) for part in range(LATENTS)
        ]
        act_low = [gelu_tanh(part).astype(B16) for part in hidden]
        keep["hidden"] = hidden
        keep["act"] = act_low
        term = sum(dot(act_low[part], weight[part, :, hidden_local:], 1, 1) for part in range(LATENTS))
        resid = resid_three + sum_tokens(term)
        saved.append(keep)
    mixed = resid

    def scatter_weights(parts):
        packed = parts.astype(B16).reshape(LATENTS * rows, -1, parts.shape[2])
        return lax.psum_scatter(packed, owners, scatter_dimension=0, tiled=False).astype(F32)

    grad = cotangent.astype(F32)
    text_grad = jnp.zeros((text_count, text_own.shape[1]), F32)
    weight_store = [None] * layers
    gain_store = [None] * layers
    skip_store = [None] * layers
    for layer in range(layers - 1, -1, -1):
        keep = saved[layer]
        weight = ffn_full[layer]
        grad_all = gather_tokens(grad.astype(B16))
        ffn_parts = []
        term = None
        for part in range(LATENTS):
            act_grad = dot(grad_all, weight[part, :, hidden_local:], 1, 0)
            hidden_grad = (act_grad * gelu_grad(keep["hidden"][part])).astype(B16)
            down_grad = dot(grad_all, keep["act"][part], 0, 0)
            up_grad = dot(keep["second_all"], hidden_grad, 0, 0)
            piece = dot(hidden_grad, weight[part, :, :hidden_local], 1, 1)
            term = piece if term is None else term + piece
            ffn_parts.append(jnp.concatenate([up_grad, down_grad], axis=1))
        norm_grad = sum_tokens(term)
        ffn_grad = scatter_weights(jnp.stack(ffn_parts))
        normed, rstd = keep["second"]
        gain_ffn = jnp.sum(norm_grad * normed, axis=0)
        grad_three = grad + norm_back(normed, rstd, norm_grad * ffn_gain[layer])

        query_w, cout_t = keep["cross_w"]
        cross_query, text_keys, text_values, cross_lse, cross_low = keep["cross"]
        grad_all = gather_tokens(grad_three.astype(B16))
        out_grad = dot(cout_t, grad_all, 0, 1).astype(B16)
        cout_grad = dot(grad_all, cross_low, 0, 1)
        query_grad, keys_grad, values_grad = attention_back(
            cross_query, text_keys, text_values, cross_lse, out_grad, tables, False
        )
        norm_grad = sum_tokens(dot(query_grad, query_w, 0, 1))
        cq_grad = dot(keep["third_all"], query_grad, 0, 1)
        cross_parts = jnp.stack(
            [
                jnp.concatenate(
                    [
                        cq_grad[:, part * local : (part + 1) * local],
                        cout_grad[:, part * local : (part + 1) * local],
                    ],
                    axis=1,
                )
                for part in range(LATENTS)
            ]
        )
        cross_grad = scatter_weights(cross_parts)
        text_parts_grad = []
        for part in range(LATENTS):
            span = slice(part * local, (part + 1) * local)
            both = jnp.concatenate([keys_grad[span], values_grad[span]], axis=0)
            text_parts_grad.append(dot(text_own, both, 0, 1))
            text_grad = text_grad + dot(both, text_full_w[layer][part], 0, 1)
        ckv_grad = scatter_weights(jnp.stack(text_parts_grad))
        normed, rstd = keep["third"]
        gain_cross = jnp.sum(norm_grad * normed, axis=0)
        grad_two = grad_three + norm_back(normed, rstd, norm_grad * attn_gain[layer, 1])

        weight = attn_full[layer]
        query, keys, values, self_lse, self_low = keep["self"]
        grad_all = gather_tokens(grad_two.astype(B16))
        out_grad = dot(keep["out_t"], grad_all, 0, 1).astype(B16)
        wout_grad = dot(grad_all, self_low, 0, 1)
        three = attention_back(query, keys, values, self_lse, out_grad, tables, True)
        term = None
        attn_parts = []
        for part in range(LATENTS):
            span = slice(part * local, (part + 1) * local)
            both = jnp.concatenate([value[span] for value in three], axis=0)
            piece = dot(both, weight[part, :, : 3 * local], 0, 1)
            term = piece if term is None else term + piece
            attn_parts.append(
                jnp.concatenate(
                    [dot(keep["first_all"], both, 0, 1), wout_grad[:, span]], axis=1
                )
            )
        norm_grad = sum_tokens(term)
        attn_grad = scatter_weights(jnp.stack(attn_parts))
        normed, rstd = keep["first"]
        gain_self = jnp.sum(norm_grad * normed, axis=0)
        shift_own = jnp.sum(norm_grad, axis=0)
        grad_one = grad_two + norm_back(normed, rstd, norm_grad * attn_gain[layer, 0])

        shift_grad = jnp.sum(
            lax.all_gather(shift_own, everyone, axis=0).reshape(rows * LATENTS, ranks, width),
            axis=1,
        )
        column = (lat * ranks + rank) * local
        shift_cols = lax.dynamic_slice_in_dim(shift_grad, column, local, axis=1).astype(B16)
        mod_grad = dot(cond_rows, shift_cols, 0, 0)

        grad_low = grad_one.astype(B16)
        norm_grad = jnp.einsum(
            "td,rdc->trc", grad_low, skip_full[layer], preferred_element_type=F32
        ).reshape(grad_low.shape[0], -1)
        skip_parts = jnp.einsum(
            "td,trc->rdc",
            grad_low,
            keep["skip_low"].reshape(grad_low.shape[0], rows, -1),
            preferred_element_type=F32,
        )
        packed = skip_parts.astype(B16).reshape(rows * LATENTS * ranks, local, -1)
        skip_w_grad = (
            lax.psum_scatter(packed, everyone, scatter_dimension=0, tiled=False).astype(F32).T
        )
        normed, rstd = keep["skip"]
        gain_skip = jnp.sum(norm_grad * normed, axis=0)
        joined_grad = norm_back(normed, rstd, norm_grad * skip_gain[layer])
        grad = joined_grad[:, :width]
        skip_store[layer] = joined_grad[:, width:]
        gain_store[layer] = (gain_skip, jnp.stack([gain_self, gain_cross]), gain_ffn)
        weight_store[layer] = (
            skip_w_grad,
            mod_grad,
            jnp.stack([attn_grad[:, index * local : (index + 1) * local] for index in range(3)]),
            attn_grad[:, 3 * local :].T,
            cross_grad[:, :local],
            jnp.stack([ckv_grad[:, index * local : (index + 1) * local] for index in range(2)]),
            cross_grad[:, local:].T,
            ffn_grad[:, :hidden_local],
            ffn_grad[:, hidden_local:].T,
        )

    weight_outs = tuple(
        jnp.stack([weight_store[layer][slot] for layer in range(layers)]) for slot in range(9)
    )
    gains = tuple(
        jnp.stack([gain_store[layer][slot] for layer in range(layers)]) for slot in range(3)
    )
    gains = lax.psum(gains, everyone)
    blocks = text_grad.astype(B16).reshape(text_count, LATENTS * ranks, -1)
    blocks = jnp.transpose(blocks, (1, 0, 2))
    blocks = lax.all_to_all(blocks, ("lat", "tp"), split_axis=0, concat_axis=0, tiled=True)
    text_out = jnp.sum(
        blocks.astype(F32).reshape((LATENTS, ranks) + blocks.shape[1:]), axis=1
    )
    return (mixed, grad, jnp.stack(skip_store), text_out) + gains + weight_outs


def solution(mesh):
    rows, columns = mesh.shape["row"], mesh.shape["col"]
    grid = Mesh(
        mesh.devices.reshape(rows, LATENTS, columns // LATENTS), ("row", "lat", "tp")
    )
    col = ("lat", "tp")
    tokens = ("row", "lat", "tp")
    return jax.shard_map(
        on_device,
        mesh=grid,
        in_specs=(
            P(tokens, None),
            P(None, tokens, None),
            P("row", None),
            P("row", None, col),
            P(),
            P(),
            P(),
            P(None, "row", col),
            P(None, "row", col),
            P(None, None, "row", col),
            P(None, col, "row"),
            P(None, "row", col),
            P(None, None, "row", col),
            P(None, col, "row"),
            P(None, "row", col),
            P(None, col, "row"),
            P(tokens, None),
        ),
        out_specs=(
            P(tokens, None),
            P(tokens, None),
            P(None, tokens, None),
            P("row", None, col),
            P(),
            P(),
            P(),
            P(None, "row", col),
            P(None, "row", col),
            P(None, None, "row", col),
            P(None, col, "row"),
            P(None, "row", col),
            P(None, None, "row", col),
            P(None, col, "row"),
            P(None, "row", col),
            P(None, col, "row"),
        ),
        check_vma=False,
    )
```

```python
import functools

import jax
import jax.numpy as jnp
from jax import lax
from jax.experimental import pallas as pl
from jax.experimental.pallas import tpu as pltpu
from jax.sharding import Mesh
from jax.sharding import PartitionSpec as P

HD = 88
SIDE = 32
SEQ = 1024
LATENTS = 2

HIGHEST = lax.Precision.HIGHEST
EPSILON = 1e-06
F32 = jnp.float32
B16 = jnp.bfloat16
SCALE = HD ** (-0.5)
VMEM_LIMIT = 48 * 2**20


def norm_stats(value):
    center = value - jnp.mean(value, axis=-1, keepdims=True)
    spread = jnp.mean(center * center, axis=-1, keepdims=True)
    rstd = lax.rsqrt(spread + EPSILON)
    return center * rstd, rstd


def norm_back(normed, rstd, grad):
    return rstd * (
        grad
        - jnp.mean(grad, axis=-1, keepdims=True)
        - normed * jnp.mean(grad * normed, axis=-1, keepdims=True)
    )


def silu(value):
    return value * jax.nn.sigmoid(value)


def gelu_tanh(value):
    inner = 0.7978845608028654 * (value + 0.044715 * value * value * value)
    return 0.5 * value * (1.0 + jnp.tanh(inner))


def gelu_grad(value):
    inner = 0.7978845608028654 * (value + 0.044715 * value * value * value)
    tanh = jnp.tanh(inner)
    slope = 0.7978845608028654 * (1.0 + 3.0 * 0.044715 * value * value)
    return 0.5 * (1.0 + tanh) + 0.5 * value * (1.0 - tanh * tanh) * slope


def rotary_tables():
    place = jnp.arange(SEQ, dtype=jnp.int32)
    grid_row = (place // SIDE).astype(F32)
    grid_col = (place % SIDE).astype(F32)
    feature = jnp.arange(HD, dtype=jnp.int32)
    pair = feature // 2
    quarter = HD // 4
    power = (pair % quarter).astype(F32) * (4.0 / HD)
    freq = jnp.exp(-power * jnp.log(10000.0))
    coordinate = jnp.where(pair[:, None] < quarter, grid_row[None, :], grid_col[None, :])
    angle = coordinate * freq[:, None]
    sign = jnp.where(feature % 2 == 0, -1.0, 1.0)[:, None]
    return (jnp.cos(angle), jnp.sin(angle) * sign)


def swap_rows(value):
    down = pltpu.roll(value, 1, 0)
    up = pltpu.roll(value, value.shape[0] - 1, 0)
    even = lax.broadcasted_iota(jnp.int32, value.shape, 0) % 2 == 0
    return jnp.where(even, up, down)


def head_stats(value):
    center = value - jnp.mean(value, axis=0, keepdims=True)
    rstd = lax.rsqrt(jnp.mean(center * center, axis=0, keepdims=True) + EPSILON)
    return center * rstd, rstd


def head_back(normed, rstd, grad):
    return rstd * (
        grad
        - jnp.mean(grad, axis=0, keepdims=True)
        - normed * jnp.mean(grad * normed, axis=0, keepdims=True)
    )


QUERY_CHUNK = 512


def attention_kernel(
    count, turn, query_ref, keys_ref, values_ref, cos_ref, sin_ref, out_ref, logsum_ref
):
    cos, sin = cos_ref[...], sin_ref[...]
    query = head_stats(query_ref[...])[0]
    query_low = (query * cos + swap_rows(query) * sin).astype(B16)
    keys = head_stats(keys_ref[...])[0]
    if turn:
        keys = keys * cos + swap_rows(keys) * sin
    keys_t = keys.astype(B16).T
    values_low = values_ref[...].astype(B16)
    for start in range(0, query_low.shape[1], QUERY_CHUNK):
        span = slice(start, start + QUERY_CHUNK)
        scores = jnp.dot(keys_t, query_low[:, span], preferred_element_type=F32) * SCALE
        if count < keys_t.shape[0]:
            inside = lax.broadcasted_iota(jnp.int32, scores.shape, 0) < count
            scores = jnp.where(inside, scores, -1e30)
        highest = jnp.max(scores, axis=0, keepdims=True)
        expo = jnp.exp(scores - highest)
        total = jnp.sum(expo, axis=0, keepdims=True)
        probs_low = (expo * (1.0 / total)).astype(B16)
        out = jnp.dot(values_low, probs_low, preferred_element_type=F32)
        out_ref[:, span] = out.astype(B16)
        logsum_ref[0, :, span] = highest + jnp.log(total)


def attention_back_kernel(
    count,
    turn,
    query_ref,
    keys_ref,
    values_ref,
    logsum_ref,
    grad_ref,
    cos_ref,
    sin_ref,
    query_out,
    keys_out,
    values_out,
    keys_sum,
    values_sum,
):
    cos, sin = cos_ref[...], sin_ref[...]
    query, query_rstd = head_stats(query_ref[...])
    query_low = (query * cos + swap_rows(query) * sin).astype(B16)
    keys, keys_rstd = head_stats(keys_ref[...])
    keys_low = (keys * cos + swap_rows(keys) * sin if turn else keys).astype(B16)
    keys_t = keys_low.T
    values_t = values_ref[...].astype(B16).T
    grad = grad_ref[...]
    grad_t = grad.T
    query_t = query_low.T
    query_grad = []
    for start in range(0, query_low.shape[1], QUERY_CHUNK):
        span = slice(start, start + QUERY_CHUNK)
        scores = jnp.dot(keys_t, query_low[:, span], preferred_element_type=F32)
        probs = jnp.exp(scores * SCALE - logsum_ref[0, :, span])
        if count < keys_t.shape[0]:
            inside = lax.broadcasted_iota(jnp.int32, scores.shape, 0) < count
            probs = jnp.where(inside, probs, 0.0)
        values_part = jnp.dot(probs.astype(B16), grad_t[span], preferred_element_type=F32)
        probs_grad = jnp.dot(values_t, grad[:, span], preferred_element_type=F32)
        delta = jnp.sum(probs * probs_grad, axis=0, keepdims=True)
        scores_grad = (probs * (probs_grad - delta)).astype(B16)
        query_grad.append(jnp.dot(keys_low, scores_grad, preferred_element_type=F32))
        keys_part = jnp.dot(scores_grad, query_t[span], preferred_element_type=F32)
        if start == 0:
            values_sum[...] = values_part
            keys_sum[...] = keys_part
        else:
            values_sum[...] += values_part
            keys_sum[...] += keys_part
    grad_query = jnp.concatenate(query_grad, axis=1) * SCALE
    grad_query = grad_query * cos - swap_rows(grad_query) * sin
    query_out[...] = head_back(query, query_rstd, grad_query).astype(B16)
    grad_keys = keys_sum[...].T * SCALE
    if turn:
        grad_keys = grad_keys * cos - swap_rows(grad_keys) * sin
    keys_out[...] = head_back(keys, keys_rstd, grad_keys).astype(B16)
    values_out[...] = values_sum[...].T.astype(B16)


def head_block(columns):
    return pl.BlockSpec((HD, columns), lambda head: (head, 0))


def logsum_block(columns):
    return pl.BlockSpec((1, 1, columns), lambda head: (head, 0, 0))


def attention(query, keys, values, tables, count, turn):
    heads, tokens, others = query.shape[0] // HD, query.shape[1], keys.shape[1]
    table = pl.BlockSpec((HD, tokens), lambda head: (0, 0))
    work = heads * tokens * others
    return pl.pallas_call(
        functools.partial(attention_kernel, count, turn),
        grid=(heads,),
        in_specs=[head_block(tokens), head_block(others), head_block(others), table, table],
        out_specs=[head_block(tokens), logsum_block(tokens)],
        out_shape=[
            jax.ShapeDtypeStruct(query.shape, B16),
            jax.ShapeDtypeStruct((heads, 1, tokens), F32),
        ],
        compiler_params=pltpu.CompilerParams(vmem_limit_bytes=VMEM_LIMIT),
        cost_estimate=pl.CostEstimate(
            flops=4 * HD * work, bytes_accessed=8 * query.size, transcendentals=work
        ),
    )(query, keys, values, *tables)


def attention_back(query, keys, values, logsum, grad_low, tables, count, turn):
    heads, tokens, others = query.shape[0] // HD, query.shape[1], keys.shape[1]
    table = pl.BlockSpec((HD, tokens), lambda head: (0, 0))
    work = heads * tokens * others
    return pl.pallas_call(
        functools.partial(attention_back_kernel, count, turn),
        grid=(heads,),
        in_specs=[
            head_block(tokens),
            head_block(others),
            head_block(others),
            logsum_block(tokens),
            head_block(tokens),
            table,
            table,
        ],
        out_specs=[head_block(tokens), head_block(others), head_block(others)],
        out_shape=[
            jax.ShapeDtypeStruct(value.shape, B16) for value in (query, keys, values)
        ],
        scratch_shapes=[pltpu.VMEM((others, HD), F32), pltpu.VMEM((others, HD), F32)],
        compiler_params=pltpu.CompilerParams(vmem_limit_bytes=VMEM_LIMIT),
        cost_estimate=pl.CostEstimate(
            flops=10 * HD * work, bytes_accessed=16 * query.size, transcendentals=work
        ),
    )(query, keys, values, logsum, grad_low, *tables)


MESH = pl.DeviceIdType.MESH
CHUNKS = 4
NUMBERS = {}


def number_of(name, key):
    return NUMBERS.setdefault((name, key), len(NUMBERS))


def here():
    return lax.axis_index("row"), lax.axis_index("lat"), lax.axis_index("tp")


def device_at(row, lat, rank):
    return {"row": row, "lat": lat, "tp": rank}


def row_peers():
    row, lat, rank = here()
    rows = lax.axis_size("row")
    return [((row + step) % rows, device_at((row + step) % rows, lat, rank)) for step in range(1, rows)]


def peers_along(axis):
    row, lat, rank = here()
    if axis == "lat":
        return lat, LATENTS, [(1 - lat, device_at(row, 1 - lat, rank))]
    fast = lax.axis_size("row") // 2
    slow_at, fast_at = row // fast, row % fast
    if axis == "a":
        other = 1 - slow_at
        return slow_at, 2, [(other, device_at(other * fast + fast_at, lat, rank))]
    others = [(fast_at + step) % fast for step in range(1, fast)]
    return fast_at, fast, [(other, device_at(slow_at * fast + other, lat, rank)) for other in others]


def lat_peer():
    return peers_along("lat")[2][0][1]


def places():
    row, lat, rank = here()
    chips = lax.axis_size("tp") // 2
    chip, core = rank // 2, rank % 2
    sibling = device_at(row, lat, 2 * chip + 1 - core)
    ahead = [(chip + step) % chips for step in range(1, chips)]
    behind = [(chip + chips - step) % chips for step in range(1, chips)]
    return rank, chip, core, sibling, ahead, behind


def chip_peer(chip, core):
    row, lat, _ = here()
    return device_at(row, lat, 2 * chip + core)


def greet(others):
    barrier = pltpu.get_barrier_semaphore()
    for device in others:
        pl.semaphore_signal(barrier, inc=1, device_id=device, device_id_type=MESH)
    pl.semaphore_wait(barrier, len(others))


def remote(source, target, sems, index, device):
    return pltpu.make_async_remote_copy(
        src_ref=source,
        dst_ref=target,
        send_sem=sems.at[0, index],
        recv_sem=sems.at[1, index],
        device_id=device,
        device_id_type=MESH,
    )


def rider_count(axis):
    return {"lat": LATENTS, "a": 2, "b": lax.axis_size("row") // 2}[axis]


def rider_shape(rider):
    kind, axis, place, part, array = rider
    shape = array.shape if part is None else array.shape[1:]
    if kind == "gather":
        shape = shape[:place] + (rider_count(axis),) + shape[place:]
    if kind == "scatter":
        shape = (rider_count(axis) - 1,) + shape[:place] + shape[place + 1 :]
    return jax.ShapeDtypeStruct(shape, array.dtype)


def rider_scratch(modes):
    if not modes:
        return []
    most = sum(rider_count(mode[1]) for mode in modes)
    return [pltpu.SemaphoreType.DMA((2, most)), pltpu.SemaphoreType.DMA((len(modes),))]


def rider_peers(modes, met=()):
    peers = []
    for axis in ("lat", "a", "b"):
        if axis not in met and any(mode[1] == axis for mode in modes):
            peers += [device for _, device in peers_along(axis)[2]]
    return peers


def piece_of(ref, place, index):
    return ref.at[index] if place == 0 else ref.at[:, index]


def start_riders(modes, sources, targets, sems, local_sems):
    copies, index = [], 0
    for order, (mode, source, target) in enumerate(zip(modes, sources, targets)):
        kind, axis, place, part = mode
        me, _, others = peers_along(axis)
        if part is not None:
            source = source.at[part]
        for step, (other, device) in enumerate(others):
            if kind == "swap":
                copies.append(remote(source, target, sems, index, device))
            if kind == "gather":
                copies.append(remote(source, piece_of(target, place, me), sems, index, device))
            if kind == "scatter":
                piece = piece_of(source, place, other)
                copies.append(remote(piece, target.at[step], sems, index, device))
            index += 1
        if kind == "gather":
            own = piece_of(target, place, me)
            copies.append(pltpu.make_async_copy(source, own, local_sems.at[order]))
    for copy in copies:
        copy.start()
    return copies


def split_riders(riders):
    modes = tuple(rider[:4] for rider in riders)
    key = tuple((mode, rider[4].shape) for mode, rider in zip(modes, riders))
    return modes, key, [rider[4] for rider in riders], [rider_shape(rider) for rider in riders]


def swap(array):
    return ("swap", "lat", 0, None, array)


def gather_everyone(source, target, sems, local_sem, between):
    row, lat, _ = here()
    ranks = lax.axis_size("tp")
    rank, chip, core, sibling, ahead, _ = places()
    chips = ranks // 2
    fast_at, fast, fast_peers = peers_along("b")
    slow_at, slow, slow_peers = peers_along("a")
    counter = iter(range(sems.shape[1]))
    sent, last = [], []

    def block(at_row, at_lat, at_rank):
        return target.at[at_row, at_lat * ranks + at_rank]

    def push(piece, device, kept):
        copy = remote(piece, piece, sems, next(counter), device)
        copy.start()
        kept.append(copy)

    def landed(copies):
        for copy in copies:
            copy.wait_recv()
        sent.extend(copies)

    mine = block(row, lat, rank)
    local = pltpu.make_async_copy(source, mine, local_sem.at[0])
    local.start()
    first = remote(source, mine, sems, next(counter), lat_peer())
    first.start()

    def finish():
        local.wait()
        landed([first])
        between()
        step = []
        for place in ahead:
            for at_lat in range(LATENTS):
                push(block(row, at_lat, rank), chip_peer(place, core), step)
        landed(step)
        step = []
        for place in range(chips):
            at_rank = 2 * place + core
            for _, device in fast_peers:
                push(block(row, 0, at_rank), device, step)
            for _, device in slow_peers:
                push(block(row, 1, at_rank), device, step)
        for place in range(chips):
            for at_lat in range(LATENTS):
                push(block(row, at_lat, 2 * place + core), sibling, last)
        landed(step)
        step = []
        for place in range(chips):
            at_rank = 2 * place + core
            for index in range(fast):
                for _, device in slow_peers:
                    push(block(slow_at * fast + index, 0, at_rank), device, step)
            for index in range(slow):
                for _, device in fast_peers:
                    push(block(index * fast + fast_at, 1, at_rank), device, step)
        for place in range(chips):
            at_rank = 2 * place + core
            for index, _ in fast_peers:
                push(block(slow_at * fast + index, 0, at_rank), sibling, last)
            for index, _ in slow_peers:
                push(block(index * fast + fast_at, 1, at_rank), sibling, last)
        landed(step)
        for place in range(chips):
            at_rank = 2 * place + core
            for other, _ in slow_peers:
                for index in range(fast):
                    push(block(other * fast + index, 0, at_rank), sibling, last)
            for other, _ in fast_peers:
                for index in range(slow):
                    push(block(index * fast + other, 1, at_rank), sibling, last)
        for copy in sent:
            copy.wait_send()
        for copy in last:
            copy.wait()

    return finish


def gather_copies():
    rows, chips = lax.axis_size("row"), lax.axis_size("tp") // 2
    fast, slow = rows // 2, 2
    count = 1 + (chips - 1) * LATENTS + chips * (fast - 1 + slow - 1)
    count += chips * (fast * (slow - 1) + slow * (fast - 1))
    return count + chips * LATENTS * rows


def token_kernel(sums, spreads, body, n_in, n_out, modes, shared, *refs):
    refs = list(refs)
    take = lambda count: [refs.pop(0) for _ in range(count)]
    part = refs.pop(0) if sums else None
    ins, sources = take(n_in), take(len(modes))
    block = refs.pop(0) if shared else None
    outs = take(n_out)
    everyone = refs.pop(0) if spreads else None
    targets = take(len(modes))
    blocks = refs.pop(0) if shared else None
    if sums:
        from_sibling, outgoing, incoming, pair_sems, sum_sems = take(5)
    if spreads:
        chip_sems, own_sems, forward_sems = take(3)
    rank, chip, core, sibling, ahead, behind = places()
    chips = len(ahead) + 1
    rows = ins[0].shape[0]
    step = rows // CHUNKS
    spans = [pl.ds(index * step, step) for index in range(CHUNKS)]
    met = [sibling] + [chip_peer(place, core) for place in ahead]
    if shared:
        met += [device for axis in ("lat", "a", "b") for _, device in peers_along(axis)[2]]
    else:
        met += rider_peers(modes)
    greet(met)
    started, riding = [], []

    def ride():
        if modes:
            riding.extend(start_riders(modes, sources, targets, *refs[:2]))

    if shared:
        finish_gather = gather_everyone(block, blocks, *refs[-2:], ride)
    if sums:
        pair = {}
        for order, place in enumerate(ahead + [chip]):
            for index, span in enumerate(spans):
                copy = remote(
                    part.at[2 * place + 1 - core, span],
                    from_sibling.at[order, span],
                    pair_sems,
                    order * CHUNKS + index,
                    sibling,
                )
                copy.start()
                pair[order, index] = copy
        crossing = {}
        for order, place in enumerate(ahead):
            for index, span in enumerate(spans):
                pair[order, index].wait_recv()
                outgoing[order, span] = (
                    part[2 * place + core, span].astype(F32)
                    + from_sibling[order, span].astype(F32)
                ).astype(B16)
                copy = remote(
                    outgoing.at[order, span],
                    incoming.at[order, span],
                    sum_sems,
                    order * CHUNKS + index,
                    chip_peer(place, core),
                )
                copy.start()
                crossing[order, index] = copy
    if not shared:
        ride()
    direct = {}
    for index, span in enumerate(spans):
        total = None
        if sums:
            pair[chips - 1, index].wait_recv()
            total = part[rank, span].astype(F32) + from_sibling[chips - 1, span].astype(F32)
            for order in range(chips - 1):
                crossing[order, index].wait_recv()
                total = total + incoming[order, span].astype(F32)
        low = body(index, span, total, ins, outs)
        if spreads:
            everyone[rank, span] = low
            mine = everyone.at[rank, span]
            for order, place in enumerate(ahead):
                copy = remote(
                    mine, mine, chip_sems, order * CHUNKS + index, chip_peer(place, core)
                )
                copy.start()
                direct[order, index] = copy
            copy = remote(mine, mine, own_sems, index, sibling)
            copy.start()
            started.append(copy)
    if shared:
        finish_gather()
    if spreads:
        for index, span in enumerate(spans):
            for order, place in enumerate(behind):
                direct[order, index].wait_recv()
                landed = everyone.at[2 * place + core, span]
                copy = remote(landed, landed, forward_sems, order * CHUNKS + index, sibling)
                copy.start()
                started.append(copy)
        for copy in direct.values():
            copy.wait_send()
        for copy in started:
            copy.wait()
    if sums:
        for copy in list(pair.values()) + list(crossing.values()):
            copy.wait_send()
    for copy in riding:
        copy.wait()


def comm_params(number):
    return pltpu.CompilerParams(
        collective_id=number, has_side_effects=True, vmem_limit_bytes=VMEM_LIMIT
    )


def token_call(name, body, part, ins, outs, spreads, riders=(), shared=None):
    ranks = lax.axis_size("tp")
    chips = ranks // 2
    rows, width = ins[0].shape
    sums = part is not None
    modes, key, cargo, cargo_shapes = split_riders(riders)
    shapes = [jax.ShapeDtypeStruct(shape, F32) for shape in outs]
    scratch = []
    if sums:
        scratch += [
            pltpu.VMEM((chips, rows, width), B16),
            pltpu.VMEM((chips - 1, rows, width), B16),
            pltpu.VMEM((chips - 1, rows, width), B16),
            pltpu.SemaphoreType.DMA((2, chips * CHUNKS)),
            pltpu.SemaphoreType.DMA((2, (chips - 1) * CHUNKS)),
        ]
    if spreads:
        shapes.append(jax.ShapeDtypeStruct((ranks, rows, width), B16))
        scratch += [
            pltpu.SemaphoreType.DMA((2, (chips - 1) * CHUNKS)),
            pltpu.SemaphoreType.DMA((2, CHUNKS)),
            pltpu.SemaphoreType.DMA((2, (chips - 1) * CHUNKS)),
        ]
    scratch += rider_scratch(modes)
    if shared is not None:
        key = key + shared.shape
        cargo = cargo + [shared]
        blocks = (lax.axis_size("row"), LATENTS * ranks) + shared.shape
        cargo_shapes = cargo_shapes + [jax.ShapeDtypeStruct(blocks, shared.dtype)]
        scratch += [
            pltpu.SemaphoreType.DMA((2, gather_copies())),
            pltpu.SemaphoreType.DMA((1,)),
        ]
    args = ([part.reshape(ranks, rows, width)] if sums else []) + list(ins)
    whole = pl.BlockSpec(memory_space=pltpu.VMEM)
    away = pl.BlockSpec(memory_space=pl.ANY)
    results = pl.pallas_call(
        functools.partial(
            token_kernel, sums, spreads, body, len(ins), len(outs), modes, shared is not None
        ),
        out_shape=shapes + cargo_shapes,
        in_specs=[whole] * len(args) + [away] * len(cargo),
        out_specs=[whole] * len(shapes) + [away] * len(cargo),
        scratch_shapes=scratch,
        name=name,
        compiler_params=comm_params(number_of(name, key)),
        cost_estimate=pl.CostEstimate(
            flops=20 * rows * width, bytes_accessed=12 * rows * width, transcendentals=0
        ),
    )(*args, *cargo)
    results = list(results)
    if spreads:
        place = len(outs)
        results[place] = results[place].reshape(ranks * rows, width)
    return results


def start_kernel(modes, *refs):
    refs = list(refs)
    take = lambda count: [refs.pop(0) for _ in range(count)]
    cond, mod = take(2)
    sources = take(len(modes))
    low_ref, out = take(2)
    targets = take(len(modes))
    got, terms, landed, cond_sems, term_sems, out_sems = take(6)
    row, lat, rank = here()
    rows, ranks = lax.axis_size("row"), lax.axis_size("tp")
    columns = LATENTS * ranks
    column = lat * ranks + rank
    others = row_peers()
    company = []
    for step in range(1, columns):
        place = (column + step) % columns
        company.append(device_at(row, place // ranks, place % ranks))
    greet([device for _, device in others] + company)
    riding = start_riders(modes, sources, targets, *refs) if modes else []
    copies = []
    got[row] = cond[row]
    for index, (other, device) in enumerate(others):
        copy = remote(cond.at[other], got.at[row], cond_sems, index, device)
        copy.start()
        copies.append(copy)
    for copy in copies:
        copy.wait()
    value = got[...]
    low = (value / (1.0 + jnp.exp(-value))).astype(B16)
    low_ref[...] = low.astype(F32)
    flat = low.reshape(rows * 8, low.shape[2])
    first = jnp.dot(flat, mod[0], preferred_element_type=F32)
    second = jnp.dot(flat, mod[1], preferred_element_type=F32)
    upper = lax.broadcasted_iota(jnp.int32, first.shape, 0) % 8 < LATENTS
    terms[...] = jnp.where(upper, first, second).reshape(terms.shape)
    copies = []
    landed[row] = terms[row]
    for index, (other, device) in enumerate(others):
        copy = remote(terms.at[other], landed.at[row], term_sems, index, device)
        copy.start()
        copies.append(copy)
    for copy in copies:
        copy.wait()
    out[column] = jnp.sum(landed[...], axis=0)
    copies = []
    for index, device in enumerate(company):
        copy = remote(out.at[column], out.at[column], out_sems, index, device)
        copy.start()
        copies.append(copy)
    for copy in copies:
        copy.wait()
    for copy in riding:
        copy.wait()


def start_call(cond, mod_w, riders):
    rows, ranks = lax.axis_size("row"), lax.axis_size("tp")
    layers, depth, local = mod_w.shape
    tall, wide = depth + -depth % 128, local + -local % 128
    blocks = jnp.transpose(cond.astype(F32).reshape(LATENTS, rows, depth), (1, 0, 2))
    blocks = jnp.concatenate([blocks] * layers, axis=1)
    blocks = jnp.pad(blocks, ((0, 0), (0, 8 - layers * LATENTS), (0, tall - depth)))
    mod = jnp.pad(mod_w, ((0, 0), (0, tall - depth), (0, wide - local)))
    modes, key, cargo, cargo_shapes = split_riders(riders)
    whole = pl.BlockSpec(memory_space=pltpu.VMEM)
    away = pl.BlockSpec(memory_space=pl.ANY)
    columns = LATENTS * ranks
    low, out, *rest = pl.pallas_call(
        functools.partial(start_kernel, modes),
        out_shape=[
            jax.ShapeDtypeStruct(blocks.shape, F32),
            jax.ShapeDtypeStruct((columns, 8, wide), F32),
        ]
        + cargo_shapes,
        in_specs=[whole] * 2 + [away] * len(cargo),
        out_specs=[whole] * 2 + [away] * len(cargo),
        scratch_shapes=[
            pltpu.VMEM(blocks.shape, F32),
            pltpu.VMEM((rows, 8, wide), F32),
            pltpu.VMEM((rows, 8, wide), F32),
            pltpu.SemaphoreType.DMA((2, rows - 1)),
            pltpu.SemaphoreType.DMA((2, rows - 1)),
            pltpu.SemaphoreType.DMA((2, columns - 1)),
        ]
        + rider_scratch(modes),
        name="shift",
        compiler_params=comm_params(number_of("shift", key)),
    )(blocks, mod, *cargo)
    cond_rows = low[:, :LATENTS, :depth].reshape(rows * LATENTS, depth).astype(B16)
    own = lax.dynamic_index_in_dim(
        out[:, : layers * LATENTS].reshape(columns, layers, LATENTS, wide),
        lax.axis_index("lat"),
        axis=2,
        keepdims=False,
    )
    shift = jnp.transpose(own[:, :, :local], (1, 0, 2)).reshape(layers, columns * local)
    return cond_rows, shift, rest


def end_kernel(modes, *refs):
    refs = list(refs)
    take = lambda count: [refs.pop(0) for _ in range(count)]
    (value,) = take(1)
    sources = take(len(modes))
    (out,) = take(1)
    targets = take(len(modes))
    parts, pair, part_sems, pair_sems, out_sems = take(5)
    row, lat, rank = here()
    ranks = lax.axis_size("tp")
    others = row_peers()
    company = [device_at(row, lat, (rank + step) % ranks) for step in range(1, ranks)]
    greet(company + [lat_peer()] + [device for _, device in others])
    riding = start_riders(modes, sources, targets, *refs) if modes else []
    copies = []
    for index, device in enumerate(company):
        copy = remote(value, parts.at[index], part_sems, index, device)
        copy.start()
        copies.append(copy)
    for copy in copies:
        copy.wait()
    pair[lat] = value[...] + jnp.sum(parts[...], axis=0)
    copy = remote(pair.at[lat], pair.at[lat], pair_sems, 0, lat_peer())
    copy.start()
    copy.wait()
    out[row] = pair[...]
    copies = []
    for index, (_, device) in enumerate(others):
        copy = remote(pair, out.at[row], out_sems, index, device)
        copy.start()
        copies.append(copy)
    for copy in copies:
        copy.wait()
    for copy in riding:
        copy.wait()


def end_call(value, riders):
    rows, ranks = lax.axis_size("row"), lax.axis_size("tp")
    modes, key, cargo, cargo_shapes = split_riders(riders)
    whole = pl.BlockSpec(memory_space=pltpu.VMEM)
    away = pl.BlockSpec(memory_space=pl.ANY)
    return pl.pallas_call(
        functools.partial(end_kernel, modes),
        out_shape=[jax.ShapeDtypeStruct((rows, LATENTS) + value.shape, F32)]
        + cargo_shapes,
        in_specs=[whole] + [away] * len(cargo),
        out_specs=[whole] + [away] * len(cargo),
        scratch_shapes=[
            pltpu.VMEM((ranks - 1,) + value.shape, F32),
            pltpu.VMEM((LATENTS,) + value.shape, F32),
            pltpu.SemaphoreType.DMA((2, ranks - 1)),
            pltpu.SemaphoreType.DMA((2, 1)),
            pltpu.SemaphoreType.DMA((2, rows - 1)),
        ]
        + rider_scratch(modes),
        name="gains",
        compiler_params=comm_params(number_of("gains", key)),
    )(value, *cargo)


def first_body(index, span, total, ins, outs):
    resid, gain, shift = ins
    return (norm_stats(resid[span])[0] * gain[...] + shift[...]).astype(B16)


def middle_body(index, span, total, ins, outs):
    resid, gain = ins
    value = resid[span] + total
    outs[0][span] = value
    return (norm_stats(value)[0] * gain[...]).astype(B16)


def last_body(index, span, total, ins, outs):
    outs[0][span] = ins[0][span] + total
    return None


def spread_body(index, span, total, ins, outs):
    return ins[0][span].astype(B16)


def add_rows(out, index, value):
    value = jnp.sum(value, axis=0, keepdims=True)
    if index == 0:
        out[...] = value
    else:
        out[...] += value


def back_body(index, span, total, ins, outs):
    grad, resid, gain = ins
    normed, rstd = norm_stats(resid[span])
    value = grad[span] + norm_back(normed, rstd, total * gain[...])
    outs[0][span] = value
    add_rows(outs[1], index, total * normed)
    return value.astype(B16)


def back_last_body(index, span, total, ins, outs):
    back_body(index, span, total, ins, outs)
    add_rows(outs[2], index, total)
    return None


def first_tokens(resid, gain, shift, riders=()):
    return token_call("first", first_body, None, [resid, gain, shift], [], True, riders)


def middle_tokens(part, resid, gain, riders=()):
    ins = [resid, gain]
    return token_call("middle", middle_body, part, ins, [resid.shape], True, riders)


def last_tokens(part, resid, riders=()):
    return token_call("last", last_body, part, [resid], [resid.shape], False, riders)


def spread_tokens(grad, riders=(), shared=None):
    return token_call("spread", spread_body, None, [grad], [], True, riders, shared)


def back_tokens(part, grad, resid, gain, riders=()):
    shapes = [grad.shape, gain.shape]
    ins = [grad, resid, gain]
    return token_call("back", back_body, part, ins, shapes, True, riders)


def back_last_tokens(part, grad, resid, gain, riders=()):
    shapes = [grad.shape, gain.shape, gain.shape]
    ins = [grad, resid, gain]
    return token_call("back_last", back_last_body, part, ins, shapes, False, riders)


def dot(left, right, left_dim, right_dim):
    return lax.dot_general(
        left, right, (((left_dim,), (right_dim,)), ((), ())), preferred_element_type=F32
    )


def skip_kernel(resid_ref, skip_ref, gain_ref, weight_ref, low_ref, out_ref):
    tokens, width = resid_ref.shape
    parts, _, depth = weight_ref.shape
    step = tokens // CHUNKS
    for index in range(CHUNKS):
        span = pl.ds(index * step, step)
        joined = jnp.concatenate([resid_ref[span], skip_ref[span].astype(F32)], axis=1)
        low_ref[span] = (norm_stats(joined)[0] * gain_ref[...]).astype(B16)
    for part in range(parts):
        low = low_ref[:, part * depth : (part + 1) * depth]
        term = dot(low, weight_ref[part], 1, 1)
        if part == 0:
            out_ref[...] = term
        else:
            out_ref[...] += term


def skip_back_kernel(
    grad_ref, low_ref, resid_ref, skip_ref, gain_ref, weight_ref, weight_out, resid_out, skip_out, gain_out, norm_grad
):
    tokens, width = resid_ref.shape
    parts, _, depth = weight_ref.shape
    step = tokens // CHUNKS
    grad_low = grad_ref[...].astype(B16)
    grad_t = grad_low.T
    for part in range(parts):
        columns = slice(part * depth, (part + 1) * depth)
        weight_out[part] = dot(grad_t, low_ref[:, columns], 1, 0).astype(B16)
        norm_grad[:, columns] = dot(grad_low, weight_ref[part], 1, 0)
    for index in range(CHUNKS):
        span = pl.ds(index * step, step)
        joined = jnp.concatenate([resid_ref[span], skip_ref[span].astype(F32)], axis=1)
        normed, rstd = norm_stats(joined)
        grad = norm_grad[span]
        add_rows(gain_out, index, grad * normed)
        value = norm_back(normed, rstd, grad * gain_ref[...])
        resid_out[span] = value[:, :width]
        skip_out[span] = value[:, width:]


def local_call(name, body, args, shapes, scratch=()):
    return pl.pallas_call(
        body,
        out_shape=shapes,
        in_specs=[pl.BlockSpec(memory_space=pltpu.VMEM)] * len(args),
        out_specs=[pl.BlockSpec(memory_space=pltpu.VMEM)] * len(shapes),
        scratch_shapes=list(scratch),
        name=name,
        compiler_params=pltpu.CompilerParams(vmem_limit_bytes=VMEM_LIMIT),
    )(*args)


def skip_forward(resid, skip, gain, weight):
    tokens, width = resid.shape
    shapes = [
        jax.ShapeDtypeStruct((tokens, 2 * width), B16),
        jax.ShapeDtypeStruct((tokens, width), F32),
    ]
    return local_call("skip", skip_kernel, [resid, skip, gain, weight], shapes)


def skip_backward(grad, low, resid, skip, gain, weight):
    tokens, width = resid.shape
    shapes = [
        jax.ShapeDtypeStruct(weight.shape, B16),
        jax.ShapeDtypeStruct(resid.shape, F32),
        jax.ShapeDtypeStruct(resid.shape, F32),
        jax.ShapeDtypeStruct(gain.shape, F32),
    ]
    scratch = [pltpu.VMEM((tokens, 2 * width), F32)]
    args = [grad, low, resid, skip, gain, weight]
    return local_call("skip_back", skip_back_kernel, args, shapes, scratch)


def on_device(
    latent,
    skips,
    cond,
    text,
    skip_gain,
    attn_gain,
    ffn_gain,
    skip_w,
    mod_w,
    qkv_w,
    out_w,
    cq_w,
    ckv_w,
    cout_w,
    fc1_w,
    fc2_w,
    cotangent,
):
    rows = lax.axis_size("row")
    ranks = lax.axis_size("tp")
    row = lax.axis_index("row")
    lat = lax.axis_index("lat")
    rank = lax.axis_index("tp")
    width = latent.shape[1]
    depth = qkv_w.shape[2]
    local = qkv_w.shape[3]
    hidden_local = fc1_w.shape[2]
    layers = skip_w.shape[0]
    text_depth = ckv_w.shape[2]
    text_count = text.shape[1]
    tables = rotary_tables()
    everyone = ("row", "lat", "tp")


    def gather_both(pack, other, sizes):
        low, high = jnp.where(lat == 0, pack, other), jnp.where(lat == 0, other, pack)
        pieces, start = [], 0
        for size in sizes:
            pieces += [low[:, start : start + size], high[:, start : start + size]]
            start += size
        return lax.all_gather(jnp.concatenate(pieces, axis=1), "row", axis=0, tiled=True)

    attn_pack, cross_pack, text_pack, up_pack, down_pack = [], [], [], [], []
    attn_full, cross_full, text_full_w = [], [], []
    for layer in range(layers):
        attn_pack.append(
            jnp.concatenate(
                [qkv_w[layer, 0], qkv_w[layer, 1], qkv_w[layer, 2], out_w[layer].T], axis=1
            )
        )
        cross_pack.append(jnp.concatenate([cq_w[layer], cout_w[layer].T], axis=1))
        text_pack.append(jnp.concatenate([ckv_w[layer, 0], ckv_w[layer, 1]], axis=1))
        up_pack.append(fc1_w[layer])
        down_pack.append(fc2_w[layer].T)

    cond_rows, shift, others = start_call(
        cond, mod_w, [swap(attn_pack[0])]
    )
    attn_full.append(gather_both(attn_pack[0], others[0], [local] * 4))


    def stack(array):
        return [("gather", "lat", 0, None, array)]

    def gather_one(array):
        return [("gather", "b", 0, 0, array), ("gather", "a", 0, 1, array)]

    def gather_two(halves):
        return [("gather", "a", 0, None, halves[0]), ("gather", "b", 1, None, halves[1])]

    def whole(halves):
        return [half.reshape(width, -1) for half in halves]

    grad = cotangent.astype(F32)
    grad_all, cross_other, text_other, up_stack, skip_blocks = spread_tokens(
        grad, [swap(cross_pack[0]), swap(text_pack[0])] + stack(up_pack[0]), skip_w[0].T
    )
    skip_full = [skip_blocks.reshape(rows, width, -1)]
    down_stack = down_half = None

    def own_text(text):
        text_parts = lax.all_gather(text, ("lat", "tp"), axis=0)
        text_own = lax.dynamic_index_in_dim(text_parts, lat, axis=1, keepdims=False)
        text_own = jnp.transpose(text_own, (1, 0, 2)).reshape(text_count, -1)
        return jnp.pad(text_own, ((0, -text_count % 128), (0, 0)))

    wide = LATENTS * local

    def thirds(stack, count):
        return [stack[index * wide : (index + 1) * wide] for index in range(count)]

    resid = latent.astype(F32)
    saved = []
    for layer in range(layers):
        keep = {}
        keep["skip_in"] = resid
        keep["skip_low"], resid_one = skip_forward(
            resid, skips[layer], skip_gain[layer : layer + 1], skip_full[layer]
        )
        keep["first"] = resid_one
        following = layer + 1 < layers
        if layer == 0:
            riders = gather_one(up_stack) + stack(down_pack[0])
        else:
            riders = [swap(cross_pack[layer]), swap(text_pack[layer])]
        first_all, *others = first_tokens(
            resid_one, attn_gain[layer, 0:1], shift[layer : layer + 1], riders
        )
        if layer == 0:
            up_half, down_stack = others[:2], others[2]
            text, cross_other, text_other, first_all = lax.optimization_barrier(
                (text, cross_other, text_other, first_all)
            )
            text_own = own_text(text)
        else:
            cross_other, text_other = others
        cross_full.append(gather_both(cross_pack[layer], cross_other, [local] * 2))
        text_full_w.append(gather_both(text_pack[layer], text_other, [local] * 2))
        keep["first_all"] = first_all
        weight = attn_full[layer]
        query, keys, values = thirds(dot(weight[:, : 3 * wide], first_all, 0, 1), 3)
        self_low, self_lse = attention(query, keys, values, tables, SEQ, True)
        keep["self"] = (query, keys, values, self_lse, self_low)
        out_t = weight[:, 3 * wide :]
        keep["out_t"] = out_t
        if following:
            skip_next, self_low = lax.optimization_barrier((skip_w[layer + 1].T, self_low))
            skip_full.append(
                lax.all_gather(skip_next, everyone, axis=0).reshape(rows, width, -1)
            )
        riders = gather_two(up_half) + gather_one(down_stack)
        if following:
            riders.append(swap(attn_pack[layer + 1]))
        resid_two, third_all, *others = middle_tokens(
            dot(self_low, out_t, 0, 1).astype(B16), resid_one, attn_gain[layer, 1:2], riders
        )
        up_w, down_half = whole(others[:2]), others[2:4]
        if following:
            attn_full.append(gather_both(attn_pack[layer + 1], others[4], [local] * 4))
        keep["third"] = resid_two
        keep["third_all"] = third_all
        weight = cross_full[layer]
        query_w, cout_t = weight[:, :wide], weight[:, wide:]
        keep["cross_w"] = (query_w, cout_t)
        cross_query = dot(query_w, third_all, 0, 1)
        text_keys, text_values = thirds(dot(text_full_w[layer], text_own, 0, 1), 2)
        cross_low, cross_lse = attention(
            cross_query, text_keys, text_values, tables, text_count, False
        )
        keep["cross"] = (cross_query, text_keys, text_values, cross_lse, cross_low)
        riders = gather_two(down_half) + (stack(up_pack[layer + 1]) if following else [])
        resid_three, second_all, *others = middle_tokens(
            dot(cross_low, cout_t, 0, 1).astype(B16),
            resid_two,
            ffn_gain[layer : layer + 1],
            riders,
        )
        down_w = whole(others[:2])
        if following:
            up_stack = others[2]
        keep["second"] = resid_three
        keep["second_all"] = second_all
        hidden = [dot(second_all, up_w[part], 1, 0) for part in range(LATENTS)]
        act_low = [gelu_tanh(part).astype(B16) for part in hidden]
        keep["hidden"] = hidden
        keep["act"] = act_low
        keep["ffn_w"] = (up_w, down_w)
        term = sum(dot(act_low[part], down_w[part], 1, 1) for part in range(LATENTS))
        riders = gather_one(up_stack) + stack(down_pack[layer + 1]) if following else []
        term = term.astype(B16)
        if following:
            resid, *others = last_tokens(term, resid_three, riders)
        if following:
            up_half, down_stack = others[:2], others[2]
        saved.append(keep)

    final_term, final_resid = term, resid_three

    def sum_over_rows(parts, counts):
        pieces = []
        for part, count in zip(parts, counts):
            pieces += [
                part[:, index * local : (index + 1) * local].astype(B16)
                for index in range(LATENTS * count)
            ]
        packed = jnp.concatenate(pieces[0::2] + pieces[1::2], axis=1)
        summed = lax.psum_scatter(packed, "row", scatter_dimension=0, tiled=True)
        half = summed.shape[1] // 2
        low, high = summed[:, :half], summed[:, half:]
        return jnp.where(lat == 0, low, high), jnp.where(lat == 0, high, low)

    def finish(mine, other):
        total = mine.astype(F32) + other.astype(F32)
        return [
            total[:, start : start + local] for start in range(0, total.shape[1], local)
        ]

    fast = rows // 2
    slow_at, fast_at = row // fast, row % fast

    def by_rows(value):
        return value.astype(B16).reshape(2, fast, -1, value.shape[1])

    def pick(value, index, axis):
        return lax.dynamic_index_in_dim(value, index, axis=axis, keepdims=False).astype(F32)

    def scatter_one(halves):
        return [("scatter", "a", 0, None, halves[0]), ("scatter", "b", 1, None, halves[1])]

    def added_one(halves, arrived):
        low = pick(halves[0], slow_at, 0) + jnp.sum(arrived[0].astype(F32), axis=0)
        high = pick(halves[1], fast_at, 1) + jnp.sum(arrived[1].astype(F32), axis=0)
        return [low.astype(B16), high.astype(B16)]

    def scatter_two(halves):
        return [("scatter", "b", 0, None, halves[0]), ("scatter", "a", 0, None, halves[1])]

    def added_two(halves, arrived):
        low = pick(halves[0], fast_at, 0) + jnp.sum(arrived[0].astype(F32), axis=0)
        high = pick(halves[1], slow_at, 0) + jnp.sum(arrived[1].astype(F32), axis=0)
        mine = jnp.where(lat == 0, low, high)
        return mine, jnp.where(lat == 0, high, low).astype(B16)

    text_grad = jnp.zeros(text_own.shape, F32)
    weight_store = [None] * layers
    gain_store = [None] * layers
    skip_store = [None] * layers
    shift_store = [None] * layers
    waiting = None
    for layer in range(layers - 1, -1, -1):
        keep = saved[layer]
        up_w, down_w = keep["ffn_w"]
        if waiting is not None:
            grad_all, other = spread_tokens(grad, [swap(waiting["down"][1])])
            waiting["store"]["down"] = waiting["down"][0] + other.astype(F32)
        ups, downs = [], []
        term = None
        for part in range(LATENTS):
            act_grad = dot(grad_all, down_w[part], 1, 0)
            hidden_grad = (act_grad * gelu_grad(keep["hidden"][part])).astype(B16)
            downs.append(by_rows(dot(grad_all, keep["act"][part], 0, 0)))
            ups.append(by_rows(dot(keep["second_all"], hidden_grad, 0, 0)))
            piece = dot(hidden_grad, up_w[part], 1, 1)
            term = piece if term is None else term + piece
        riders = scatter_one(ups)
        names = ("attn", "cross", "text")
        if waiting is not None:
            riders += [swap(waiting[name][1]) for name in names]
        grad_three, gain_ffn, grad_all, *others = back_tokens(
            term.astype(B16), grad, keep["second"], ffn_gain[layer : layer + 1], riders
        )
        ups = added_one(ups, others[:2])
        if waiting is not None:
            for name, other in zip(names, others[2:]):
                waiting["store"][name] = finish(waiting[name][0], other)

        query_w, cout_t = keep["cross_w"]
        cross_query, text_keys, text_values, cross_lse, cross_low = keep["cross"]
        out_grad = dot(cout_t, grad_all, 0, 1).astype(B16)
        cout_grad = dot(grad_all, cross_low, 0, 1)
        query_grad, keys_grad, values_grad = attention_back(
            cross_query, text_keys, text_values, cross_lse, out_grad, tables, text_count, False
        )
        cq_grad = dot(keep["third_all"], query_grad, 0, 1)
        cross_sum = sum_over_rows([cq_grad, cout_grad], [1, 1])
        both = jnp.concatenate([keys_grad, values_grad], axis=0)
        text_sum = sum_over_rows([dot(text_own, both, 0, 1)], [2])
        text_grad = text_grad + dot(both, text_full_w[layer], 0, 1)
        riders = scatter_two(ups) + scatter_one(downs)
        if waiting is not None:
            query_grad, waiting["store"]["skip"] = lax.optimization_barrier(
                (query_grad, waiting["store"]["skip"])
            )
        grad_two, gain_cross, grad_all, *others = back_tokens(
            dot(query_grad, query_w, 0, 1).astype(B16),
            grad_three,
            keep["third"],
            attn_gain[layer, 1:2],
            riders,
        )
        up_mine, up_theirs = added_two(ups, others[:2])
        downs = added_one(downs, others[2:])

        weight = attn_full[layer]
        query, keys, values, self_lse, self_low = keep["self"]
        out_grad = dot(keep["out_t"], grad_all, 0, 1).astype(B16)
        wout_grad = dot(grad_all, self_low, 0, 1)
        three = attention_back(query, keys, values, self_lse, out_grad, tables, SEQ, True)
        both = jnp.concatenate(three, axis=0)
        term = dot(both, weight[:, : 3 * wide], 0, 1)
        qkv_grad = dot(keep["first_all"], both, 0, 1)
        grad_one, gain_self, shift_own, *others = back_last_tokens(
            term.astype(B16),
            grad_two,
            keep["first"],
            attn_gain[layer, 0:1],
            scatter_two(downs) + [swap(up_theirs)],
        )
        down_sum = added_two(downs, others[:2])
        up_grad = up_mine + others[2].astype(F32)
        attn_sum = sum_over_rows([qkv_grad, wout_grad], [3, 1])

        packed, grad, skip_store[layer], gain_skip = skip_backward(
            grad_one,
            keep["skip_low"],
            keep["skip_in"],
            skips[layer],
            skip_gain[layer : layer + 1],
            skip_full[layer],
        )
        packed = packed.reshape(rows * LATENTS * ranks, local, -1)
        skip_sum = lax.psum_scatter(packed, everyone, scatter_dimension=0, tiled=False)
        gain_store[layer] = (gain_skip[0], jnp.concatenate([gain_self, gain_cross]), gain_ffn[0])
        store = dict(skip=skip_sum, up=up_grad)
        waiting = dict(attn=attn_sum, cross=cross_sum, text=text_sum, down=down_sum, store=store)
        weight_store[layer] = store
        shift_store[layer] = shift_own

    sizes = [gain_store[0][slot].size for slot in range(3)] + [width]
    flat = jnp.concatenate(
        [
            gain_store[layer][slot].reshape(-1)
            for slot in range(3)
            for layer in range(layers)
        ]
        + [shift_store[layer].reshape(-1) for layer in range(layers)]
    )
    flat = jnp.pad(flat, (0, -flat.size % 1024)).reshape(-1, 128)
    flat_all, down_other, *others = end_call(
        flat, [swap(waiting[name][1]) for name in ("down",) + names]
    )
    waiting["store"]["down"] = waiting["down"][0] + down_other.astype(F32)
    for name, other in zip(names, others):
        waiting["store"][name] = finish(waiting[name][0], other)
    final_term, text_grad, flat_all = lax.optimization_barrier((final_term, text_grad, flat_all))
    mixed = last_tokens(final_term, final_resid)[0]
    flat_all = flat_all.reshape(rows * LATENTS, -1)
    totals = jnp.sum(flat_all, axis=0)
    gains, start = [], 0
    for slot in range(3):
        size = layers * sizes[slot]
        gains.append(
            totals[start : start + size].reshape((layers,) + gain_store[0][slot].shape)
        )
        start += size
    shift_grad = flat_all[:, start : start + layers * width].reshape(-1, layers, width)
    column = (lat * ranks + rank) * local
    shift_cols = lax.dynamic_slice_in_dim(shift_grad, column, local, axis=2).astype(B16)

    weight_store = [
        (
            store["skip"].astype(F32).T,
            dot(cond_rows, shift_cols[:, layer], 0, 0),
            jnp.stack(store["attn"][:3]),
            store["attn"][3].T,
            store["cross"][0],
            jnp.stack(store["text"]),
            store["cross"][1].T,
            store["up"],
            store["down"].T,
        )
        for layer, store in enumerate(weight_store)
    ]
    weight_outs = tuple(
        jnp.stack([weight_store[layer][slot] for layer in range(layers)]) for slot in range(9)
    )
    blocks = text_grad[:text_count].astype(B16).reshape(text_count, LATENTS * ranks, -1)
    blocks = jnp.transpose(blocks, (1, 0, 2))
    blocks = lax.all_to_all(blocks, ("lat", "tp"), split_axis=0, concat_axis=0, tiled=True)
    text_out = jnp.sum(
        blocks.astype(F32).reshape((LATENTS, ranks) + blocks.shape[1:]), axis=1
    )
    return (mixed, grad, jnp.stack(skip_store), text_out) + tuple(gains) + weight_outs


def solution(mesh):
    NUMBERS.clear()
    rows, columns = mesh.shape["row"], mesh.shape["col"]
    grid = Mesh(
        mesh.devices.reshape(rows, LATENTS, columns // LATENTS), ("row", "lat", "tp")
    )
    col = ("lat", "tp")
    tokens = ("row", "lat", "tp")
    return jax.shard_map(
        on_device,
        mesh=grid,
        in_specs=(
            P(tokens, None),
            P(None, tokens, None),
            P("row", None),
            P("row", None, col),
            P(),
            P(),
            P(),
            P(None, "row", col),
            P(None, "row", col),
            P(None, None, "row", col),
            P(None, col, "row"),
            P(None, "row", col),
            P(None, None, "row", col),
            P(None, col, "row"),
            P(None, "row", col),
            P(None, col, "row"),
            P(tokens, None),
        ),
        out_specs=(
            P(tokens, None),
            P(tokens, None),
            P(None, tokens, None),
            P("row", None, col),
            P(),
            P(),
            P(),
            P(None, "row", col),
            P(None, "row", col),
            P(None, None, "row", col),
            P(None, col, "row"),
            P(None, "row", col),
            P(None, None, "row", col),
            P(None, col, "row"),
            P(None, "row", col),
            P(None, col, "row"),
        ),
        check_vma=False,
    )
```

```python
import functools

import jax
import jax.numpy as jnp
from jax import lax
from jax.experimental import pallas as pl
from jax.experimental.pallas import tpu as pltpu
from jax.sharding import Mesh
from jax.sharding import PartitionSpec as P

HD = 88
SIDE = 32
SEQ = 1024
LATENTS = 2

HIGHEST = lax.Precision.HIGHEST
EPSILON = 1e-06
F32 = jnp.float32
B16 = jnp.bfloat16
SCALE = HD ** (-0.5)
VMEM_LIMIT = 48 * 2**20


def norm_stats(value):
    center = value - jnp.mean(value, axis=-1, keepdims=True)
    spread = jnp.mean(center * center, axis=-1, keepdims=True)
    rstd = lax.rsqrt(spread + EPSILON)
    return center * rstd, rstd


def norm_back(normed, rstd, grad):
    return rstd * (
        grad
        - jnp.mean(grad, axis=-1, keepdims=True)
        - normed * jnp.mean(grad * normed, axis=-1, keepdims=True)
    )


def silu(value):
    return value * jax.nn.sigmoid(value)


def gelu_tanh(value):
    inner = 0.7978845608028654 * (value + 0.044715 * value * value * value)
    return 0.5 * value * (1.0 + jnp.tanh(inner))


def gelu_grad(value):
    inner = 0.7978845608028654 * (value + 0.044715 * value * value * value)
    tanh = jnp.tanh(inner)
    slope = 0.7978845608028654 * (1.0 + 3.0 * 0.044715 * value * value)
    return 0.5 * (1.0 + tanh) + 0.5 * value * (1.0 - tanh * tanh) * slope


def rotary_tables():
    place = jnp.arange(SEQ, dtype=jnp.int32)
    grid_row = (place // SIDE).astype(F32)
    grid_col = (place % SIDE).astype(F32)
    feature = jnp.arange(HD, dtype=jnp.int32)
    pair = feature // 2
    quarter = HD // 4
    power = (pair % quarter).astype(F32) * (4.0 / HD)
    freq = jnp.exp(-power * jnp.log(10000.0))
    coordinate = jnp.where(pair[:, None] < quarter, grid_row[None, :], grid_col[None, :])
    angle = coordinate * freq[:, None]
    sign = jnp.where(feature % 2 == 0, -1.0, 1.0)[:, None]
    return (jnp.cos(angle), jnp.sin(angle) * sign)


def swap_rows(value):
    down = pltpu.roll(value, 1, 0)
    up = pltpu.roll(value, value.shape[0] - 1, 0)
    even = lax.broadcasted_iota(jnp.int32, value.shape, 0) % 2 == 0
    return jnp.where(even, up, down)


def head_stats(value):
    center = value - jnp.mean(value, axis=0, keepdims=True)
    rstd = lax.rsqrt(jnp.mean(center * center, axis=0, keepdims=True) + EPSILON)
    return center * rstd, rstd


def head_back(normed, rstd, grad):
    return rstd * (
        grad
        - jnp.mean(grad, axis=0, keepdims=True)
        - normed * jnp.mean(grad * normed, axis=0, keepdims=True)
    )


QUERY_CHUNK = 512


def attention_kernel(
    count, turn, query_ref, keys_ref, values_ref, cos_ref, sin_ref, out_ref, logsum_ref
):
    cos, sin = cos_ref[...], sin_ref[...]
    query = head_stats(query_ref[...])[0]
    query_low = (query * cos + swap_rows(query) * sin).astype(B16)
    keys = head_stats(keys_ref[...])[0]
    if turn:
        keys = keys * cos + swap_rows(keys) * sin
    keys_t = keys.astype(B16).T
    values_low = values_ref[...].astype(B16)
    for start in range(0, query_low.shape[1], QUERY_CHUNK):
        span = slice(start, start + QUERY_CHUNK)
        scores = jnp.dot(keys_t, query_low[:, span], preferred_element_type=F32) * SCALE
        if count < keys_t.shape[0]:
            inside = lax.broadcasted_iota(jnp.int32, scores.shape, 0) < count
            scores = jnp.where(inside, scores, -1e30)
        highest = jnp.max(scores, axis=0, keepdims=True)
        expo = jnp.exp(scores - highest)
        total = jnp.sum(expo, axis=0, keepdims=True)
        probs_low = (expo * (1.0 / total)).astype(B16)
        out = jnp.dot(values_low, probs_low, preferred_element_type=F32)
        out_ref[:, span] = out.astype(B16)
        logsum_ref[0, :, span] = highest + jnp.log(total)


def attention_back_kernel(
    count,
    turn,
    query_ref,
    keys_ref,
    values_ref,
    logsum_ref,
    grad_ref,
    cos_ref,
    sin_ref,
    query_out,
    keys_out,
    values_out,
    keys_sum,
    values_sum,
):
    cos, sin = cos_ref[...], sin_ref[...]
    query, query_rstd = head_stats(query_ref[...])
    query_low = (query * cos + swap_rows(query) * sin).astype(B16)
    keys, keys_rstd = head_stats(keys_ref[...])
    keys_low = (keys * cos + swap_rows(keys) * sin if turn else keys).astype(B16)
    keys_t = keys_low.T
    values_t = values_ref[...].astype(B16).T
    grad = grad_ref[...]
    grad_t = grad.T
    query_t = query_low.T
    query_grad = []
    for start in range(0, query_low.shape[1], QUERY_CHUNK):
        span = slice(start, start + QUERY_CHUNK)
        scores = jnp.dot(keys_t, query_low[:, span], preferred_element_type=F32)
        probs = jnp.exp(scores * SCALE - logsum_ref[0, :, span])
        if count < keys_t.shape[0]:
            inside = lax.broadcasted_iota(jnp.int32, scores.shape, 0) < count
            probs = jnp.where(inside, probs, 0.0)
        values_part = jnp.dot(probs.astype(B16), grad_t[span], preferred_element_type=F32)
        probs_grad = jnp.dot(values_t, grad[:, span], preferred_element_type=F32)
        delta = jnp.sum(probs * probs_grad, axis=0, keepdims=True)
        scores_grad = (probs * (probs_grad - delta)).astype(B16)
        query_grad.append(jnp.dot(keys_low, scores_grad, preferred_element_type=F32))
        keys_part = jnp.dot(scores_grad, query_t[span], preferred_element_type=F32)
        if start == 0:
            values_sum[...] = values_part
            keys_sum[...] = keys_part
        else:
            values_sum[...] += values_part
            keys_sum[...] += keys_part
    grad_query = jnp.concatenate(query_grad, axis=1) * SCALE
    grad_query = grad_query * cos - swap_rows(grad_query) * sin
    query_out[...] = head_back(query, query_rstd, grad_query).astype(B16)
    grad_keys = keys_sum[...].T * SCALE
    if turn:
        grad_keys = grad_keys * cos - swap_rows(grad_keys) * sin
    keys_out[...] = head_back(keys, keys_rstd, grad_keys).astype(B16)
    values_out[...] = values_sum[...].T.astype(B16)


def head_block(columns):
    return pl.BlockSpec((HD, columns), lambda head: (head, 0))


def logsum_block(columns):
    return pl.BlockSpec((1, 1, columns), lambda head: (head, 0, 0))


def attention(query, keys, values, tables, count, turn):
    heads, tokens, others = query.shape[0] // HD, query.shape[1], keys.shape[1]
    table = pl.BlockSpec((HD, tokens), lambda head: (0, 0))
    work = heads * tokens * others
    return pl.pallas_call(
        functools.partial(attention_kernel, count, turn),
        grid=(heads,),
        in_specs=[head_block(tokens), head_block(others), head_block(others), table, table],
        out_specs=[head_block(tokens), logsum_block(tokens)],
        out_shape=[
            jax.ShapeDtypeStruct(query.shape, B16),
            jax.ShapeDtypeStruct((heads, 1, tokens), F32),
        ],
        compiler_params=pltpu.CompilerParams(vmem_limit_bytes=VMEM_LIMIT),
        cost_estimate=pl.CostEstimate(
            flops=4 * HD * work, bytes_accessed=8 * query.size, transcendentals=work
        ),
    )(query, keys, values, *tables)


def attention_back(query, keys, values, logsum, grad_low, tables, count, turn):
    heads, tokens, others = query.shape[0] // HD, query.shape[1], keys.shape[1]
    table = pl.BlockSpec((HD, tokens), lambda head: (0, 0))
    work = heads * tokens * others
    return pl.pallas_call(
        functools.partial(attention_back_kernel, count, turn),
        grid=(heads,),
        in_specs=[
            head_block(tokens),
            head_block(others),
            head_block(others),
            logsum_block(tokens),
            head_block(tokens),
            table,
            table,
        ],
        out_specs=[head_block(tokens), head_block(others), head_block(others)],
        out_shape=[
            jax.ShapeDtypeStruct(value.shape, B16) for value in (query, keys, values)
        ],
        scratch_shapes=[pltpu.VMEM((others, HD), F32), pltpu.VMEM((others, HD), F32)],
        compiler_params=pltpu.CompilerParams(vmem_limit_bytes=VMEM_LIMIT),
        cost_estimate=pl.CostEstimate(
            flops=10 * HD * work, bytes_accessed=16 * query.size, transcendentals=work
        ),
    )(query, keys, values, logsum, grad_low, *tables)


MESH = pl.DeviceIdType.MESH
CHUNKS = 4
NUMBERS = {}


def number_of(name, key):
    return NUMBERS.setdefault((name, key), len(NUMBERS))


def here():
    rank = 2 * lax.axis_index("chip") + lax.axis_index("core")
    return lax.axis_index("row"), lax.axis_index("lat"), rank


def rank_count():
    return 2 * lax.axis_size("chip")


def device_at(row, lat, rank):
    return {"row": row, "lat": lat, "chip": rank // 2, "core": rank % 2}


def row_peers():
    row, lat, rank = here()
    rows = lax.axis_size("row")
    return [((row + step) % rows, device_at((row + step) % rows, lat, rank)) for step in range(1, rows)]


def peers_along(axis):
    row, lat, rank = here()
    if axis == "core":
        other = 1 - rank % 2
        return rank % 2, 2, [(other, device_at(row, lat, rank // 2 * 2 + other))]
    if axis == "chip":
        count = rank_count() // 2
        me = rank // 2
        places = [(me + step) % count for step in range(1, count)]
        return me, count, [(place, device_at(row, lat, 2 * place + rank % 2)) for place in places]
    if axis == "lat":
        return lat, LATENTS, [(1 - lat, device_at(row, 1 - lat, rank))]
    fast = lax.axis_size("row") // 2
    slow_at, fast_at = row // fast, row % fast
    if axis == "a":
        other = 1 - slow_at
        return slow_at, 2, [(other, device_at(other * fast + fast_at, lat, rank))]
    others = [(fast_at + step) % fast for step in range(1, fast)]
    return fast_at, fast, [(other, device_at(slow_at * fast + other, lat, rank)) for other in others]


def lat_peer():
    return peers_along("lat")[2][0][1]


def places():
    row, lat, rank = here()
    chips = rank_count() // 2
    chip, core = rank // 2, rank % 2
    sibling = device_at(row, lat, 2 * chip + 1 - core)
    ahead = [(chip + step) % chips for step in range(1, chips)]
    behind = [(chip + chips - step) % chips for step in range(1, chips)]
    return rank, chip, core, sibling, ahead, behind


def chip_peer(chip, core):
    row, lat, _ = here()
    return device_at(row, lat, 2 * chip + core)


def greet(others):
    barrier = pltpu.get_barrier_semaphore()
    for device in others:
        pl.semaphore_signal(barrier, inc=1, device_id=device, device_id_type=MESH)
    pl.semaphore_wait(barrier, len(others))


def remote(source, target, sems, index, device):
    return pltpu.make_async_remote_copy(
        src_ref=source,
        dst_ref=target,
        send_sem=sems.at[0, index],
        recv_sem=sems.at[1, index],
        device_id=device,
        device_id_type=MESH,
    )


def rider_count(axis):
    counts = {"lat": LATENTS, "a": 2, "b": lax.axis_size("row") // 2, "chip": rank_count() // 2}
    return counts[axis]


def rider_shape(rider):
    kind, axis, place, part, array = rider
    shape = array.shape if part is None else array.shape[1:]
    if kind == "gather":
        shape = shape[:place] + (rider_count(axis),) + shape[place:]
    if kind == "scatter":
        shape = (rider_count(axis) - 1,) + shape[:place] + shape[place + 1 :]
    return jax.ShapeDtypeStruct(shape, array.dtype)


def rider_scratch(modes):
    if not modes:
        return []
    most = sum(rider_count(mode[1]) for mode in modes)
    return [pltpu.SemaphoreType.DMA((2, most)), pltpu.SemaphoreType.DMA((len(modes),))]


def rider_peers(modes, met=()):
    peers = []
    for axis in ("lat", "a", "b"):
        if axis not in met and any(mode[1] == axis for mode in modes):
            peers += [device for _, device in peers_along(axis)[2]]
    return peers


def piece_of(ref, place, index):
    return ref.at[index] if place == 0 else ref.at[:, index]


def start_riders(modes, sources, targets, sems, local_sems):
    copies, index = [], 0
    for order, (mode, source, target) in enumerate(zip(modes, sources, targets)):
        kind, axis, place, part = mode
        me, _, others = peers_along(axis)
        if part is not None:
            source = source.at[part]
        for step, (other, device) in enumerate(others):
            if kind == "swap":
                copies.append(remote(source, target, sems, index, device))
            if kind == "gather":
                copies.append(remote(source, piece_of(target, place, me), sems, index, device))
            if kind == "scatter":
                piece = piece_of(source, place, other)
                copies.append(remote(piece, target.at[step], sems, index, device))
            index += 1
        if kind == "gather":
            own = piece_of(target, place, me)
            copies.append(pltpu.make_async_copy(source, own, local_sems.at[order]))
    for copy in copies:
        copy.start()
    return copies


def split_riders(riders):
    modes = tuple(rider[:4] for rider in riders)
    key = tuple((mode, rider[4].shape) for mode, rider in zip(modes, riders))
    return modes, key, [rider[4] for rider in riders], [rider_shape(rider) for rider in riders]


def swap(array):
    return ("swap", "lat", 0, None, array)


def gather_everyone(source, target, sems, local_sem, between):
    row, lat, _ = here()
    ranks = rank_count()
    rank, chip, core, sibling, ahead, _ = places()
    chips = ranks // 2
    fast_at, fast, fast_peers = peers_along("b")
    slow_at, slow, slow_peers = peers_along("a")
    counter = iter(range(sems.shape[1]))
    sent, last = [], []

    def block(at_row, at_lat, at_rank):
        return target.at[at_row, at_lat * ranks + at_rank]

    def push(piece, device, kept):
        copy = remote(piece, piece, sems, next(counter), device)
        copy.start()
        kept.append(copy)

    def landed(copies):
        for copy in copies:
            copy.wait_recv()
        sent.extend(copies)

    mine = block(row, lat, rank)
    local = pltpu.make_async_copy(source, mine, local_sem.at[0])
    local.start()
    first = remote(source, mine, sems, next(counter), lat_peer())
    first.start()

    def finish():
        local.wait()
        landed([first])
        between()
        step = []
        for place in ahead:
            for at_lat in range(LATENTS):
                push(block(row, at_lat, rank), chip_peer(place, core), step)
        landed(step)
        step = []
        for place in range(chips):
            at_rank = 2 * place + core
            for _, device in fast_peers:
                push(block(row, 0, at_rank), device, step)
            for _, device in slow_peers:
                push(block(row, 1, at_rank), device, step)
        for place in range(chips):
            for at_lat in range(LATENTS):
                push(block(row, at_lat, 2 * place + core), sibling, last)
        landed(step)
        step = []
        for place in range(chips):
            at_rank = 2 * place + core
            for index in range(fast):
                for _, device in slow_peers:
                    push(block(slow_at * fast + index, 0, at_rank), device, step)
            for index in range(slow):
                for _, device in fast_peers:
                    push(block(index * fast + fast_at, 1, at_rank), device, step)
        for place in range(chips):
            at_rank = 2 * place + core
            for index, _ in fast_peers:
                push(block(slow_at * fast + index, 0, at_rank), sibling, last)
            for index, _ in slow_peers:
                push(block(index * fast + fast_at, 1, at_rank), sibling, last)
        landed(step)
        for place in range(chips):
            at_rank = 2 * place + core
            for other, _ in slow_peers:
                for index in range(fast):
                    push(block(other * fast + index, 0, at_rank), sibling, last)
            for other, _ in fast_peers:
                for index in range(slow):
                    push(block(index * fast + other, 1, at_rank), sibling, last)
        for copy in sent:
            copy.wait_send()
        for copy in last:
            copy.wait()

    return finish


def gather_copies():
    rows, chips = lax.axis_size("row"), rank_count() // 2
    fast, slow = rows // 2, 2
    count = 1 + (chips - 1) * LATENTS + chips * (fast - 1 + slow - 1)
    count += chips * (fast * (slow - 1) + slow * (fast - 1))
    return count + chips * LATENTS * rows


def token_kernel(sums, spreads, body, n_in, n_out, modes, shared, *refs):
    refs = list(refs)
    take = lambda count: [refs.pop(0) for _ in range(count)]
    if sums:
        lefts, rights = take(sums[1]), take(sums[1])
    ins, sources = take(n_in), take(len(modes))
    block = refs.pop(0) if shared else None
    outs = take(n_out)
    everyone = refs.pop(0) if spreads else None
    targets = take(len(modes))
    blocks = refs.pop(0) if shared else None
    if sums:
        part, from_sibling, outgoing, incoming, pair_sems, sum_sems = take(6)
        if sums[0]:
            turned = take(1)
            turned[0][...] = lefts[0][...].T
            lefts = turned
    if spreads:
        chip_sems, own_sems, forward_sems = take(3)
    rank, chip, core, sibling, ahead, behind = places()
    chips = len(ahead) + 1
    rows = ins[0].shape[0]
    step = rows // CHUNKS
    spans = [pl.ds(index * step, step) for index in range(CHUNKS)]
    met = [sibling] + [chip_peer(place, core) for place in ahead]
    if shared:
        met += [device for axis in ("lat", "a", "b") for _, device in peers_along(axis)[2]]
    else:
        met += rider_peers(modes)
    greet(met)
    started, riding = [], []

    def multiply(place):
        some = pl.ds(pl.multiple_of(place * rows, 128), rows)
        term = None
        for left, right in zip(lefts, rights):
            piece = dot(left[some], right[...], 1, 1)
            term = piece if term is None else term + piece
        part[place] = term.astype(B16)


    def ride():
        if modes:
            riding.extend(start_riders(modes, sources, targets, *refs[:2]))

    if shared:
        finish_gather = gather_everyone(block, blocks, *refs[-2:], ride)
    if sums:
        pair = {}
        for order, place in enumerate(ahead + [chip]):
            multiply(2 * place + 1 - core)
            for index, span in enumerate(spans):
                copy = remote(
                    part.at[2 * place + 1 - core, span],
                    from_sibling.at[order, span],
                    pair_sems,
                    order * CHUNKS + index,
                    sibling,
                )
                copy.start()
                pair[order, index] = copy
        crossing = {}
        for order, place in enumerate(ahead):
            multiply(2 * place + core)
            for index, span in enumerate(spans):
                pair[order, index].wait_recv()
                outgoing[order, span] = (
                    part[2 * place + core, span].astype(F32)
                    + from_sibling[order, span].astype(F32)
                ).astype(B16)
                copy = remote(
                    outgoing.at[order, span],
                    incoming.at[order, span],
                    sum_sems,
                    order * CHUNKS + index,
                    chip_peer(place, core),
                )
                copy.start()
                crossing[order, index] = copy
    if not shared:
        ride()
    if sums:
        multiply(rank)
    direct = {}
    for index, span in enumerate(spans):
        total = None
        if sums:
            pair[chips - 1, index].wait_recv()
            total = part[rank, span].astype(F32) + from_sibling[chips - 1, span].astype(F32)
            for order in range(chips - 1):
                crossing[order, index].wait_recv()
                total = total + incoming[order, span].astype(F32)
        low = body(index, span, total, ins, outs)
        if spreads:
            everyone[rank, span] = low
            mine = everyone.at[rank, span]
            for order, place in enumerate(ahead):
                copy = remote(
                    mine, mine, chip_sems, order * CHUNKS + index, chip_peer(place, core)
                )
                copy.start()
                direct[order, index] = copy
            copy = remote(mine, mine, own_sems, index, sibling)
            copy.start()
            started.append(copy)
    if shared:
        finish_gather()
    if spreads:
        for index, span in enumerate(spans):
            for order, place in enumerate(behind):
                direct[order, index].wait_recv()
                landed = everyone.at[2 * place + core, span]
                copy = remote(landed, landed, forward_sems, order * CHUNKS + index, sibling)
                copy.start()
                started.append(copy)
        for copy in direct.values():
            copy.wait_send()
        for copy in started:
            copy.wait()
    if sums:
        for copy in list(pair.values()) + list(crossing.values()):
            copy.wait_send()
    for copy in riding:
        copy.wait()


def comm_params(number):
    return pltpu.CompilerParams(
        collective_id=number, has_side_effects=True, vmem_limit_bytes=VMEM_LIMIT
    )


def token_call(name, body, part, ins, outs, spreads, riders=(), shared=None):
    ranks = rank_count()
    chips = ranks // 2
    rows, width = ins[0].shape
    sums = None
    if part is not None:
        turn, lefts, rights = part
        sums = (turn, len(lefts))
    modes, key, cargo, cargo_shapes = split_riders(riders)
    shapes = [jax.ShapeDtypeStruct(shape, F32) for shape in outs]
    scratch = []
    if sums:
        key = key + tuple(left.shape for left in lefts)
        scratch += [
            pltpu.VMEM((ranks, rows, width), B16),
            pltpu.VMEM((chips, rows, width), B16),
            pltpu.VMEM((chips - 1, rows, width), B16),
            pltpu.VMEM((chips - 1, rows, width), B16),
            pltpu.SemaphoreType.DMA((2, chips * CHUNKS)),
            pltpu.SemaphoreType.DMA((2, (chips - 1) * CHUNKS)),
        ]
        if turn:
            scratch.append(pltpu.VMEM(lefts[0].shape[::-1], B16))
    if spreads:
        shapes.append(jax.ShapeDtypeStruct((ranks, rows, width), B16))
        scratch += [
            pltpu.SemaphoreType.DMA((2, (chips - 1) * CHUNKS)),
            pltpu.SemaphoreType.DMA((2, CHUNKS)),
            pltpu.SemaphoreType.DMA((2, (chips - 1) * CHUNKS)),
        ]
    scratch += rider_scratch(modes)
    if shared is not None:
        key = key + shared.shape
        cargo = cargo + [shared]
        blocks = (lax.axis_size("row"), LATENTS * ranks) + shared.shape
        cargo_shapes = cargo_shapes + [jax.ShapeDtypeStruct(blocks, shared.dtype)]
        scratch += [
            pltpu.SemaphoreType.DMA((2, gather_copies())),
            pltpu.SemaphoreType.DMA((1,)),
        ]
    args = (list(lefts) + list(rights) if sums else []) + list(ins)
    whole = pl.BlockSpec(memory_space=pltpu.VMEM)
    away = pl.BlockSpec(memory_space=pl.ANY)
    results = pl.pallas_call(
        functools.partial(
            token_kernel, sums, spreads, body, len(ins), len(outs), modes, shared is not None
        ),
        out_shape=shapes + cargo_shapes,
        in_specs=[whole] * len(args) + [away] * len(cargo),
        out_specs=[whole] * len(shapes) + [away] * len(cargo),
        scratch_shapes=scratch,
        name=name,
        compiler_params=comm_params(number_of(name, key)),
        cost_estimate=pl.CostEstimate(
            flops=20 * rows * width, bytes_accessed=12 * rows * width, transcendentals=0
        ),
    )(*args, *cargo)
    results = list(results)
    if spreads:
        place = len(outs)
        results[place] = results[place].reshape(ranks * rows, width)
    return results


def start_kernel(modes, *refs):
    refs = list(refs)
    take = lambda count: [refs.pop(0) for _ in range(count)]
    cond, mod = take(2)
    sources = take(len(modes))
    low_ref, out = take(2)
    targets = take(len(modes))
    got, terms, landed, cond_sems, term_sems, out_sems = take(6)
    row, lat, rank = here()
    rows, ranks = lax.axis_size("row"), rank_count()
    columns = LATENTS * ranks
    column = lat * ranks + rank
    others = row_peers()
    company = []
    for step in range(1, columns):
        place = (column + step) % columns
        company.append(device_at(row, place // ranks, place % ranks))
    greet([device for _, device in others] + company)
    riding = start_riders(modes, sources, targets, *refs) if modes else []
    copies = []
    got[row] = cond[row]
    for index, (other, device) in enumerate(others):
        copy = remote(cond.at[other], got.at[row], cond_sems, index, device)
        copy.start()
        copies.append(copy)
    for copy in copies:
        copy.wait()
    value = got[...]
    low = (value / (1.0 + jnp.exp(-value))).astype(B16)
    low_ref[...] = low.astype(F32)
    flat = low.reshape(rows * 8, low.shape[2])
    first = jnp.dot(flat, mod[0], preferred_element_type=F32)
    second = jnp.dot(flat, mod[1], preferred_element_type=F32)
    upper = lax.broadcasted_iota(jnp.int32, first.shape, 0) % 8 < LATENTS
    terms[...] = jnp.where(upper, first, second).reshape(terms.shape)
    copies = []
    landed[row] = terms[row]
    for index, (other, device) in enumerate(others):
        copy = remote(terms.at[other], landed.at[row], term_sems, index, device)
        copy.start()
        copies.append(copy)
    for copy in copies:
        copy.wait()
    out[column] = jnp.sum(landed[...], axis=0)
    copies = []
    for index, device in enumerate(company):
        copy = remote(out.at[column], out.at[column], out_sems, index, device)
        copy.start()
        copies.append(copy)
    for copy in copies:
        copy.wait()
    for copy in riding:
        copy.wait()


def start_call(cond, mod_w, riders):
    rows, ranks = lax.axis_size("row"), rank_count()
    layers, depth, local = mod_w.shape
    tall, wide = depth + -depth % 128, local + -local % 128
    blocks = jnp.transpose(cond.astype(F32).reshape(LATENTS, rows, depth), (1, 0, 2))
    blocks = jnp.concatenate([blocks] * layers, axis=1)
    blocks = jnp.pad(blocks, ((0, 0), (0, 8 - layers * LATENTS), (0, tall - depth)))
    mod = jnp.pad(mod_w, ((0, 0), (0, tall - depth), (0, wide - local)))
    modes, key, cargo, cargo_shapes = split_riders(riders)
    whole = pl.BlockSpec(memory_space=pltpu.VMEM)
    away = pl.BlockSpec(memory_space=pl.ANY)
    columns = LATENTS * ranks
    low, out, *rest = pl.pallas_call(
        functools.partial(start_kernel, modes),
        out_shape=[
            jax.ShapeDtypeStruct(blocks.shape, F32),
            jax.ShapeDtypeStruct((columns, 8, wide), F32),
        ]
        + cargo_shapes,
        in_specs=[whole] * 2 + [away] * len(cargo),
        out_specs=[whole] * 2 + [away] * len(cargo),
        scratch_shapes=[
            pltpu.VMEM(blocks.shape, F32),
            pltpu.VMEM((rows, 8, wide), F32),
            pltpu.VMEM((rows, 8, wide), F32),
            pltpu.SemaphoreType.DMA((2, rows - 1)),
            pltpu.SemaphoreType.DMA((2, rows - 1)),
            pltpu.SemaphoreType.DMA((2, columns - 1)),
        ]
        + rider_scratch(modes),
        name="shift",
        compiler_params=comm_params(number_of("shift", key)),
    )(blocks, mod, *cargo)
    cond_rows = low[:, :LATENTS, :depth].reshape(rows * LATENTS, depth).astype(B16)
    own = lax.dynamic_index_in_dim(
        out[:, : layers * LATENTS].reshape(columns, layers, LATENTS, wide),
        lax.axis_index("lat"),
        axis=2,
        keepdims=False,
    )
    shift = jnp.transpose(own[:, :, :local], (1, 0, 2)).reshape(layers, columns * local)
    return cond_rows, shift, rest


def end_kernel(modes, *refs):
    refs = list(refs)
    take = lambda count: [refs.pop(0) for _ in range(count)]
    (value,) = take(1)
    sources = take(len(modes))
    (out,) = take(1)
    targets = take(len(modes))
    parts, pair, part_sems, pair_sems, out_sems = take(5)
    row, lat, rank = here()
    ranks = rank_count()
    others = row_peers()
    company = [device_at(row, lat, (rank + step) % ranks) for step in range(1, ranks)]
    greet(company + [lat_peer()] + [device for _, device in others])
    riding = start_riders(modes, sources, targets, *refs) if modes else []
    copies = []
    for index, device in enumerate(company):
        copy = remote(value, parts.at[index], part_sems, index, device)
        copy.start()
        copies.append(copy)
    for copy in copies:
        copy.wait()
    pair[lat] = value[...] + jnp.sum(parts[...], axis=0)
    copy = remote(pair.at[lat], pair.at[lat], pair_sems, 0, lat_peer())
    copy.start()
    copy.wait()
    out[row] = pair[...]
    copies = []
    for index, (_, device) in enumerate(others):
        copy = remote(pair, out.at[row], out_sems, index, device)
        copy.start()
        copies.append(copy)
    for copy in copies:
        copy.wait()
    for copy in riding:
        copy.wait()


def end_call(value, riders):
    rows, ranks = lax.axis_size("row"), rank_count()
    modes, key, cargo, cargo_shapes = split_riders(riders)
    whole = pl.BlockSpec(memory_space=pltpu.VMEM)
    away = pl.BlockSpec(memory_space=pl.ANY)
    return pl.pallas_call(
        functools.partial(end_kernel, modes),
        out_shape=[jax.ShapeDtypeStruct((rows, LATENTS) + value.shape, F32)]
        + cargo_shapes,
        in_specs=[whole] + [away] * len(cargo),
        out_specs=[whole] + [away] * len(cargo),
        scratch_shapes=[
            pltpu.VMEM((ranks - 1,) + value.shape, F32),
            pltpu.VMEM((LATENTS,) + value.shape, F32),
            pltpu.SemaphoreType.DMA((2, ranks - 1)),
            pltpu.SemaphoreType.DMA((2, 1)),
            pltpu.SemaphoreType.DMA((2, rows - 1)),
        ]
        + rider_scratch(modes),
        name="gains",
        compiler_params=comm_params(number_of("gains", key)),
    )(value, *cargo)


def first_body(index, span, total, ins, outs):
    resid, gain, shift = ins
    return (norm_stats(resid[span])[0] * gain[...] + shift[...]).astype(B16)


def middle_body(index, span, total, ins, outs):
    resid, gain = ins
    value = resid[span] + total
    outs[0][span] = value
    return (norm_stats(value)[0] * gain[...]).astype(B16)


def last_body(index, span, total, ins, outs):
    outs[0][span] = ins[0][span] + total
    return None


def spread_body(index, span, total, ins, outs):
    return ins[0][span].astype(B16)


def add_rows(out, index, value):
    value = jnp.sum(value, axis=0, keepdims=True)
    if index == 0:
        out[...] = value
    else:
        out[...] += value


def back_body(index, span, total, ins, outs):
    grad, resid, gain = ins
    normed, rstd = norm_stats(resid[span])
    value = grad[span] + norm_back(normed, rstd, total * gain[...])
    outs[0][span] = value
    add_rows(outs[1], index, total * normed)
    return value.astype(B16)


def back_last_body(index, span, total, ins, outs):
    back_body(index, span, total, ins, outs)
    add_rows(outs[2], index, total)
    return None


def first_tokens(resid, gain, shift, riders=()):
    return token_call("first", first_body, None, [resid, gain, shift], [], True, riders)


def middle_tokens(part, resid, gain, riders=()):
    ins = [resid, gain]
    return token_call("middle", middle_body, part, ins, [resid.shape], True, riders)


def last_tokens(part, resid, riders=()):
    return token_call("last", last_body, part, [resid], [resid.shape], False, riders)


def spread_tokens(grad, riders=(), shared=None):
    return token_call("spread", spread_body, None, [grad], [], True, riders, shared)


def back_tokens(part, grad, resid, gain, riders=()):
    shapes = [grad.shape, gain.shape]
    ins = [grad, resid, gain]
    return token_call("back", back_body, part, ins, shapes, True, riders)


def back_last_tokens(part, grad, resid, gain, riders=()):
    shapes = [grad.shape, gain.shape, gain.shape]
    ins = [grad, resid, gain]
    return token_call("back_last", back_last_body, part, ins, shapes, False, riders)


def dot(left, right, left_dim, right_dim):
    return lax.dot_general(
        left, right, (((left_dim,), (right_dim,)), ((), ())), preferred_element_type=F32
    )


def skip_kernel(resid_ref, skip_ref, gain_ref, weight_ref, low_ref, out_ref):
    tokens, width = resid_ref.shape
    parts, _, depth = weight_ref.shape
    step = tokens // CHUNKS
    for index in range(CHUNKS):
        span = pl.ds(index * step, step)
        joined = jnp.concatenate([resid_ref[span], skip_ref[span].astype(F32)], axis=1)
        low_ref[span] = (norm_stats(joined)[0] * gain_ref[...]).astype(B16)
    for part in range(parts):
        low = low_ref[:, part * depth : (part + 1) * depth]
        term = dot(low, weight_ref[part], 1, 1)
        if part == 0:
            out_ref[...] = term
        else:
            out_ref[...] += term


def skip_back_kernel(
    grad_ref,
    low_ref,
    resid_ref,
    skip_ref,
    gain_ref,
    weight_ref,
    weight_out,
    resid_out,
    skip_out,
    gain_out,
    norm_grad,
    leaving,
    grad_sibling,
    low_sibling,
    sems,
):
    tokens, width = resid_ref.shape
    parts, _, depth = weight_ref.shape
    blocks = LATENTS * rank_count()
    local = width // blocks
    step = tokens // CHUNKS
    sibling = peers_along("core")[2][0][1]
    core = lax.axis_index("core")
    greet([sibling])
    grad_low = grad_ref[...].astype(B16)
    even, odd = [], []
    for block in range(0, blocks, 2):
        even.append(grad_ref[:, block * local : (block + 1) * local])
        odd.append(grad_ref[:, (block + 1) * local : (block + 2) * local])
    even, odd = jnp.concatenate(even, axis=1), jnp.concatenate(odd, axis=1)
    leaving[...] = jnp.where(core == 0, odd, even).astype(B16)
    staying = jnp.where(core == 0, even, odd).astype(B16)
    copies = [
        remote(leaving, grad_sibling, sems, 0, sibling),
        remote(low_ref, low_sibling, sems, 1, sibling),
    ]
    for copy in copies:
        copy.start()
    for part in range(parts):
        columns = slice(part * depth, (part + 1) * depth)
        norm_grad[:, columns] = dot(grad_low, weight_ref[part], 1, 0)
    for index in range(CHUNKS):
        span = pl.ds(index * step, step)
        joined = jnp.concatenate([resid_ref[span], skip_ref[span].astype(F32)], axis=1)
        normed, rstd = norm_stats(joined)
        grad = norm_grad[span]
        add_rows(gain_out, index, grad * normed)
        value = norm_back(normed, rstd, grad * gain_ref[...])
        resid_out[span] = value[:, :width]
        skip_out[span] = value[:, width:]
    for copy in copies:
        copy.wait()
    mine_t, theirs_t = staying.T, grad_sibling[...].T
    for part in range(parts):
        columns = slice(part * depth, (part + 1) * depth)
        term = dot(mine_t, low_ref[:, columns], 1, 0)
        term = term + dot(theirs_t, low_sibling[:, columns], 1, 0)
        weight_out[part] = term.astype(B16)


def local_call(name, body, args, shapes, scratch=(), params=None):
    return pl.pallas_call(
        body,
        out_shape=shapes,
        in_specs=[pl.BlockSpec(memory_space=pltpu.VMEM)] * len(args),
        out_specs=[pl.BlockSpec(memory_space=pltpu.VMEM)] * len(shapes),
        scratch_shapes=list(scratch),
        name=name,
        compiler_params=params or pltpu.CompilerParams(vmem_limit_bytes=VMEM_LIMIT),
    )(*args)


def skip_forward(resid, skip, gain, weight):
    tokens, width = resid.shape
    shapes = [
        jax.ShapeDtypeStruct((tokens, 2 * width), B16),
        jax.ShapeDtypeStruct((tokens, width), F32),
    ]
    return local_call("skip", skip_kernel, [resid, skip, gain, weight], shapes)


def skip_backward(grad, low, resid, skip, gain, weight):
    tokens, width = resid.shape
    parts, _, depth = weight.shape
    half = width // 2
    shapes = [
        jax.ShapeDtypeStruct((parts, half, depth), B16),
        jax.ShapeDtypeStruct(resid.shape, F32),
        jax.ShapeDtypeStruct(resid.shape, F32),
        jax.ShapeDtypeStruct(gain.shape, F32),
    ]
    scratch = [
        pltpu.VMEM((tokens, 2 * width), F32),
        pltpu.VMEM((tokens, half), B16),
        pltpu.VMEM((tokens, half), B16),
        pltpu.VMEM((tokens, 2 * width), B16),
        pltpu.SemaphoreType.DMA((2, 2)),
    ]
    args = [grad, low, resid, skip, gain, weight]
    params = comm_params(number_of("skip_back", ()))
    return local_call("skip_back", skip_back_kernel, args, shapes, scratch, params)


def on_device(
    latent,
    skips,
    cond,
    text,
    skip_gain,
    attn_gain,
    ffn_gain,
    skip_w,
    mod_w,
    qkv_w,
    out_w,
    cq_w,
    ckv_w,
    cout_w,
    fc1_w,
    fc2_w,
    cotangent,
):
    rows = lax.axis_size("row")
    ranks = rank_count()
    row = lax.axis_index("row")
    lat = lax.axis_index("lat")
    rank = here()[2]
    width = latent.shape[1]
    depth = qkv_w.shape[2]
    local = qkv_w.shape[3]
    hidden_local = fc1_w.shape[2]
    layers = skip_w.shape[0]
    text_depth = ckv_w.shape[2]
    text_count = text.shape[1]
    tables = rotary_tables()


    def gather_both(pack, other, sizes):
        low, high = jnp.where(lat == 0, pack, other), jnp.where(lat == 0, other, pack)
        pieces, start = [], 0
        for size in sizes:
            pieces += [low[:, start : start + size], high[:, start : start + size]]
            start += size
        return lax.all_gather(jnp.concatenate(pieces, axis=1), "row", axis=0, tiled=True)

    attn_pack, cross_pack, text_pack, up_pack, down_pack = [], [], [], [], []
    attn_full, cross_full, text_full_w = [], [], []
    for layer in range(layers):
        attn_pack.append(
            jnp.concatenate(
                [qkv_w[layer, 0], qkv_w[layer, 1], qkv_w[layer, 2], out_w[layer].T], axis=1
            )
        )
        cross_pack.append(jnp.concatenate([cq_w[layer], cout_w[layer].T], axis=1))
        text_pack.append(jnp.concatenate([ckv_w[layer, 0], ckv_w[layer, 1]], axis=1))
        up_pack.append(fc1_w[layer])
        down_pack.append(fc2_w[layer].T)

    cond_rows, shift, others = start_call(
        cond, mod_w, [swap(attn_pack[0])]
    )
    attn_full.append(gather_both(attn_pack[0], others[0], [local] * 4))


    def stack(array):
        return [("gather", "lat", 0, None, array)]

    def gather_one(array):
        return [("gather", "b", 0, 0, array), ("gather", "a", 0, 1, array)]

    def gather_two(halves):
        return [("gather", "a", 0, None, halves[0]), ("gather", "b", 1, None, halves[1])]

    def whole(halves):
        return [half.reshape(width, -1) for half in halves]

    grad = cotangent.astype(F32)
    grad_all, cross_other, text_other, up_stack, skip_blocks = spread_tokens(
        grad, [swap(cross_pack[0]), swap(text_pack[0])] + stack(up_pack[0]), skip_w[0].T
    )
    skip_full = [skip_blocks.reshape(rows, width, -1)]
    down_stack = down_half = None

    def own_text(text):
        text_parts = lax.all_gather(text, ("lat", "chip", "core"), axis=0)
        text_own = lax.dynamic_index_in_dim(text_parts, lat, axis=1, keepdims=False)
        text_own = jnp.transpose(text_own, (1, 0, 2)).reshape(text_count, -1)
        return jnp.pad(text_own, ((0, -text_count % 128), (0, 0)))

    wide = LATENTS * local

    def thirds(stack, count):
        return [stack[index * wide : (index + 1) * wide] for index in range(count)]

    resid = latent.astype(F32)
    saved = []
    for layer in range(layers):
        keep = {}
        keep["skip_in"] = resid
        keep["skip_low"], resid_one = skip_forward(
            resid, skips[layer], skip_gain[layer : layer + 1], skip_full[layer]
        )
        keep["first"] = resid_one
        following = layer + 1 < layers
        if layer == 0:
            riders = gather_one(up_stack) + stack(down_pack[0])
        else:
            riders = [swap(cross_pack[layer]), swap(text_pack[layer])]
        first_all, *others = first_tokens(
            resid_one, attn_gain[layer, 0:1], shift[layer : layer + 1], riders
        )
        if layer == 0:
            up_half, down_stack = others[:2], others[2]
            text, cross_other, text_other, first_all = lax.optimization_barrier(
                (text, cross_other, text_other, first_all)
            )
            text_own = own_text(text)
        else:
            cross_other, text_other = others
        cross_full.append(gather_both(cross_pack[layer], cross_other, [local] * 2))
        text_full_w.append(gather_both(text_pack[layer], text_other, [local] * 2))
        keep["first_all"] = first_all
        weight = attn_full[layer]
        query, keys, values = thirds(dot(weight[:, : 3 * wide], first_all, 0, 1), 3)
        self_low, self_lse = attention(query, keys, values, tables, SEQ, True)
        keep["self"] = (query, keys, values, self_lse, self_low)
        out_t = weight[:, 3 * wide :]
        keep["out_t"] = out_t
        if following:
            skip_next, self_low = lax.optimization_barrier((skip_w[layer + 1].T, self_low))
            skip_full.append(
                lax.all_gather(skip_next, ("row", "lat", "chip", "core"), axis=0).reshape(
                    rows, width, -1
                )
            )
        riders = gather_two(up_half) + gather_one(down_stack)
        if following:
            riders.append(swap(attn_pack[layer + 1]))
        resid_two, third_all, *others = middle_tokens(
            (True, [self_low], [out_t]), resid_one, attn_gain[layer, 1:2], riders
        )
        up_w, down_half = whole(others[:2]), others[2:4]
        if following:
            attn_full.append(gather_both(attn_pack[layer + 1], others[4], [local] * 4))
        keep["third"] = resid_two
        keep["third_all"] = third_all
        weight = cross_full[layer]
        query_w, cout_t = weight[:, :wide], weight[:, wide:]
        keep["cross_w"] = (query_w, cout_t)
        cross_query = dot(query_w, third_all, 0, 1)
        text_keys, text_values = thirds(dot(text_full_w[layer], text_own, 0, 1), 2)
        cross_low, cross_lse = attention(
            cross_query, text_keys, text_values, tables, text_count, False
        )
        keep["cross"] = (cross_query, text_keys, text_values, cross_lse, cross_low)
        riders = gather_two(down_half) + (stack(up_pack[layer + 1]) if following else [])
        resid_three, second_all, *others = middle_tokens(
            (True, [cross_low], [cout_t]),
            resid_two,
            ffn_gain[layer : layer + 1],
            riders,
        )
        down_w = whole(others[:2])
        if following:
            up_stack = others[2]
        keep["second"] = resid_three
        keep["second_all"] = second_all
        hidden = [dot(second_all, up_w[part], 1, 0) for part in range(LATENTS)]
        act_low = [gelu_tanh(part).astype(B16) for part in hidden]
        keep["hidden"] = hidden
        keep["act"] = act_low
        keep["ffn_w"] = (up_w, down_w)
        term = (False, act_low, down_w)
        if following:
            riders = gather_one(up_stack) + stack(down_pack[layer + 1])
        if following:
            resid, *others = last_tokens(term, resid_three, riders)
        if following:
            up_half, down_stack = others[:2], others[2]
        saved.append(keep)

    final_term, final_resid = term, resid_three

    def sum_over_rows(parts, counts):
        pieces = []
        for part, count in zip(parts, counts):
            pieces += [
                part[:, index * local : (index + 1) * local].astype(B16)
                for index in range(LATENTS * count)
            ]
        packed = jnp.concatenate(pieces[0::2] + pieces[1::2], axis=1)
        summed = lax.psum_scatter(packed, "row", scatter_dimension=0, tiled=True)
        half = summed.shape[1] // 2
        low, high = summed[:, :half], summed[:, half:]
        return jnp.where(lat == 0, low, high), jnp.where(lat == 0, high, low)

    def finish(mine, other):
        total = mine.astype(F32) + other.astype(F32)
        return [
            total[:, start : start + local] for start in range(0, total.shape[1], local)
        ]

    fast = rows // 2
    slow_at, fast_at = row // fast, row % fast

    def by_rows(value):
        return value.astype(B16).reshape(2, fast, -1, value.shape[1])

    def pick(value, index, axis):
        return lax.dynamic_index_in_dim(value, index, axis=axis, keepdims=False).astype(F32)

    def scatter_one(halves):
        return [("scatter", "a", 0, None, halves[0]), ("scatter", "b", 1, None, halves[1])]

    def added_one(halves, arrived):
        low = pick(halves[0], slow_at, 0) + jnp.sum(arrived[0].astype(F32), axis=0)
        high = pick(halves[1], fast_at, 1) + jnp.sum(arrived[1].astype(F32), axis=0)
        return [low.astype(B16), high.astype(B16)]

    def chip_rider(value):
        return ("scatter", "chip", 1, None, value)

    def added_chips(value, arrived):
        total = pick(value, rank // 2, 1) + jnp.sum(arrived.astype(F32), axis=0)
        mine = jnp.where(lat == 0, total[0], total[1])
        return mine, jnp.where(lat == 0, total[1], total[0]).astype(B16)

    def scatter_two(halves):
        return [("scatter", "b", 0, None, halves[0]), ("scatter", "a", 0, None, halves[1])]

    def added_two(halves, arrived):
        low = pick(halves[0], fast_at, 0) + jnp.sum(arrived[0].astype(F32), axis=0)
        high = pick(halves[1], slow_at, 0) + jnp.sum(arrived[1].astype(F32), axis=0)
        mine = jnp.where(lat == 0, low, high)
        return mine, jnp.where(lat == 0, high, low).astype(B16)

    text_grad = jnp.zeros(text_own.shape, F32)
    weight_store = [None] * layers
    gain_store = [None] * layers
    skip_store = [None] * layers
    shift_store = [None] * layers
    waiting = None
    for layer in range(layers - 1, -1, -1):
        keep = saved[layer]
        up_w, down_w = keep["ffn_w"]
        if waiting is not None:
            grad_all, other = spread_tokens(grad, [swap(waiting["down"][1])])
            waiting["store"]["down"] = waiting["down"][0] + other.astype(F32)
        ups, downs, hidden_grads = [], [], []
        for part in range(LATENTS):
            act_grad = dot(grad_all, down_w[part], 1, 0)
            hidden_grad = (act_grad * gelu_grad(keep["hidden"][part])).astype(B16)
            downs.append(by_rows(dot(grad_all, keep["act"][part], 0, 0)))
            ups.append(by_rows(dot(keep["second_all"], hidden_grad, 0, 0)))
            hidden_grads.append(hidden_grad)
        riders = scatter_one(ups)
        if waiting is not None:
            riders.append(chip_rider(waiting["skip"]))
        names = ("attn", "cross", "text")
        if waiting is not None:
            riders += [swap(waiting[name][1]) for name in names]
        grad_three, gain_ffn, grad_all, *others = back_tokens(
            (False, hidden_grads, up_w), grad, keep["second"], ffn_gain[layer : layer + 1], riders
        )
        ups = added_one(ups, others[:2])
        if waiting is not None:
            waiting["skip"] = added_chips(waiting["skip"], others[2])
            for name, other in zip(names, others[3:]):
                waiting["store"][name] = finish(waiting[name][0], other)

        query_w, cout_t = keep["cross_w"]
        cross_query, text_keys, text_values, cross_lse, cross_low = keep["cross"]
        out_grad = dot(cout_t, grad_all, 0, 1).astype(B16)
        cout_grad = dot(grad_all, cross_low, 0, 1)
        query_grad, keys_grad, values_grad = attention_back(
            cross_query, text_keys, text_values, cross_lse, out_grad, tables, text_count, False
        )
        cq_grad = dot(keep["third_all"], query_grad, 0, 1)
        cross_sum = sum_over_rows([cq_grad, cout_grad], [1, 1])
        both = jnp.concatenate([keys_grad, values_grad], axis=0)
        text_sum = sum_over_rows([dot(text_own, both, 0, 1)], [2])
        text_grad = text_grad + dot(both, text_full_w[layer], 0, 1)
        riders = scatter_two(ups) + scatter_one(downs)
        if waiting is not None:
            riders.append(swap(waiting["skip"][1]))
        grad_two, gain_cross, grad_all, *others = back_tokens(
            (True, [query_grad], [query_w]),
            grad_three,
            keep["third"],
            attn_gain[layer, 1:2],
            riders,
        )
        up_mine, up_theirs = added_two(ups, others[:2])
        downs = added_one(downs, others[2:4])
        if waiting is not None:
            waiting["store"]["skip"] = waiting["skip"][0] + others[4].astype(F32)

        weight = attn_full[layer]
        query, keys, values, self_lse, self_low = keep["self"]
        out_grad = dot(keep["out_t"], grad_all, 0, 1).astype(B16)
        wout_grad = dot(grad_all, self_low, 0, 1)
        three = attention_back(query, keys, values, self_lse, out_grad, tables, SEQ, True)
        both = jnp.concatenate(three, axis=0)
        qkv_grad = dot(keep["first_all"], both, 0, 1)
        riders = scatter_two(downs) + [swap(up_theirs)]
        if layer == 0:
            blocks = text_grad[:text_count].astype(B16).reshape(text_count, LATENTS * ranks, -1)
            blocks = jnp.transpose(blocks, (1, 0, 2))
            blocks = lax.all_to_all(
                blocks, ("lat", "chip", "core"), split_axis=0, concat_axis=0, tiled=True
            )
            both, blocks = lax.optimization_barrier((both, blocks))
            text_out = jnp.sum(
                blocks.astype(F32).reshape((LATENTS, ranks) + blocks.shape[1:]), axis=1
            )
            riders += [swap(cross_sum[1]), swap(text_sum[1])]
        grad_one, gain_self, shift_own, *others = back_last_tokens(
            (True, [both], [weight[:, : 3 * wide]]),
            grad_two,
            keep["first"],
            attn_gain[layer, 0:1],
            riders,
        )
        down_sum = added_two(downs, others[:2])
        up_grad = up_mine + others[2].astype(F32)
        early = others[3:]
        attn_sum = sum_over_rows([qkv_grad, wout_grad], [3, 1])

        packed, grad, skip_store[layer], gain_skip = skip_backward(
            grad_one,
            keep["skip_low"],
            keep["skip_in"],
            skips[layer],
            skip_gain[layer : layer + 1],
            skip_full[layer],
        )
        skip_sum = lax.psum_scatter(packed, "row", scatter_dimension=0, tiled=False)
        skip_sum = skip_sum.reshape(LATENTS, ranks // 2, local, -1)
        gain_store[layer] = (gain_skip[0], jnp.concatenate([gain_self, gain_cross]), gain_ffn[0])
        store = dict(up=up_grad)
        waiting = dict(attn=attn_sum, cross=cross_sum, text=text_sum, down=down_sum, store=store)
        waiting["skip"] = skip_sum
        weight_store[layer] = store
        shift_store[layer] = shift_own

    sizes = [gain_store[0][slot].size for slot in range(3)] + [width]
    flat = jnp.concatenate(
        [
            gain_store[layer][slot].reshape(-1)
            for slot in range(3)
            for layer in range(layers)
        ]
        + [shift_store[layer].reshape(-1) for layer in range(layers)]
    )
    flat = jnp.pad(flat, (0, -flat.size % 1024)).reshape(-1, 128)
    flat_all, down_other = end_call(flat, [swap(waiting["down"][1])])
    waiting["store"]["down"] = waiting["down"][0] + down_other.astype(F32)
    final_resid, flat_all = lax.optimization_barrier((final_resid, flat_all))
    riders = [chip_rider(waiting["skip"]), swap(waiting["attn"][1])]
    mixed, arrived, attn_other = last_tokens(final_term, final_resid, riders)
    mine, theirs = added_chips(waiting["skip"], arrived)
    other = lax.ppermute(theirs, "lat", [(0, 1), (1, 0)])
    waiting["store"]["skip"] = mine + other.astype(F32)
    for name, other in zip(names, [attn_other] + early):
        waiting["store"][name] = finish(waiting[name][0], other)
    flat_all = flat_all.reshape(rows * LATENTS, -1)
    totals = jnp.sum(flat_all, axis=0)
    gains, start = [], 0
    for slot in range(3):
        size = layers * sizes[slot]
        gains.append(
            totals[start : start + size].reshape((layers,) + gain_store[0][slot].shape)
        )
        start += size
    shift_grad = flat_all[:, start : start + layers * width].reshape(-1, layers, width)
    column = (lat * ranks + rank) * local
    shift_cols = lax.dynamic_slice_in_dim(shift_grad, column, local, axis=2).astype(B16)

    weight_store = [
        (
            store["skip"].T,
            dot(cond_rows, shift_cols[:, layer], 0, 0),
            jnp.stack(store["attn"][:3]),
            store["attn"][3].T,
            store["cross"][0],
            jnp.stack(store["text"]),
            store["cross"][1].T,
            store["up"],
            store["down"].T,
        )
        for layer, store in enumerate(weight_store)
    ]
    weight_outs = tuple(
        jnp.stack([weight_store[layer][slot] for layer in range(layers)]) for slot in range(9)
    )
    return (mixed, grad, jnp.stack(skip_store), text_out) + tuple(gains) + weight_outs


def solution(mesh):
    NUMBERS.clear()
    rows, columns = mesh.shape["row"], mesh.shape["col"]
    grid = Mesh(
        mesh.devices.reshape(rows, LATENTS, columns // (2 * LATENTS), 2),
        ("row", "lat", "chip", "core"),
    )
    col = ("lat", "chip", "core")
    tokens = ("row", "lat", "chip", "core")
    return jax.shard_map(
        on_device,
        mesh=grid,
        in_specs=(
            P(tokens, None),
            P(None, tokens, None),
            P("row", None),
            P("row", None, col),
            P(),
            P(),
            P(),
            P(None, "row", col),
            P(None, "row", col),
            P(None, None, "row", col),
            P(None, col, "row"),
            P(None, "row", col),
            P(None, None, "row", col),
            P(None, col, "row"),
            P(None, "row", col),
            P(None, col, "row"),
            P(tokens, None),
        ),
        out_specs=(
            P(tokens, None),
            P(tokens, None),
            P(None, tokens, None),
            P("row", None, col),
            P(),
            P(),
            P(),
            P(None, "row", col),
            P(None, "row", col),
            P(None, None, "row", col),
            P(None, col, "row"),
            P(None, "row", col),
            P(None, None, "row", col),
            P(None, col, "row"),
            P(None, "row", col),
            P(None, col, "row"),
        ),
        check_vma=False,
    )
```

```python
import functools

import jax
import jax.numpy as jnp
from jax import lax
from jax.experimental import pallas as pl
from jax.experimental.pallas import tpu as pltpu
from jax.sharding import Mesh
from jax.sharding import PartitionSpec as P

HD = 88
SIDE = 32
SEQ = 1024
LATENTS = 2

HIGHEST = lax.Precision.HIGHEST
EPSILON = 1e-06
F32 = jnp.float32
B16 = jnp.bfloat16
SCALE = HD ** (-0.5)
VMEM_LIMIT = 48 * 2**20


def norm_stats(value):
    center = value - jnp.mean(value, axis=-1, keepdims=True)
    spread = jnp.mean(center * center, axis=-1, keepdims=True)
    rstd = lax.rsqrt(spread + EPSILON)
    return center * rstd, rstd


def norm_back(normed, rstd, grad):
    return rstd * (
        grad
        - jnp.mean(grad, axis=-1, keepdims=True)
        - normed * jnp.mean(grad * normed, axis=-1, keepdims=True)
    )


def silu(value):
    return value * jax.nn.sigmoid(value)


def gelu_tanh(value):
    inner = 0.7978845608028654 * (value + 0.044715 * value * value * value)
    return 0.5 * value * (1.0 + jnp.tanh(inner))


def gelu_grad(value):
    inner = 0.7978845608028654 * (value + 0.044715 * value * value * value)
    tanh = jnp.tanh(inner)
    slope = 0.7978845608028654 * (1.0 + 3.0 * 0.044715 * value * value)
    return 0.5 * (1.0 + tanh) + 0.5 * value * (1.0 - tanh * tanh) * slope


def rotary_tables():
    place = jnp.arange(SEQ, dtype=jnp.int32)
    grid_row = (place // SIDE).astype(F32)
    grid_col = (place % SIDE).astype(F32)
    feature = jnp.arange(HD, dtype=jnp.int32)
    pair = feature // 2
    quarter = HD // 4
    power = (pair % quarter).astype(F32) * (4.0 / HD)
    freq = jnp.exp(-power * jnp.log(10000.0))
    coordinate = jnp.where(pair[:, None] < quarter, grid_row[None, :], grid_col[None, :])
    angle = coordinate * freq[:, None]
    sign = jnp.where(feature % 2 == 0, -1.0, 1.0)[:, None]
    return (jnp.cos(angle), jnp.sin(angle) * sign)


def swap_rows(value):
    down = pltpu.roll(value, 1, 0)
    up = pltpu.roll(value, value.shape[0] - 1, 0)
    even = lax.broadcasted_iota(jnp.int32, value.shape, 0) % 2 == 0
    return jnp.where(even, up, down)


def head_stats(value):
    center = value - jnp.mean(value, axis=0, keepdims=True)
    rstd = lax.rsqrt(jnp.mean(center * center, axis=0, keepdims=True) + EPSILON)
    return center * rstd, rstd


def head_back(normed, rstd, grad):
    return rstd * (
        grad
        - jnp.mean(grad, axis=0, keepdims=True)
        - normed * jnp.mean(grad * normed, axis=0, keepdims=True)
    )


QUERY_CHUNK = 1024
BACK_CHUNK = 512


def attention_kernel(
    count, turn, query_ref, keys_ref, values_ref, cos_ref, sin_ref, out_ref, logsum_ref
):
    cos, sin = cos_ref[...], sin_ref[...]
    query = head_stats(query_ref[...])[0]
    query_low = (query * cos + swap_rows(query) * sin).astype(B16)
    keys = head_stats(keys_ref[...])[0]
    if turn:
        keys = keys * cos + swap_rows(keys) * sin
    keys_t = keys.astype(B16).T
    values_low = values_ref[...].astype(B16)
    for start in range(0, query_low.shape[1], QUERY_CHUNK):
        span = slice(start, start + QUERY_CHUNK)
        scores = jnp.dot(keys_t, query_low[:, span], preferred_element_type=F32) * SCALE
        if count < keys_t.shape[0]:
            inside = lax.broadcasted_iota(jnp.int32, scores.shape, 0) < count
            scores = jnp.where(inside, scores, -1e30)
        highest = jnp.max(scores, axis=0, keepdims=True)
        expo = jnp.exp(scores - highest)
        total = jnp.sum(expo, axis=0, keepdims=True)
        probs_low = (expo * (1.0 / total)).astype(B16)
        out = jnp.dot(values_low, probs_low, preferred_element_type=F32)
        out_ref[:, span] = out.astype(B16)
        logsum_ref[0, :, span] = highest + jnp.log(total)


def attention_back_kernel(
    count,
    turn,
    query_ref,
    keys_ref,
    values_ref,
    logsum_ref,
    grad_ref,
    cos_ref,
    sin_ref,
    query_out,
    keys_out,
    values_out,
    keys_sum,
    values_sum,
):
    cos, sin = cos_ref[...], sin_ref[...]
    query, query_rstd = head_stats(query_ref[...])
    query_low = (query * cos + swap_rows(query) * sin).astype(B16)
    keys, keys_rstd = head_stats(keys_ref[...])
    keys_low = (keys * cos + swap_rows(keys) * sin if turn else keys).astype(B16)
    keys_t = keys_low.T
    values_t = values_ref[...].astype(B16).T
    grad = grad_ref[...]
    grad_t = grad.T
    query_t = query_low.T
    query_grad = []
    for start in range(0, query_low.shape[1], BACK_CHUNK):
        span = slice(start, start + BACK_CHUNK)
        scores = jnp.dot(keys_t, query_low[:, span], preferred_element_type=F32)
        probs = jnp.exp(scores * SCALE - logsum_ref[0, :, span])
        if count < keys_t.shape[0]:
            inside = lax.broadcasted_iota(jnp.int32, scores.shape, 0) < count
            probs = jnp.where(inside, probs, 0.0)
        values_part = jnp.dot(probs.astype(B16), grad_t[span], preferred_element_type=F32)
        probs_grad = jnp.dot(values_t, grad[:, span], preferred_element_type=F32)
        delta = jnp.sum(probs * probs_grad, axis=0, keepdims=True)
        scores_grad = (probs * (probs_grad - delta)).astype(B16)
        query_grad.append(jnp.dot(keys_low, scores_grad, preferred_element_type=F32))
        keys_part = jnp.dot(scores_grad, query_t[span], preferred_element_type=F32)
        if start == 0:
            values_sum[...] = values_part
            keys_sum[...] = keys_part
        else:
            values_sum[...] += values_part
            keys_sum[...] += keys_part
    grad_query = jnp.concatenate(query_grad, axis=1) * SCALE
    grad_query = grad_query * cos - swap_rows(grad_query) * sin
    query_out[...] = head_back(query, query_rstd, grad_query).astype(B16)
    grad_keys = keys_sum[...].T * SCALE
    if turn:
        grad_keys = grad_keys * cos - swap_rows(grad_keys) * sin
    keys_out[...] = head_back(keys, keys_rstd, grad_keys).astype(B16)
    values_out[...] = values_sum[...].T.astype(B16)


def head_block(columns):
    return pl.BlockSpec((HD, columns), lambda head: (head, 0))


def logsum_block(columns):
    return pl.BlockSpec((1, 1, columns), lambda head: (head, 0, 0))


def attention(query, keys, values, tables, count, turn):
    heads, tokens, others = query.shape[0] // HD, query.shape[1], keys.shape[1]
    table = pl.BlockSpec((HD, tokens), lambda head: (0, 0))
    work = heads * tokens * others
    return pl.pallas_call(
        functools.partial(attention_kernel, count, turn),
        grid=(heads,),
        in_specs=[head_block(tokens), head_block(others), head_block(others), table, table],
        out_specs=[head_block(tokens), logsum_block(tokens)],
        out_shape=[
            jax.ShapeDtypeStruct(query.shape, B16),
            jax.ShapeDtypeStruct((heads, 1, tokens), F32),
        ],
        compiler_params=pltpu.CompilerParams(vmem_limit_bytes=VMEM_LIMIT),
        cost_estimate=pl.CostEstimate(
            flops=4 * HD * work, bytes_accessed=8 * query.size, transcendentals=work
        ),
    )(query, keys, values, *tables)


def attention_back(query, keys, values, logsum, grad_low, tables, count, turn):
    heads, tokens, others = query.shape[0] // HD, query.shape[1], keys.shape[1]
    table = pl.BlockSpec((HD, tokens), lambda head: (0, 0))
    work = heads * tokens * others
    return pl.pallas_call(
        functools.partial(attention_back_kernel, count, turn),
        grid=(heads,),
        in_specs=[
            head_block(tokens),
            head_block(others),
            head_block(others),
            logsum_block(tokens),
            head_block(tokens),
            table,
            table,
        ],
        out_specs=[head_block(tokens), head_block(others), head_block(others)],
        out_shape=[
            jax.ShapeDtypeStruct(value.shape, B16) for value in (query, keys, values)
        ],
        scratch_shapes=[pltpu.VMEM((others, HD), F32), pltpu.VMEM((others, HD), F32)],
        compiler_params=pltpu.CompilerParams(vmem_limit_bytes=VMEM_LIMIT),
        cost_estimate=pl.CostEstimate(
            flops=10 * HD * work, bytes_accessed=16 * query.size, transcendentals=work
        ),
    )(query, keys, values, logsum, grad_low, *tables)


MESH = pl.DeviceIdType.MESH
CHUNKS = 4
NUMBERS = {}


def number_of(name, key):
    return NUMBERS.setdefault((name, key), len(NUMBERS))


def here():
    rank = 2 * lax.axis_index("chip") + lax.axis_index("core")
    return lax.axis_index("row"), lax.axis_index("lat"), rank


def rank_count():
    return 2 * lax.axis_size("chip")


def device_at(row, lat, rank):
    return {"row": row, "lat": lat, "chip": rank // 2, "core": rank % 2}


def row_peers():
    row, lat, rank = here()
    rows = lax.axis_size("row")
    return [((row + step) % rows, device_at((row + step) % rows, lat, rank)) for step in range(1, rows)]


def peers_along(axis):
    row, lat, rank = here()
    if axis == "core":
        other = 1 - rank % 2
        return rank % 2, 2, [(other, device_at(row, lat, rank // 2 * 2 + other))]
    if axis == "chip":
        count = rank_count() // 2
        me = rank // 2
        places = [(me + step) % count for step in range(1, count)]
        return me, count, [(place, device_at(row, lat, 2 * place + rank % 2)) for place in places]
    if axis == "lat":
        return lat, LATENTS, [(1 - lat, device_at(row, 1 - lat, rank))]
    fast = lax.axis_size("row") // 2
    slow_at, fast_at = row // fast, row % fast
    if axis == "a":
        other = 1 - slow_at
        return slow_at, 2, [(other, device_at(other * fast + fast_at, lat, rank))]
    others = [(fast_at + step) % fast for step in range(1, fast)]
    return fast_at, fast, [(other, device_at(slow_at * fast + other, lat, rank)) for other in others]


def lat_peer():
    return peers_along("lat")[2][0][1]


def places():
    row, lat, rank = here()
    chips = rank_count() // 2
    chip, core = rank // 2, rank % 2
    sibling = device_at(row, lat, 2 * chip + 1 - core)
    ahead = [(chip + step) % chips for step in range(1, chips)]
    behind = [(chip + chips - step) % chips for step in range(1, chips)]
    return rank, chip, core, sibling, ahead, behind


def chip_peer(chip, core):
    row, lat, _ = here()
    return device_at(row, lat, 2 * chip + core)


def greet(others):
    barrier = pltpu.get_barrier_semaphore()
    for device in others:
        pl.semaphore_signal(barrier, inc=1, device_id=device, device_id_type=MESH)
    pl.semaphore_wait(barrier, len(others))


def remote(source, target, sems, index, device):
    return pltpu.make_async_remote_copy(
        src_ref=source,
        dst_ref=target,
        send_sem=sems.at[0, index],
        recv_sem=sems.at[1, index],
        device_id=device,
        device_id_type=MESH,
    )


def rider_count(axis):
    counts = {"lat": LATENTS, "a": 2, "b": lax.axis_size("row") // 2, "chip": rank_count() // 2}
    return counts[axis]


def rider_shape(rider):
    kind, axis, place, part, array = rider
    shape = array.shape if part is None else array.shape[1:]
    if kind == "gather":
        shape = shape[:place] + (rider_count(axis),) + shape[place:]
    if kind == "scatter":
        shape = (rider_count(axis) - 1,) + shape[:place] + shape[place + 1 :]
    return jax.ShapeDtypeStruct(shape, array.dtype)


def rider_scratch(modes):
    if not modes:
        return []
    most = sum(rider_count(mode[1]) for mode in modes)
    return [pltpu.SemaphoreType.DMA((2, most)), pltpu.SemaphoreType.DMA((len(modes),))]


def rider_peers(modes, met=()):
    peers = []
    for axis in ("lat", "a", "b"):
        if axis not in met and any(mode[1] == axis for mode in modes):
            peers += [device for _, device in peers_along(axis)[2]]
    return peers


def piece_of(ref, place, index):
    return ref.at[index] if place == 0 else ref.at[:, index]


def start_riders(modes, sources, targets, sems, local_sems):
    copies, index = [], 0
    for order, (mode, source, target) in enumerate(zip(modes, sources, targets)):
        kind, axis, place, part = mode
        me, _, others = peers_along(axis)
        if part is not None:
            source = source.at[part]
        for step, (other, device) in enumerate(others):
            if kind == "swap":
                copies.append(remote(source, target, sems, index, device))
            if kind == "gather":
                copies.append(remote(source, piece_of(target, place, me), sems, index, device))
            if kind == "scatter":
                piece = piece_of(source, place, other)
                copies.append(remote(piece, target.at[step], sems, index, device))
            index += 1
        if kind == "gather":
            own = piece_of(target, place, me)
            copies.append(pltpu.make_async_copy(source, own, local_sems.at[order]))
    for copy in copies:
        copy.start()
    return copies


def split_riders(riders):
    modes = tuple(rider[:4] for rider in riders)
    key = tuple((mode, rider[4].shape) for mode, rider in zip(modes, riders))
    return modes, key, [rider[4] for rider in riders], [rider_shape(rider) for rider in riders]


def swap(array):
    return ("swap", "lat", 0, None, array)


def gather_everyone(source, target, sems, local_sem, between):
    row, lat, _ = here()
    ranks = rank_count()
    rank, chip, core, sibling, ahead, _ = places()
    chips = ranks // 2
    fast_at, fast, fast_peers = peers_along("b")
    slow_at, slow, slow_peers = peers_along("a")
    counter = iter(range(sems.shape[1]))
    sent, last = [], []

    def block(at_row, at_lat, at_rank):
        return target.at[at_row, at_lat * ranks + at_rank]

    def push(piece, device, kept):
        copy = remote(piece, piece, sems, next(counter), device)
        copy.start()
        kept.append(copy)

    def landed(copies):
        for copy in copies:
            copy.wait_recv()
        sent.extend(copies)

    mine = block(row, lat, rank)
    local = pltpu.make_async_copy(source, mine, local_sem.at[0])
    local.start()
    first = remote(source, mine, sems, next(counter), lat_peer())
    first.start()

    def finish():
        local.wait()
        landed([first])
        between()
        step = []
        for place in ahead:
            for at_lat in range(LATENTS):
                push(block(row, at_lat, rank), chip_peer(place, core), step)
        landed(step)
        step = []
        for place in range(chips):
            at_rank = 2 * place + core
            for _, device in fast_peers:
                push(block(row, 0, at_rank), device, step)
            for _, device in slow_peers:
                push(block(row, 1, at_rank), device, step)
        for place in range(chips):
            for at_lat in range(LATENTS):
                push(block(row, at_lat, 2 * place + core), sibling, last)
        landed(step)
        step = []
        for place in range(chips):
            at_rank = 2 * place + core
            for index in range(fast):
                for _, device in slow_peers:
                    push(block(slow_at * fast + index, 0, at_rank), device, step)
            for index in range(slow):
                for _, device in fast_peers:
                    push(block(index * fast + fast_at, 1, at_rank), device, step)
        for place in range(chips):
            at_rank = 2 * place + core
            for index, _ in fast_peers:
                push(block(slow_at * fast + index, 0, at_rank), sibling, last)
            for index, _ in slow_peers:
                push(block(index * fast + fast_at, 1, at_rank), sibling, last)
        landed(step)
        for place in range(chips):
            at_rank = 2 * place + core
            for other, _ in slow_peers:
                for index in range(fast):
                    push(block(other * fast + index, 0, at_rank), sibling, last)
            for other, _ in fast_peers:
                for index in range(slow):
                    push(block(index * fast + other, 1, at_rank), sibling, last)
        for copy in sent:
            copy.wait_send()
        for copy in last:
            copy.wait()

    return finish


def gather_copies():
    rows, chips = lax.axis_size("row"), rank_count() // 2
    fast, slow = rows // 2, 2
    count = 1 + (chips - 1) * LATENTS + chips * (fast - 1 + slow - 1)
    count += chips * (fast * (slow - 1) + slow * (fast - 1))
    return count + chips * LATENTS * rows


def token_kernel(sums, spreads, body, n_in, n_out, modes, shared, *refs):
    refs = list(refs)
    take = lambda count: [refs.pop(0) for _ in range(count)]
    if sums:
        lefts, rights = take(sums[1]), take(sums[1])
    ins, sources = take(n_in), take(len(modes))
    block = refs.pop(0) if shared else None
    outs = take(n_out)
    everyone = refs.pop(0) if spreads else None
    targets = take(len(modes))
    blocks = refs.pop(0) if shared else None
    if sums:
        part, from_sibling, outgoing, incoming, pair_sems, sum_sems = take(6)
        if sums[0]:
            turned = take(1)
            turned[0][...] = lefts[0][...].T
            lefts = turned
    if spreads:
        chip_sems, own_sems, forward_sems = take(3)
    rank, chip, core, sibling, ahead, behind = places()
    chips = len(ahead) + 1
    rows = ins[0].shape[0]
    step = rows // CHUNKS
    spans = [pl.ds(index * step, step) for index in range(CHUNKS)]
    met = [sibling] + [chip_peer(place, core) for place in ahead]
    if shared:
        met += [device for axis in ("lat", "a", "b") for _, device in peers_along(axis)[2]]
    else:
        met += rider_peers(modes)
    greet(met)
    started, riding = [], []

    def multiply(place):
        some = pl.ds(pl.multiple_of(place * rows, 128), rows)
        term = None
        for left, right in zip(lefts, rights):
            piece = dot(left[some], right[...], 1, 1)
            term = piece if term is None else term + piece
        part[place] = term.astype(B16)


    def ride():
        if modes:
            riding.extend(start_riders(modes, sources, targets, *refs[:2]))

    if shared:
        finish_gather = gather_everyone(block, blocks, *refs[-2:], ride)
    if sums:
        pair = {}
        for order, place in enumerate(ahead + [chip]):
            multiply(2 * place + 1 - core)
            for index, span in enumerate(spans):
                copy = remote(
                    part.at[2 * place + 1 - core, span],
                    from_sibling.at[order, span],
                    pair_sems,
                    order * CHUNKS + index,
                    sibling,
                )
                copy.start()
                pair[order, index] = copy
        crossing = {}
        for order, place in enumerate(ahead):
            multiply(2 * place + core)
            for index, span in enumerate(spans):
                pair[order, index].wait_recv()
                outgoing[order, span] = (
                    part[2 * place + core, span].astype(F32)
                    + from_sibling[order, span].astype(F32)
                ).astype(B16)
                copy = remote(
                    outgoing.at[order, span],
                    incoming.at[order, span],
                    sum_sems,
                    order * CHUNKS + index,
                    chip_peer(place, core),
                )
                copy.start()
                crossing[order, index] = copy
    if not shared:
        ride()
    if sums:
        multiply(rank)
    direct = {}
    for index, span in enumerate(spans):
        total = None
        if sums:
            pair[chips - 1, index].wait_recv()
            total = part[rank, span].astype(F32) + from_sibling[chips - 1, span].astype(F32)
            for order in range(chips - 1):
                crossing[order, index].wait_recv()
                total = total + incoming[order, span].astype(F32)
        low = body(index, span, total, ins, outs)
        if spreads:
            everyone[rank, span] = low
            mine = everyone.at[rank, span]
            for order, place in enumerate(ahead):
                copy = remote(
                    mine, mine, chip_sems, order * CHUNKS + index, chip_peer(place, core)
                )
                copy.start()
                direct[order, index] = copy
            copy = remote(mine, mine, own_sems, index, sibling)
            copy.start()
            started.append(copy)
    if shared:
        finish_gather()
    if spreads:
        for index, span in enumerate(spans):
            for order, place in enumerate(behind):
                direct[order, index].wait_recv()
                landed = everyone.at[2 * place + core, span]
                copy = remote(landed, landed, forward_sems, order * CHUNKS + index, sibling)
                copy.start()
                started.append(copy)
        for copy in direct.values():
            copy.wait_send()
        for copy in started:
            copy.wait()
    if sums:
        for copy in list(pair.values()) + list(crossing.values()):
            copy.wait_send()
    for copy in riding:
        copy.wait()


def comm_params(number):
    return pltpu.CompilerParams(
        collective_id=number, has_side_effects=True, vmem_limit_bytes=VMEM_LIMIT
    )


def token_call(name, body, part, ins, outs, spreads, riders=(), shared=None):
    ranks = rank_count()
    chips = ranks // 2
    rows, width = ins[0].shape
    sums = None
    if part is not None:
        turn, lefts, rights = part
        sums = (turn, len(lefts))
    modes, key, cargo, cargo_shapes = split_riders(riders)
    shapes = [jax.ShapeDtypeStruct(shape, F32) for shape in outs]
    scratch = []
    if sums:
        key = key + tuple(left.shape for left in lefts)
        scratch += [
            pltpu.VMEM((ranks, rows, width), B16),
            pltpu.VMEM((chips, rows, width), B16),
            pltpu.VMEM((chips - 1, rows, width), B16),
            pltpu.VMEM((chips - 1, rows, width), B16),
            pltpu.SemaphoreType.DMA((2, chips * CHUNKS)),
            pltpu.SemaphoreType.DMA((2, (chips - 1) * CHUNKS)),
        ]
        if turn:
            scratch.append(pltpu.VMEM(lefts[0].shape[::-1], B16))
    if spreads:
        shapes.append(jax.ShapeDtypeStruct((ranks, rows, width), B16))
        scratch += [
            pltpu.SemaphoreType.DMA((2, (chips - 1) * CHUNKS)),
            pltpu.SemaphoreType.DMA((2, CHUNKS)),
            pltpu.SemaphoreType.DMA((2, (chips - 1) * CHUNKS)),
        ]
    scratch += rider_scratch(modes)
    if shared is not None:
        key = key + shared.shape
        cargo = cargo + [shared]
        blocks = (lax.axis_size("row"), LATENTS * ranks) + shared.shape
        cargo_shapes = cargo_shapes + [jax.ShapeDtypeStruct(blocks, shared.dtype)]
        scratch += [
            pltpu.SemaphoreType.DMA((2, gather_copies())),
            pltpu.SemaphoreType.DMA((1,)),
        ]
    args = (list(lefts) + list(rights) if sums else []) + list(ins)
    whole = pl.BlockSpec(memory_space=pltpu.VMEM)
    away = pl.BlockSpec(memory_space=pl.ANY)
    results = pl.pallas_call(
        functools.partial(
            token_kernel, sums, spreads, body, len(ins), len(outs), modes, shared is not None
        ),
        out_shape=shapes + cargo_shapes,
        in_specs=[whole] * len(args) + [away] * len(cargo),
        out_specs=[whole] * len(shapes) + [away] * len(cargo),
        scratch_shapes=scratch,
        name=name,
        compiler_params=comm_params(number_of(name, key)),
        cost_estimate=pl.CostEstimate(
            flops=20 * rows * width, bytes_accessed=12 * rows * width, transcendentals=0
        ),
    )(*args, *cargo)
    results = list(results)
    if spreads:
        place = len(outs)
        results[place] = results[place].reshape(ranks * rows, width)
    return results


def start_kernel(modes, *refs):
    refs = list(refs)
    take = lambda count: [refs.pop(0) for _ in range(count)]
    cond, mod = take(2)
    sources = take(len(modes))
    low_ref, out = take(2)
    targets = take(len(modes))
    got, terms, landed, cond_sems, term_sems, out_sems = take(6)
    row, lat, rank = here()
    rows, ranks = lax.axis_size("row"), rank_count()
    columns = LATENTS * ranks
    column = lat * ranks + rank
    others = row_peers()
    company = []
    for step in range(1, columns):
        place = (column + step) % columns
        company.append(device_at(row, place // ranks, place % ranks))
    greet([device for _, device in others] + company)
    riding = start_riders(modes, sources, targets, *refs) if modes else []
    copies = []
    got[row] = cond[row]
    for index, (other, device) in enumerate(others):
        copy = remote(cond.at[other], got.at[row], cond_sems, index, device)
        copy.start()
        copies.append(copy)
    for copy in copies:
        copy.wait()
    value = got[...]
    low = (value / (1.0 + jnp.exp(-value))).astype(B16)
    low_ref[...] = low.astype(F32)
    flat = low.reshape(rows * 8, low.shape[2])
    first = jnp.dot(flat, mod[0], preferred_element_type=F32)
    second = jnp.dot(flat, mod[1], preferred_element_type=F32)
    upper = lax.broadcasted_iota(jnp.int32, first.shape, 0) % 8 < LATENTS
    terms[...] = jnp.where(upper, first, second).reshape(terms.shape)
    copies = []
    landed[row] = terms[row]
    for index, (other, device) in enumerate(others):
        copy = remote(terms.at[other], landed.at[row], term_sems, index, device)
        copy.start()
        copies.append(copy)
    for copy in copies:
        copy.wait()
    out[column] = jnp.sum(landed[...], axis=0)
    copies = []
    for index, device in enumerate(company):
        copy = remote(out.at[column], out.at[column], out_sems, index, device)
        copy.start()
        copies.append(copy)
    for copy in copies:
        copy.wait()
    for copy in riding:
        copy.wait()


def start_call(cond, mod_w, riders):
    rows, ranks = lax.axis_size("row"), rank_count()
    layers, depth, local = mod_w.shape
    tall, wide = depth + -depth % 128, local + -local % 128
    blocks = jnp.transpose(cond.astype(F32).reshape(LATENTS, rows, depth), (1, 0, 2))
    blocks = jnp.concatenate([blocks] * layers, axis=1)
    blocks = jnp.pad(blocks, ((0, 0), (0, 8 - layers * LATENTS), (0, tall - depth)))
    mod = jnp.pad(mod_w, ((0, 0), (0, tall - depth), (0, wide - local)))
    modes, key, cargo, cargo_shapes = split_riders(riders)
    whole = pl.BlockSpec(memory_space=pltpu.VMEM)
    away = pl.BlockSpec(memory_space=pl.ANY)
    columns = LATENTS * ranks
    low, out, *rest = pl.pallas_call(
        functools.partial(start_kernel, modes),
        out_shape=[
            jax.ShapeDtypeStruct(blocks.shape, F32),
            jax.ShapeDtypeStruct((columns, 8, wide), F32),
        ]
        + cargo_shapes,
        in_specs=[whole] * 2 + [away] * len(cargo),
        out_specs=[whole] * 2 + [away] * len(cargo),
        scratch_shapes=[
            pltpu.VMEM(blocks.shape, F32),
            pltpu.VMEM((rows, 8, wide), F32),
            pltpu.VMEM((rows, 8, wide), F32),
            pltpu.SemaphoreType.DMA((2, rows - 1)),
            pltpu.SemaphoreType.DMA((2, rows - 1)),
            pltpu.SemaphoreType.DMA((2, columns - 1)),
        ]
        + rider_scratch(modes),
        name="shift",
        compiler_params=comm_params(number_of("shift", key)),
    )(blocks, mod, *cargo)
    cond_rows = low[:, :LATENTS, :depth].reshape(rows * LATENTS, depth).astype(B16)
    own = lax.dynamic_index_in_dim(
        out[:, : layers * LATENTS].reshape(columns, layers, LATENTS, wide),
        lax.axis_index("lat"),
        axis=2,
        keepdims=False,
    )
    shift = jnp.transpose(own[:, :, :local], (1, 0, 2)).reshape(layers, columns * local)
    return cond_rows, shift, rest


def end_kernel(modes, *refs):
    refs = list(refs)
    take = lambda count: [refs.pop(0) for _ in range(count)]
    (value,) = take(1)
    sources = take(len(modes))
    (out,) = take(1)
    targets = take(len(modes))
    parts, pair, part_sems, pair_sems, out_sems = take(5)
    row, lat, rank = here()
    ranks = rank_count()
    others = row_peers()
    company = [device_at(row, lat, (rank + step) % ranks) for step in range(1, ranks)]
    greet(company + [lat_peer()] + [device for _, device in others])
    riding = start_riders(modes, sources, targets, *refs) if modes else []
    copies = []
    for index, device in enumerate(company):
        copy = remote(value, parts.at[index], part_sems, index, device)
        copy.start()
        copies.append(copy)
    for copy in copies:
        copy.wait()
    pair[lat] = value[...] + jnp.sum(parts[...], axis=0)
    copy = remote(pair.at[lat], pair.at[lat], pair_sems, 0, lat_peer())
    copy.start()
    copy.wait()
    out[row] = pair[...]
    copies = []
    for index, (_, device) in enumerate(others):
        copy = remote(pair, out.at[row], out_sems, index, device)
        copy.start()
        copies.append(copy)
    for copy in copies:
        copy.wait()
    for copy in riding:
        copy.wait()


def end_call(value, riders):
    rows, ranks = lax.axis_size("row"), rank_count()
    modes, key, cargo, cargo_shapes = split_riders(riders)
    whole = pl.BlockSpec(memory_space=pltpu.VMEM)
    away = pl.BlockSpec(memory_space=pl.ANY)
    return pl.pallas_call(
        functools.partial(end_kernel, modes),
        out_shape=[jax.ShapeDtypeStruct((rows, LATENTS) + value.shape, F32)]
        + cargo_shapes,
        in_specs=[whole] + [away] * len(cargo),
        out_specs=[whole] + [away] * len(cargo),
        scratch_shapes=[
            pltpu.VMEM((ranks - 1,) + value.shape, F32),
            pltpu.VMEM((LATENTS,) + value.shape, F32),
            pltpu.SemaphoreType.DMA((2, ranks - 1)),
            pltpu.SemaphoreType.DMA((2, 1)),
            pltpu.SemaphoreType.DMA((2, rows - 1)),
        ]
        + rider_scratch(modes),
        name="gains",
        compiler_params=comm_params(number_of("gains", key)),
    )(value, *cargo)


def first_body(index, span, total, ins, outs):
    resid, gain, shift = ins
    return (norm_stats(resid[span])[0] * gain[...] + shift[...]).astype(B16)


def middle_body(index, span, total, ins, outs):
    resid, gain = ins
    value = resid[span] + total
    outs[0][span] = value
    return (norm_stats(value)[0] * gain[...]).astype(B16)


def last_body(index, span, total, ins, outs):
    outs[0][span] = ins[0][span] + total
    return None


def spread_body(index, span, total, ins, outs):
    return ins[0][span].astype(B16)


def add_rows(out, index, value):
    value = jnp.sum(value, axis=0, keepdims=True)
    if index == 0:
        out[...] = value
    else:
        out[...] += value


def back_body(index, span, total, ins, outs):
    grad, resid, gain = ins
    normed, rstd = norm_stats(resid[span])
    value = grad[span] + norm_back(normed, rstd, total * gain[...])
    outs[0][span] = value
    add_rows(outs[1], index, total * normed)
    return value.astype(B16)


def back_last_body(index, span, total, ins, outs):
    back_body(index, span, total, ins, outs)
    add_rows(outs[2], index, total)
    return None


def first_tokens(resid, gain, shift, riders=()):
    return token_call("first", first_body, None, [resid, gain, shift], [], True, riders)


def middle_tokens(part, resid, gain, riders=()):
    ins = [resid, gain]
    return token_call("middle", middle_body, part, ins, [resid.shape], True, riders)


def last_tokens(part, resid, riders=()):
    return token_call("last", last_body, part, [resid], [resid.shape], False, riders)


def spread_tokens(grad, riders=(), shared=None):
    return token_call("spread", spread_body, None, [grad], [], True, riders, shared)


def back_tokens(part, grad, resid, gain, riders=()):
    shapes = [grad.shape, gain.shape]
    ins = [grad, resid, gain]
    return token_call("back", back_body, part, ins, shapes, True, riders)


def back_last_tokens(part, grad, resid, gain, riders=()):
    shapes = [grad.shape, gain.shape, gain.shape]
    ins = [grad, resid, gain]
    return token_call("back_last", back_last_body, part, ins, shapes, False, riders)


def dot(left, right, left_dim, right_dim):
    return lax.dot_general(
        left, right, (((left_dim,), (right_dim,)), ((), ())), preferred_element_type=F32
    )


def skip_kernel(resid_ref, skip_ref, gain_ref, weight_ref, low_ref, out_ref):
    tokens, width = resid_ref.shape
    parts, _, depth = weight_ref.shape
    step = tokens // CHUNKS
    for index in range(CHUNKS):
        span = pl.ds(index * step, step)
        joined = jnp.concatenate([resid_ref[span], skip_ref[span].astype(F32)], axis=1)
        low_ref[span] = (norm_stats(joined)[0] * gain_ref[...]).astype(B16)
    for part in range(parts):
        low = low_ref[:, part * depth : (part + 1) * depth]
        term = dot(low, weight_ref[part], 1, 1)
        if part == 0:
            out_ref[...] = term
        else:
            out_ref[...] += term


def skip_back_kernel(
    grad_ref,
    low_ref,
    resid_ref,
    skip_ref,
    gain_ref,
    weight_ref,
    weight_out,
    resid_out,
    skip_out,
    gain_out,
    norm_grad,
    leaving,
    grad_sibling,
    low_sibling,
    sems,
):
    tokens, width = resid_ref.shape
    parts, _, depth = weight_ref.shape
    blocks = LATENTS * rank_count()
    local = width // blocks
    step = tokens // CHUNKS
    sibling = peers_along("core")[2][0][1]
    core = lax.axis_index("core")
    greet([sibling])
    grad_low = grad_ref[...].astype(B16)
    even, odd = [], []
    for block in range(0, blocks, 2):
        even.append(grad_ref[:, block * local : (block + 1) * local])
        odd.append(grad_ref[:, (block + 1) * local : (block + 2) * local])
    even, odd = jnp.concatenate(even, axis=1), jnp.concatenate(odd, axis=1)
    leaving[...] = jnp.where(core == 0, odd, even).astype(B16)
    staying = jnp.where(core == 0, even, odd).astype(B16)
    copies = [
        remote(leaving, grad_sibling, sems, 0, sibling),
        remote(low_ref, low_sibling, sems, 1, sibling),
    ]
    for copy in copies:
        copy.start()
    for part in range(parts):
        columns = slice(part * depth, (part + 1) * depth)
        norm_grad[:, columns] = dot(grad_low, weight_ref[part], 1, 0)
    for index in range(CHUNKS):
        span = pl.ds(index * step, step)
        joined = jnp.concatenate([resid_ref[span], skip_ref[span].astype(F32)], axis=1)
        normed, rstd = norm_stats(joined)
        grad = norm_grad[span]
        add_rows(gain_out, index, grad * normed)
        value = norm_back(normed, rstd, grad * gain_ref[...])
        resid_out[span] = value[:, :width]
        skip_out[span] = value[:, width:]
    for copy in copies:
        copy.wait()
    mine_t, theirs_t = staying.T, grad_sibling[...].T
    for part in range(parts):
        columns = slice(part * depth, (part + 1) * depth)
        term = dot(mine_t, low_ref[:, columns], 1, 0)
        term = term + dot(theirs_t, low_sibling[:, columns], 1, 0)
        weight_out[part] = term.astype(B16)


def local_call(name, body, args, shapes, scratch=(), params=None):
    return pl.pallas_call(
        body,
        out_shape=shapes,
        in_specs=[pl.BlockSpec(memory_space=pltpu.VMEM)] * len(args),
        out_specs=[pl.BlockSpec(memory_space=pltpu.VMEM)] * len(shapes),
        scratch_shapes=list(scratch),
        name=name,
        compiler_params=params or pltpu.CompilerParams(vmem_limit_bytes=VMEM_LIMIT),
    )(*args)


def skip_forward(resid, skip, gain, weight):
    tokens, width = resid.shape
    shapes = [
        jax.ShapeDtypeStruct((tokens, 2 * width), B16),
        jax.ShapeDtypeStruct((tokens, width), F32),
    ]
    return local_call("skip", skip_kernel, [resid, skip, gain, weight], shapes)


def skip_backward(grad, low, resid, skip, gain, weight):
    tokens, width = resid.shape
    parts, _, depth = weight.shape
    half = width // 2
    shapes = [
        jax.ShapeDtypeStruct((parts, half, depth), B16),
        jax.ShapeDtypeStruct(resid.shape, F32),
        jax.ShapeDtypeStruct(resid.shape, F32),
        jax.ShapeDtypeStruct(gain.shape, F32),
    ]
    scratch = [
        pltpu.VMEM((tokens, 2 * width), F32),
        pltpu.VMEM((tokens, half), B16),
        pltpu.VMEM((tokens, half), B16),
        pltpu.VMEM((tokens, 2 * width), B16),
        pltpu.SemaphoreType.DMA((2, 2)),
    ]
    args = [grad, low, resid, skip, gain, weight]
    params = comm_params(number_of("skip_back", ()))
    return local_call("skip_back", skip_back_kernel, args, shapes, scratch, params)


def on_device(
    latent,
    skips,
    cond,
    text,
    skip_gain,
    attn_gain,
    ffn_gain,
    skip_w,
    mod_w,
    qkv_w,
    out_w,
    cq_w,
    ckv_w,
    cout_w,
    fc1_w,
    fc2_w,
    cotangent,
):
    rows = lax.axis_size("row")
    ranks = rank_count()
    row = lax.axis_index("row")
    lat = lax.axis_index("lat")
    rank = here()[2]
    width = latent.shape[1]
    depth = qkv_w.shape[2]
    local = qkv_w.shape[3]
    hidden_local = fc1_w.shape[2]
    layers = skip_w.shape[0]
    text_depth = ckv_w.shape[2]
    text_count = text.shape[1]
    tables = rotary_tables()


    def gather_both(pack, other, sizes):
        low, high = jnp.where(lat == 0, pack, other), jnp.where(lat == 0, other, pack)
        pieces, start = [], 0
        for size in sizes:
            pieces += [low[:, start : start + size], high[:, start : start + size]]
            start += size
        return lax.all_gather(jnp.concatenate(pieces, axis=1), "row", axis=0, tiled=True)

    attn_pack, cross_pack, text_pack, up_pack, down_pack = [], [], [], [], []
    attn_full, cross_full, text_full_w = [], [], []
    for layer in range(layers):
        attn_pack.append(
            jnp.concatenate(
                [qkv_w[layer, 0], qkv_w[layer, 1], qkv_w[layer, 2], out_w[layer].T], axis=1
            )
        )
        cross_pack.append(jnp.concatenate([cq_w[layer], cout_w[layer].T], axis=1))
        text_pack.append(jnp.concatenate([ckv_w[layer, 0], ckv_w[layer, 1]], axis=1))
        up_pack.append(fc1_w[layer])
        down_pack.append(fc2_w[layer].T)

    cond_rows, shift, others = start_call(
        cond, mod_w, [swap(attn_pack[0])]
    )
    attn_full.append(gather_both(attn_pack[0], others[0], [local] * 4))


    def stack(array):
        return [("gather", "lat", 0, None, array)]

    def gather_one(array):
        return [("gather", "b", 0, 0, array), ("gather", "a", 0, 1, array)]

    def gather_two(halves):
        return [("gather", "a", 0, None, halves[0]), ("gather", "b", 1, None, halves[1])]

    def whole(halves):
        return [half.reshape(width, -1) for half in halves]

    grad = cotangent.astype(F32)
    grad_all, cross_other, text_other, up_stack, skip_blocks = spread_tokens(
        grad, [swap(cross_pack[0]), swap(text_pack[0])] + stack(up_pack[0]), skip_w[0].T
    )
    skip_full = [skip_blocks.reshape(rows, width, -1)]
    down_stack = down_half = None

    def own_text(text):
        text_parts = lax.all_gather(text, ("lat", "chip", "core"), axis=0)
        text_own = lax.dynamic_index_in_dim(text_parts, lat, axis=1, keepdims=False)
        text_own = jnp.transpose(text_own, (1, 0, 2)).reshape(text_count, -1)
        return jnp.pad(text_own, ((0, -text_count % 128), (0, 0)))

    wide = LATENTS * local

    def thirds(stack, count):
        return [stack[index * wide : (index + 1) * wide] for index in range(count)]

    resid = latent.astype(F32)
    saved = []
    for layer in range(layers):
        keep = {}
        keep["skip_in"] = resid
        keep["skip_low"], resid_one = skip_forward(
            resid, skips[layer], skip_gain[layer : layer + 1], skip_full[layer]
        )
        keep["first"] = resid_one
        following = layer + 1 < layers
        if layer == 0:
            riders = gather_one(up_stack) + stack(down_pack[0])
        else:
            riders = [swap(cross_pack[layer]), swap(text_pack[layer])]
        first_all, *others = first_tokens(
            resid_one, attn_gain[layer, 0:1], shift[layer : layer + 1], riders
        )
        if layer == 0:
            up_half, down_stack = others[:2], others[2]
            text_own = own_text(lax.optimization_barrier((text, cross_other))[0])
        else:
            cross_other, text_other = others
        cross_full.append(gather_both(cross_pack[layer], cross_other, [local] * 2))
        text_full_w.append(gather_both(text_pack[layer], text_other, [local] * 2))
        keep["first_all"] = first_all
        weight = attn_full[layer]
        query, keys, values = thirds(dot(weight[:, : 3 * wide], first_all, 0, 1), 3)
        self_low, self_lse = attention(query, keys, values, tables, SEQ, True)
        keep["self"] = (query, keys, values, self_lse, self_low)
        out_t = weight[:, 3 * wide :]
        keep["out_t"] = out_t
        if following:
            skip_next, self_low = lax.optimization_barrier((skip_w[layer + 1].T, self_low))
            skip_full.append(
                lax.all_gather(skip_next, ("row", "lat", "chip", "core"), axis=0).reshape(
                    rows, width, -1
                )
            )
        riders = gather_two(up_half) + gather_one(down_stack)
        if following:
            riders.append(swap(attn_pack[layer + 1]))
        resid_two, third_all, *others = middle_tokens(
            (True, [self_low], [out_t]), resid_one, attn_gain[layer, 1:2], riders
        )
        up_w, down_half = whole(others[:2]), others[2:4]
        if following:
            attn_full.append(gather_both(attn_pack[layer + 1], others[4], [local] * 4))
        keep["third"] = resid_two
        keep["third_all"] = third_all
        weight = cross_full[layer]
        query_w, cout_t = weight[:, :wide], weight[:, wide:]
        keep["cross_w"] = (query_w, cout_t)
        cross_query = dot(query_w, third_all, 0, 1)
        text_keys, text_values = thirds(dot(text_full_w[layer], text_own, 0, 1), 2)
        cross_low, cross_lse = attention(
            cross_query, text_keys, text_values, tables, text_count, False
        )
        keep["cross"] = (cross_query, text_keys, text_values, cross_lse, cross_low)
        riders = gather_two(down_half) + (stack(up_pack[layer + 1]) if following else [])
        resid_three, second_all, *others = middle_tokens(
            (True, [cross_low], [cout_t]),
            resid_two,
            ffn_gain[layer : layer + 1],
            riders,
        )
        down_w = whole(others[:2])
        if following:
            up_stack = others[2]
        keep["second"] = resid_three
        keep["second_all"] = second_all
        hidden = [dot(second_all, up_w[part], 1, 0) for part in range(LATENTS)]
        act_low = [gelu_tanh(part).astype(B16) for part in hidden]
        keep["hidden"] = hidden
        keep["act"] = act_low
        keep["ffn_w"] = (up_w, down_w)
        term = (False, act_low, down_w)
        if following:
            riders = gather_one(up_stack) + stack(down_pack[layer + 1])
        if following:
            resid, *others = last_tokens(term, resid_three, riders)
        if following:
            up_half, down_stack = others[:2], others[2]
        saved.append(keep)

    final_term, final_resid = term, resid_three

    def sum_over_rows(parts, counts):
        pieces = []
        for part, count in zip(parts, counts):
            pieces += [
                part[:, index * local : (index + 1) * local].astype(B16)
                for index in range(LATENTS * count)
            ]
        packed = jnp.concatenate(pieces[0::2] + pieces[1::2], axis=1)
        summed = lax.psum_scatter(packed, "row", scatter_dimension=0, tiled=True)
        half = summed.shape[1] // 2
        low, high = summed[:, :half], summed[:, half:]
        return jnp.where(lat == 0, low, high), jnp.where(lat == 0, high, low)

    def finish(mine, other):
        total = mine.astype(F32) + other.astype(F32)
        return [
            total[:, start : start + local] for start in range(0, total.shape[1], local)
        ]

    fast = rows // 2
    slow_at, fast_at = row // fast, row % fast

    def by_rows(value):
        return value.astype(B16).reshape(2, fast, -1, value.shape[1])

    def pick(value, index, axis):
        return lax.dynamic_index_in_dim(value, index, axis=axis, keepdims=False).astype(F32)

    def scatter_one(halves):
        return [("scatter", "a", 0, None, halves[0]), ("scatter", "b", 1, None, halves[1])]

    def added_one(halves, arrived):
        low = pick(halves[0], slow_at, 0) + jnp.sum(arrived[0].astype(F32), axis=0)
        high = pick(halves[1], fast_at, 1) + jnp.sum(arrived[1].astype(F32), axis=0)
        return [low.astype(B16), high.astype(B16)]

    def chip_rider(value):
        return ("scatter", "chip", 1, None, value)

    def added_chips(value, arrived):
        total = pick(value, rank // 2, 1) + jnp.sum(arrived.astype(F32), axis=0)
        mine = jnp.where(lat == 0, total[0], total[1])
        return mine, jnp.where(lat == 0, total[1], total[0]).astype(B16)

    def scatter_two(halves):
        return [("scatter", "b", 0, None, halves[0]), ("scatter", "a", 0, None, halves[1])]

    def added_two(halves, arrived):
        low = pick(halves[0], fast_at, 0) + jnp.sum(arrived[0].astype(F32), axis=0)
        high = pick(halves[1], slow_at, 0) + jnp.sum(arrived[1].astype(F32), axis=0)
        mine = jnp.where(lat == 0, low, high)
        return mine, jnp.where(lat == 0, high, low).astype(B16)

    text_grad = jnp.zeros(text_own.shape, F32)
    weight_store = [None] * layers
    gain_store = [None] * layers
    skip_store = [None] * layers
    shift_store = [None] * layers
    waiting = None
    for layer in range(layers - 1, -1, -1):
        keep = saved[layer]
        up_w, down_w = keep["ffn_w"]
        if waiting is not None:
            grad_all, other = spread_tokens(grad, [swap(waiting["down"][1])])
            waiting["store"]["down"] = waiting["down"][0] + other.astype(F32)
        ups, downs, hidden_grads = [], [], []
        for part in range(LATENTS):
            act_grad = dot(grad_all, down_w[part], 1, 0)
            hidden_grad = (act_grad * gelu_grad(keep["hidden"][part])).astype(B16)
            downs.append(by_rows(dot(grad_all, keep["act"][part], 0, 0)))
            ups.append(by_rows(dot(keep["second_all"], hidden_grad, 0, 0)))
            hidden_grads.append(hidden_grad)
        riders = scatter_one(ups)
        if waiting is not None:
            riders.append(chip_rider(waiting["skip"]))
        names = ("attn", "cross", "text")
        if waiting is not None:
            riders += [swap(waiting[name][1]) for name in names]
        grad_three, gain_ffn, grad_all, *others = back_tokens(
            (False, hidden_grads, up_w), grad, keep["second"], ffn_gain[layer : layer + 1], riders
        )
        ups = added_one(ups, others[:2])
        if waiting is not None:
            waiting["skip"] = added_chips(waiting["skip"], others[2])
            for name, other in zip(names, others[3:]):
                waiting["store"][name] = finish(waiting[name][0], other)

        query_w, cout_t = keep["cross_w"]
        cross_query, text_keys, text_values, cross_lse, cross_low = keep["cross"]
        out_grad = dot(cout_t, grad_all, 0, 1).astype(B16)
        cout_grad = dot(grad_all, cross_low, 0, 1)
        query_grad, keys_grad, values_grad = attention_back(
            cross_query, text_keys, text_values, cross_lse, out_grad, tables, text_count, False
        )
        cq_grad = dot(keep["third_all"], query_grad, 0, 1)
        cross_sum = sum_over_rows([cq_grad, cout_grad], [1, 1])
        both = jnp.concatenate([keys_grad, values_grad], axis=0)
        text_sum = sum_over_rows([dot(text_own, both, 0, 1)], [2])
        text_grad = text_grad + dot(both, text_full_w[layer], 0, 1)
        riders = scatter_two(ups) + scatter_one(downs)
        if waiting is not None:
            riders.append(swap(waiting["skip"][1]))
        grad_two, gain_cross, grad_all, *others = back_tokens(
            (True, [query_grad], [query_w]),
            grad_three,
            keep["third"],
            attn_gain[layer, 1:2],
            riders,
        )
        up_mine, up_theirs = added_two(ups, others[:2])
        downs = added_one(downs, others[2:4])
        if waiting is not None:
            waiting["store"]["skip"] = waiting["skip"][0] + others[4].astype(F32)

        weight = attn_full[layer]
        query, keys, values, self_lse, self_low = keep["self"]
        out_grad = dot(keep["out_t"], grad_all, 0, 1).astype(B16)
        wout_grad = dot(grad_all, self_low, 0, 1)
        three = attention_back(query, keys, values, self_lse, out_grad, tables, SEQ, True)
        both = jnp.concatenate(three, axis=0)
        qkv_grad = dot(keep["first_all"], both, 0, 1)
        riders = scatter_two(downs) + [swap(up_theirs)]
        if layer == 0:
            blocks = text_grad[:text_count].astype(B16).reshape(text_count, LATENTS * ranks, -1)
            blocks = jnp.transpose(blocks, (1, 0, 2))
            blocks = lax.all_to_all(
                blocks, ("lat", "chip", "core"), split_axis=0, concat_axis=0, tiled=True
            )
            both, blocks = lax.optimization_barrier((both, blocks))
            text_out = jnp.sum(
                blocks.astype(F32).reshape((LATENTS, ranks) + blocks.shape[1:]), axis=1
            )
            riders += [swap(cross_sum[1]), swap(text_sum[1])]
        grad_one, gain_self, shift_own, *others = back_last_tokens(
            (True, [both], [weight[:, : 3 * wide]]),
            grad_two,
            keep["first"],
            attn_gain[layer, 0:1],
            riders,
        )
        down_sum = added_two(downs, others[:2])
        up_grad = up_mine + others[2].astype(F32)
        early = others[3:]
        attn_sum = sum_over_rows([qkv_grad, wout_grad], [3, 1])

        packed, grad, skip_store[layer], gain_skip = skip_backward(
            grad_one,
            keep["skip_low"],
            keep["skip_in"],
            skips[layer],
            skip_gain[layer : layer + 1],
            skip_full[layer],
        )
        skip_sum = lax.psum_scatter(packed, "row", scatter_dimension=0, tiled=False)
        skip_sum = skip_sum.reshape(LATENTS, ranks // 2, local, -1)
        gain_store[layer] = (gain_skip[0], jnp.concatenate([gain_self, gain_cross]), gain_ffn[0])
        store = dict(up=up_grad)
        waiting = dict(attn=attn_sum, cross=cross_sum, text=text_sum, down=down_sum, store=store)
        waiting["skip"] = skip_sum
        weight_store[layer] = store
        shift_store[layer] = shift_own

    sizes = [gain_store[0][slot].size for slot in range(3)] + [width]
    flat = jnp.concatenate(
        [
            gain_store[layer][slot].reshape(-1)
            for slot in range(3)
            for layer in range(layers)
        ]
        + [shift_store[layer].reshape(-1) for layer in range(layers)]
    )
    flat = jnp.pad(flat, (0, -flat.size % 1024)).reshape(-1, 128)
    flat_all, down_other = end_call(flat, [swap(waiting["down"][1])])
    waiting["store"]["down"] = waiting["down"][0] + down_other.astype(F32)
    final_resid, flat_all = lax.optimization_barrier((final_resid, flat_all))
    riders = [chip_rider(waiting["skip"]), swap(waiting["attn"][1])]
    mixed, arrived, attn_other = last_tokens(final_term, final_resid, riders)
    mine, theirs = added_chips(waiting["skip"], arrived)
    other = lax.ppermute(theirs, "lat", [(0, 1), (1, 0)])
    waiting["store"]["skip"] = mine + other.astype(F32)
    for name, other in zip(names, [attn_other] + early):
        waiting["store"][name] = finish(waiting[name][0], other)
    flat_all = flat_all.reshape(rows * LATENTS, -1)
    totals = jnp.sum(flat_all, axis=0)
    gains, start = [], 0
    for slot in range(3):
        size = layers * sizes[slot]
        gains.append(
            totals[start : start + size].reshape((layers,) + gain_store[0][slot].shape)
        )
        start += size
    shift_grad = flat_all[:, start : start + layers * width].reshape(-1, layers, width)
    column = (lat * ranks + rank) * local
    shift_cols = lax.dynamic_slice_in_dim(shift_grad, column, local, axis=2).astype(B16)

    weight_store = [
        (
            store["skip"].T,
            dot(cond_rows, shift_cols[:, layer], 0, 0),
            jnp.stack(store["attn"][:3]),
            store["attn"][3].T,
            store["cross"][0],
            jnp.stack(store["text"]),
            store["cross"][1].T,
            store["up"],
            store["down"].T,
        )
        for layer, store in enumerate(weight_store)
    ]
    weight_outs = tuple(
        jnp.stack([weight_store[layer][slot] for layer in range(layers)]) for slot in range(9)
    )
    return (mixed, grad, jnp.stack(skip_store), text_out) + tuple(gains) + weight_outs


def solution(mesh):
    NUMBERS.clear()
    rows, columns = mesh.shape["row"], mesh.shape["col"]
    grid = Mesh(
        mesh.devices.reshape(rows, LATENTS, columns // (2 * LATENTS), 2),
        ("row", "lat", "chip", "core"),
    )
    col = ("lat", "chip", "core")
    tokens = ("row", "lat", "chip", "core")
    return jax.shard_map(
        on_device,
        mesh=grid,
        in_specs=(
            P(tokens, None),
            P(None, tokens, None),
            P("row", None),
            P("row", None, col),
            P(),
            P(),
            P(),
            P(None, "row", col),
            P(None, "row", col),
            P(None, None, "row", col),
            P(None, col, "row"),
            P(None, "row", col),
            P(None, None, "row", col),
            P(None, col, "row"),
            P(None, "row", col),
            P(None, col, "row"),
            P(tokens, None),
        ),
        out_specs=(
            P(tokens, None),
            P(tokens, None),
            P(None, tokens, None),
            P("row", None, col),
            P(),
            P(),
            P(),
            P(None, "row", col),
            P(None, "row", col),
            P(None, None, "row", col),
            P(None, col, "row"),
            P(None, "row", col),
            P(None, None, "row", col),
            P(None, col, "row"),
            P(None, "row", col),
            P(None, col, "row"),
        ),
        check_vma=False,
    )
```

```python
import functools

import jax
import jax.numpy as jnp
from jax import lax
from jax.experimental import pallas as pl
from jax.experimental.pallas import tpu as pltpu
from jax.sharding import Mesh
from jax.sharding import PartitionSpec as P

HD = 88
SIDE = 32
SEQ = 1024
LATENTS = 2

HIGHEST = lax.Precision.HIGHEST
EPSILON = 1e-06
F32 = jnp.float32
B16 = jnp.bfloat16
SCALE = HD ** (-0.5)
VMEM_LIMIT = 48 * 2**20


def norm_stats(value):
    center = value - jnp.mean(value, axis=-1, keepdims=True)
    spread = jnp.mean(center * center, axis=-1, keepdims=True)
    rstd = lax.rsqrt(spread + EPSILON)
    return center * rstd, rstd


def norm_back(normed, rstd, grad):
    return rstd * (
        grad
        - jnp.mean(grad, axis=-1, keepdims=True)
        - normed * jnp.mean(grad * normed, axis=-1, keepdims=True)
    )


def silu(value):
    return value * jax.nn.sigmoid(value)


def gelu_tanh(value):
    inner = 0.7978845608028654 * (value + 0.044715 * value * value * value)
    return 0.5 * value * (1.0 + jnp.tanh(inner))


def gelu_grad(value):
    inner = 0.7978845608028654 * (value + 0.044715 * value * value * value)
    tanh = jnp.tanh(inner)
    slope = 0.7978845608028654 * (1.0 + 3.0 * 0.044715 * value * value)
    return 0.5 * (1.0 + tanh) + 0.5 * value * (1.0 - tanh * tanh) * slope


def rotary_tables():
    place = jnp.arange(SEQ, dtype=jnp.int32)
    grid_row = (place // SIDE).astype(F32)
    grid_col = (place % SIDE).astype(F32)
    feature = jnp.arange(HD, dtype=jnp.int32)
    pair = feature // 2
    quarter = HD // 4
    power = (pair % quarter).astype(F32) * (4.0 / HD)
    freq = jnp.exp(-power * jnp.log(10000.0))
    coordinate = jnp.where(pair[:, None] < quarter, grid_row[None, :], grid_col[None, :])
    angle = coordinate * freq[:, None]
    sign = jnp.where(feature % 2 == 0, -1.0, 1.0)[:, None]
    return (jnp.cos(angle), jnp.sin(angle) * sign)


def swap_rows(value):
    down = pltpu.roll(value, 1, 0)
    up = pltpu.roll(value, value.shape[0] - 1, 0)
    even = lax.broadcasted_iota(jnp.int32, value.shape, 0) % 2 == 0
    return jnp.where(even, up, down)


def head_stats(value):
    center = value - jnp.mean(value, axis=0, keepdims=True)
    rstd = lax.rsqrt(jnp.mean(center * center, axis=0, keepdims=True) + EPSILON)
    return center * rstd, rstd


def head_back(normed, rstd, grad):
    return rstd * (
        grad
        - jnp.mean(grad, axis=0, keepdims=True)
        - normed * jnp.mean(grad * normed, axis=0, keepdims=True)
    )


QUERY_CHUNK = 1024
BACK_CHUNK = 512


def attention_kernel(
    count, turn, query_ref, keys_ref, values_ref, cos_ref, sin_ref, out_ref, logsum_ref
):
    cos, sin = cos_ref[...], sin_ref[...]
    query = head_stats(query_ref[...])[0]
    query_low = (query * cos + swap_rows(query) * sin).astype(B16)
    keys = head_stats(keys_ref[...])[0]
    if turn:
        keys = keys * cos + swap_rows(keys) * sin
    keys_t = keys.astype(B16).T
    values_low = values_ref[...].astype(B16)
    for start in range(0, query_low.shape[1], QUERY_CHUNK):
        span = slice(start, start + QUERY_CHUNK)
        scores = jnp.dot(keys_t, query_low[:, span], preferred_element_type=F32) * SCALE
        if count < keys_t.shape[0]:
            inside = lax.broadcasted_iota(jnp.int32, scores.shape, 0) < count
            scores = jnp.where(inside, scores, -1e30)
        highest = jnp.max(scores, axis=0, keepdims=True)
        expo = jnp.exp(scores - highest)
        total = jnp.sum(expo, axis=0, keepdims=True)
        probs_low = (expo * (1.0 / total)).astype(B16)
        out = jnp.dot(values_low, probs_low, preferred_element_type=F32)
        out_ref[:, span] = out.astype(B16)
        logsum_ref[0, :, span] = highest + jnp.log(total)


def attention_back_kernel(
    count,
    turn,
    query_ref,
    keys_ref,
    values_ref,
    logsum_ref,
    grad_ref,
    cos_ref,
    sin_ref,
    query_out,
    keys_out,
    values_out,
    keys_sum,
    values_sum,
):
    cos, sin = cos_ref[...], sin_ref[...]
    query, query_rstd = head_stats(query_ref[...])
    query_low = (query * cos + swap_rows(query) * sin).astype(B16)
    keys, keys_rstd = head_stats(keys_ref[...])
    keys_low = (keys * cos + swap_rows(keys) * sin if turn else keys).astype(B16)
    keys_t = keys_low.T
    values_t = values_ref[...].astype(B16).T
    grad = grad_ref[...]
    grad_t = grad.T
    query_t = query_low.T
    query_grad = []
    for start in range(0, query_low.shape[1], BACK_CHUNK):
        span = slice(start, start + BACK_CHUNK)
        scores = jnp.dot(keys_t, query_low[:, span], preferred_element_type=F32)
        probs = jnp.exp(scores * SCALE - logsum_ref[0, :, span])
        if count < keys_t.shape[0]:
            inside = lax.broadcasted_iota(jnp.int32, scores.shape, 0) < count
            probs = jnp.where(inside, probs, 0.0)
        values_part = jnp.dot(probs.astype(B16), grad_t[span], preferred_element_type=F32)
        probs_grad = jnp.dot(values_t, grad[:, span], preferred_element_type=F32)
        delta = jnp.sum(probs * probs_grad, axis=0, keepdims=True)
        scores_grad = (probs * (probs_grad - delta)).astype(B16)
        query_grad.append(jnp.dot(keys_low, scores_grad, preferred_element_type=F32))
        keys_part = jnp.dot(scores_grad, query_t[span], preferred_element_type=F32)
        if start == 0:
            values_sum[...] = values_part
            keys_sum[...] = keys_part
        else:
            values_sum[...] += values_part
            keys_sum[...] += keys_part
    grad_query = jnp.concatenate(query_grad, axis=1) * SCALE
    grad_query = grad_query * cos - swap_rows(grad_query) * sin
    query_out[...] = head_back(query, query_rstd, grad_query).astype(B16)
    grad_keys = keys_sum[...].T * SCALE
    if turn:
        grad_keys = grad_keys * cos - swap_rows(grad_keys) * sin
    keys_out[...] = head_back(keys, keys_rstd, grad_keys).astype(B16)
    values_out[...] = values_sum[...].T.astype(B16)


def head_block(columns):
    return pl.BlockSpec((HD, columns), lambda head: (head, 0))


def logsum_block(columns):
    return pl.BlockSpec((1, 1, columns), lambda head: (head, 0, 0))


def attention(query, keys, values, tables, count, turn):
    heads, tokens, others = query.shape[0] // HD, query.shape[1], keys.shape[1]
    table = pl.BlockSpec((HD, tokens), lambda head: (0, 0))
    work = heads * tokens * others
    return pl.pallas_call(
        functools.partial(attention_kernel, count, turn),
        grid=(heads,),
        in_specs=[head_block(tokens), head_block(others), head_block(others), table, table],
        out_specs=[head_block(tokens), logsum_block(tokens)],
        out_shape=[
            jax.ShapeDtypeStruct(query.shape, B16),
            jax.ShapeDtypeStruct((heads, 1, tokens), F32),
        ],
        compiler_params=pltpu.CompilerParams(vmem_limit_bytes=VMEM_LIMIT),
        cost_estimate=pl.CostEstimate(
            flops=4 * HD * work, bytes_accessed=8 * query.size, transcendentals=work
        ),
    )(query, keys, values, *tables)


def attention_back(query, keys, values, logsum, grad_low, tables, count, turn):
    heads, tokens, others = query.shape[0] // HD, query.shape[1], keys.shape[1]
    table = pl.BlockSpec((HD, tokens), lambda head: (0, 0))
    work = heads * tokens * others
    return pl.pallas_call(
        functools.partial(attention_back_kernel, count, turn),
        grid=(heads,),
        in_specs=[
            head_block(tokens),
            head_block(others),
            head_block(others),
            logsum_block(tokens),
            head_block(tokens),
            table,
            table,
        ],
        out_specs=[head_block(tokens), head_block(others), head_block(others)],
        out_shape=[
            jax.ShapeDtypeStruct(value.shape, B16) for value in (query, keys, values)
        ],
        scratch_shapes=[pltpu.VMEM((others, HD), F32), pltpu.VMEM((others, HD), F32)],
        compiler_params=pltpu.CompilerParams(vmem_limit_bytes=VMEM_LIMIT),
        cost_estimate=pl.CostEstimate(
            flops=10 * HD * work, bytes_accessed=16 * query.size, transcendentals=work
        ),
    )(query, keys, values, logsum, grad_low, *tables)


MESH = pl.DeviceIdType.MESH
CHUNKS = 4
NUMBERS = {}


def number_of(name, key):
    return NUMBERS.setdefault((name, key), len(NUMBERS))


def here():
    rank = 2 * lax.axis_index("chip") + lax.axis_index("core")
    return lax.axis_index("row"), lax.axis_index("lat"), rank


def rank_count():
    return 2 * lax.axis_size("chip")


def device_at(row, lat, rank):
    return {"row": row, "lat": lat, "chip": rank // 2, "core": rank % 2}


def row_peers():
    row, lat, rank = here()
    rows = lax.axis_size("row")
    return [((row + step) % rows, device_at((row + step) % rows, lat, rank)) for step in range(1, rows)]


def peers_along(axis):
    row, lat, rank = here()
    if axis == "core":
        other = 1 - rank % 2
        return rank % 2, 2, [(other, device_at(row, lat, rank // 2 * 2 + other))]
    if axis == "chip":
        count = rank_count() // 2
        me = rank // 2
        places = [(me + step) % count for step in range(1, count)]
        return me, count, [(place, device_at(row, lat, 2 * place + rank % 2)) for place in places]
    if axis == "lat":
        return lat, LATENTS, [(1 - lat, device_at(row, 1 - lat, rank))]
    fast = lax.axis_size("row") // 2
    slow_at, fast_at = row // fast, row % fast
    if axis == "a":
        other = 1 - slow_at
        return slow_at, 2, [(other, device_at(other * fast + fast_at, lat, rank))]
    others = [(fast_at + step) % fast for step in range(1, fast)]
    return fast_at, fast, [(other, device_at(slow_at * fast + other, lat, rank)) for other in others]


def lat_peer():
    return peers_along("lat")[2][0][1]


def places():
    row, lat, rank = here()
    chips = rank_count() // 2
    chip, core = rank // 2, rank % 2
    sibling = device_at(row, lat, 2 * chip + 1 - core)
    ahead = [(chip + step) % chips for step in range(1, chips)]
    behind = [(chip + chips - step) % chips for step in range(1, chips)]
    return rank, chip, core, sibling, ahead, behind


def chip_peer(chip, core):
    row, lat, _ = here()
    return device_at(row, lat, 2 * chip + core)


def greet(others):
    barrier = pltpu.get_barrier_semaphore()
    for device in others:
        pl.semaphore_signal(barrier, inc=1, device_id=device, device_id_type=MESH)
    pl.semaphore_wait(barrier, len(others))


def remote(source, target, sems, index, device):
    return pltpu.make_async_remote_copy(
        src_ref=source,
        dst_ref=target,
        send_sem=sems.at[0, index],
        recv_sem=sems.at[1, index],
        device_id=device,
        device_id_type=MESH,
    )


def rider_count(axis):
    counts = {"lat": LATENTS, "a": 2, "b": lax.axis_size("row") // 2, "chip": rank_count() // 2}
    return counts[axis]


def rider_shape(rider):
    kind, axis, place, part, array = rider
    shape = array.shape if part is None else array.shape[1:]
    if kind == "gather":
        shape = shape[:place] + (rider_count(axis),) + shape[place:]
    if kind == "scatter":
        shape = (rider_count(axis) - 1,) + shape[:place] + shape[place + 1 :]
    return jax.ShapeDtypeStruct(shape, array.dtype)


def rider_scratch(modes):
    if not modes:
        return []
    most = sum(rider_count(mode[1]) for mode in modes)
    return [pltpu.SemaphoreType.DMA((2, most)), pltpu.SemaphoreType.DMA((len(modes),))]


def rider_peers(modes, met=()):
    peers = []
    for axis in ("lat", "a", "b"):
        if axis not in met and any(mode[1] == axis for mode in modes):
            peers += [device for _, device in peers_along(axis)[2]]
    return peers


def piece_of(ref, place, index):
    return ref.at[index] if place == 0 else ref.at[:, index]


def start_riders(modes, sources, targets, sems, local_sems):
    copies, index = [], 0
    for order, (mode, source, target) in enumerate(zip(modes, sources, targets)):
        kind, axis, place, part = mode
        me, _, others = peers_along(axis)
        if part is not None:
            source = source.at[part]
        for step, (other, device) in enumerate(others):
            if kind == "swap":
                copies.append(remote(source, target, sems, index, device))
            if kind == "gather":
                copies.append(remote(source, piece_of(target, place, me), sems, index, device))
            if kind == "scatter":
                piece = piece_of(source, place, other)
                copies.append(remote(piece, target.at[step], sems, index, device))
            index += 1
        if kind == "gather":
            own = piece_of(target, place, me)
            copies.append(pltpu.make_async_copy(source, own, local_sems.at[order]))
    for copy in copies:
        copy.start()
    return copies


def split_riders(riders):
    modes = tuple(rider[:4] for rider in riders)
    key = tuple((mode, rider[4].shape) for mode, rider in zip(modes, riders))
    return modes, key, [rider[4] for rider in riders], [rider_shape(rider) for rider in riders]


def swap(array):
    return ("swap", "lat", 0, None, array)


def gather_everyone(source, target, sems, local_sem, between):
    row, lat, _ = here()
    ranks = rank_count()
    rank, chip, core, sibling, ahead, _ = places()
    chips = ranks // 2
    fast_at, fast, fast_peers = peers_along("b")
    slow_at, slow, slow_peers = peers_along("a")
    counter = iter(range(sems.shape[1]))
    sent, last = [], []

    def block(at_row, at_lat, at_rank):
        return target.at[at_row, at_lat * ranks + at_rank]

    def push(piece, device, kept):
        copy = remote(piece, piece, sems, next(counter), device)
        copy.start()
        kept.append(copy)

    def landed(copies):
        for copy in copies:
            copy.wait_recv()
        sent.extend(copies)

    mine = block(row, lat, rank)
    local = pltpu.make_async_copy(source, mine, local_sem.at[0])
    local.start()
    first = remote(source, mine, sems, next(counter), lat_peer())
    first.start()

    def finish():
        local.wait()
        landed([first])
        between()
        step = []
        for place in ahead:
            for at_lat in range(LATENTS):
                push(block(row, at_lat, rank), chip_peer(place, core), step)
        landed(step)
        step = []
        for place in range(chips):
            at_rank = 2 * place + core
            for _, device in fast_peers:
                push(block(row, 0, at_rank), device, step)
            for _, device in slow_peers:
                push(block(row, 1, at_rank), device, step)
        for place in range(chips):
            for at_lat in range(LATENTS):
                push(block(row, at_lat, 2 * place + core), sibling, last)
        landed(step)
        step = []
        for place in range(chips):
            at_rank = 2 * place + core
            for index in range(fast):
                for _, device in slow_peers:
                    push(block(slow_at * fast + index, 0, at_rank), device, step)
            for index in range(slow):
                for _, device in fast_peers:
                    push(block(index * fast + fast_at, 1, at_rank), device, step)
        for place in range(chips):
            at_rank = 2 * place + core
            for index, _ in fast_peers:
                push(block(slow_at * fast + index, 0, at_rank), sibling, last)
            for index, _ in slow_peers:
                push(block(index * fast + fast_at, 1, at_rank), sibling, last)
        landed(step)
        for place in range(chips):
            at_rank = 2 * place + core
            for other, _ in slow_peers:
                for index in range(fast):
                    push(block(other * fast + index, 0, at_rank), sibling, last)
            for other, _ in fast_peers:
                for index in range(slow):
                    push(block(index * fast + other, 1, at_rank), sibling, last)
        for copy in sent:
            copy.wait_send()
        for copy in last:
            copy.wait()

    return finish


def gather_copies():
    rows, chips = lax.axis_size("row"), rank_count() // 2
    fast, slow = rows // 2, 2
    count = 1 + (chips - 1) * LATENTS + chips * (fast - 1 + slow - 1)
    count += chips * (fast * (slow - 1) + slow * (fast - 1))
    return count + chips * LATENTS * rows


def token_kernel(sums, spreads, body, n_in, n_out, modes, shared, *refs):
    refs = list(refs)
    take = lambda count: [refs.pop(0) for _ in range(count)]
    if sums:
        lefts, rights = take(sums[1]), take(sums[1])
    ins, sources = take(n_in), take(len(modes))
    block = refs.pop(0) if shared else None
    outs = take(n_out)
    everyone = refs.pop(0) if spreads else None
    targets = take(len(modes))
    blocks = refs.pop(0) if shared else None
    if sums:
        part, from_sibling, outgoing, incoming, pair_sems, sum_sems = take(6)
        if sums[0]:
            turned = take(1)
            turned[0][...] = lefts[0][...].T
            lefts = turned
    if spreads:
        chip_sems, own_sems, forward_sems = take(3)
    rank, chip, core, sibling, ahead, behind = places()
    chips = len(ahead) + 1
    rows = ins[0].shape[0]
    step = rows // CHUNKS
    spans = [pl.ds(index * step, step) for index in range(CHUNKS)]
    met = [sibling] + [chip_peer(place, core) for place in ahead]
    if shared:
        met += [device for axis in ("lat", "a", "b") for _, device in peers_along(axis)[2]]
    else:
        met += rider_peers(modes)
    greet(met)
    started, riding = [], []

    def multiply(place):
        some = pl.ds(pl.multiple_of(place * rows, 128), rows)
        term = None
        for left, right in zip(lefts, rights):
            piece = dot(left[some], right[...], 1, 1)
            term = piece if term is None else term + piece
        part[place] = term.astype(B16)


    def ride():
        if modes:
            riding.extend(start_riders(modes, sources, targets, *refs[:2]))

    if shared:
        finish_gather = gather_everyone(block, blocks, *refs[-2:], ride)
    if sums:
        pair = {}
        for order, place in enumerate(ahead + [chip]):
            multiply(2 * place + 1 - core)
            for index, span in enumerate(spans):
                copy = remote(
                    part.at[2 * place + 1 - core, span],
                    from_sibling.at[order, span],
                    pair_sems,
                    order * CHUNKS + index,
                    sibling,
                )
                copy.start()
                pair[order, index] = copy
        crossing = {}
        for order, place in enumerate(ahead):
            multiply(2 * place + core)
            for index, span in enumerate(spans):
                pair[order, index].wait_recv()
                outgoing[order, span] = (
                    part[2 * place + core, span].astype(F32)
                    + from_sibling[order, span].astype(F32)
                ).astype(B16)
                copy = remote(
                    outgoing.at[order, span],
                    incoming.at[order, span],
                    sum_sems,
                    order * CHUNKS + index,
                    chip_peer(place, core),
                )
                copy.start()
                crossing[order, index] = copy
    if not shared:
        ride()
    if sums:
        multiply(rank)
    direct = {}
    for index, span in enumerate(spans):
        total = None
        if sums:
            pair[chips - 1, index].wait_recv()
            total = part[rank, span].astype(F32) + from_sibling[chips - 1, span].astype(F32)
            for order in range(chips - 1):
                crossing[order, index].wait_recv()
                total = total + incoming[order, span].astype(F32)
        low = body(index, span, total, ins, outs)
        if spreads:
            everyone[rank, span] = low
            mine = everyone.at[rank, span]
            for order, place in enumerate(ahead):
                copy = remote(
                    mine, mine, chip_sems, order * CHUNKS + index, chip_peer(place, core)
                )
                copy.start()
                direct[order, index] = copy
            copy = remote(mine, mine, own_sems, index, sibling)
            copy.start()
            started.append(copy)
    if shared:
        finish_gather()
    if spreads:
        for index, span in enumerate(spans):
            for order, place in enumerate(behind):
                direct[order, index].wait_recv()
                landed = everyone.at[2 * place + core, span]
                copy = remote(landed, landed, forward_sems, order * CHUNKS + index, sibling)
                copy.start()
                started.append(copy)
        for copy in direct.values():
            copy.wait_send()
        for copy in started:
            copy.wait()
    if sums:
        for copy in list(pair.values()) + list(crossing.values()):
            copy.wait_send()
    for copy in riding:
        copy.wait()


def comm_params(number):
    return pltpu.CompilerParams(
        collective_id=number, has_side_effects=True, vmem_limit_bytes=VMEM_LIMIT
    )


def token_call(name, body, part, ins, outs, spreads, riders=(), shared=None):
    ranks = rank_count()
    chips = ranks // 2
    rows, width = ins[0].shape
    sums = None
    if part is not None:
        turn, lefts, rights = part
        sums = (turn, len(lefts))
    modes, key, cargo, cargo_shapes = split_riders(riders)
    shapes = [jax.ShapeDtypeStruct(shape, F32) for shape in outs]
    scratch = []
    if sums:
        key = key + tuple(left.shape for left in lefts)
        scratch += [
            pltpu.VMEM((ranks, rows, width), B16),
            pltpu.VMEM((chips, rows, width), B16),
            pltpu.VMEM((chips - 1, rows, width), B16),
            pltpu.VMEM((chips - 1, rows, width), B16),
            pltpu.SemaphoreType.DMA((2, chips * CHUNKS)),
            pltpu.SemaphoreType.DMA((2, (chips - 1) * CHUNKS)),
        ]
        if turn:
            scratch.append(pltpu.VMEM(lefts[0].shape[::-1], B16))
    if spreads:
        shapes.append(jax.ShapeDtypeStruct((ranks, rows, width), B16))
        scratch += [
            pltpu.SemaphoreType.DMA((2, (chips - 1) * CHUNKS)),
            pltpu.SemaphoreType.DMA((2, CHUNKS)),
            pltpu.SemaphoreType.DMA((2, (chips - 1) * CHUNKS)),
        ]
    scratch += rider_scratch(modes)
    if shared is not None:
        key = key + shared.shape
        cargo = cargo + [shared]
        blocks = (lax.axis_size("row"), LATENTS * ranks) + shared.shape
        cargo_shapes = cargo_shapes + [jax.ShapeDtypeStruct(blocks, shared.dtype)]
        scratch += [
            pltpu.SemaphoreType.DMA((2, gather_copies())),
            pltpu.SemaphoreType.DMA((1,)),
        ]
    args = (list(lefts) + list(rights) if sums else []) + list(ins)
    whole = pl.BlockSpec(memory_space=pltpu.VMEM)
    away = pl.BlockSpec(memory_space=pl.ANY)
    results = pl.pallas_call(
        functools.partial(
            token_kernel, sums, spreads, body, len(ins), len(outs), modes, shared is not None
        ),
        out_shape=shapes + cargo_shapes,
        in_specs=[whole] * len(args) + [away] * len(cargo),
        out_specs=[whole] * len(shapes) + [away] * len(cargo),
        scratch_shapes=scratch,
        name=name,
        compiler_params=comm_params(number_of(name, key)),
        cost_estimate=pl.CostEstimate(
            flops=20 * rows * width, bytes_accessed=12 * rows * width, transcendentals=0
        ),
    )(*args, *cargo)
    results = list(results)
    if spreads:
        place = len(outs)
        results[place] = results[place].reshape(ranks * rows, width)
    return results


def start_kernel(modes, *refs):
    refs = list(refs)
    take = lambda count: [refs.pop(0) for _ in range(count)]
    cond, mod = take(2)
    sources = take(len(modes))
    low_ref, out = take(2)
    targets = take(len(modes))
    got, terms, landed, cond_sems, term_sems, out_sems = take(6)
    row, lat, rank = here()
    rows, ranks = lax.axis_size("row"), rank_count()
    columns = LATENTS * ranks
    column = lat * ranks + rank
    others = row_peers()
    company = []
    for step in range(1, columns):
        place = (column + step) % columns
        company.append(device_at(row, place // ranks, place % ranks))
    greet([device for _, device in others] + company)
    riding = start_riders(modes, sources, targets, *refs) if modes else []
    copies = []
    got[row] = cond[row]
    for index, (other, device) in enumerate(others):
        copy = remote(cond.at[other], got.at[row], cond_sems, index, device)
        copy.start()
        copies.append(copy)
    for copy in copies:
        copy.wait()
    value = got[...]
    low = (value / (1.0 + jnp.exp(-value))).astype(B16)
    low_ref[...] = low.astype(F32)
    flat = low.reshape(rows * 8, low.shape[2])
    first = jnp.dot(flat, mod[0], preferred_element_type=F32)
    second = jnp.dot(flat, mod[1], preferred_element_type=F32)
    upper = lax.broadcasted_iota(jnp.int32, first.shape, 0) % 8 < LATENTS
    terms[...] = jnp.where(upper, first, second).reshape(terms.shape)
    copies = []
    landed[row] = terms[row]
    for index, (other, device) in enumerate(others):
        copy = remote(terms.at[other], landed.at[row], term_sems, index, device)
        copy.start()
        copies.append(copy)
    for copy in copies:
        copy.wait()
    out[column] = jnp.sum(landed[...], axis=0)
    copies = []
    for index, device in enumerate(company):
        copy = remote(out.at[column], out.at[column], out_sems, index, device)
        copy.start()
        copies.append(copy)
    for copy in copies:
        copy.wait()
    for copy in riding:
        copy.wait()


def start_call(cond, mod_w, riders):
    rows, ranks = lax.axis_size("row"), rank_count()
    layers, depth, local = mod_w.shape
    tall, wide = depth + -depth % 128, local + -local % 128
    blocks = jnp.transpose(cond.astype(F32).reshape(LATENTS, rows, depth), (1, 0, 2))
    blocks = jnp.concatenate([blocks] * layers, axis=1)
    blocks = jnp.pad(blocks, ((0, 0), (0, 8 - layers * LATENTS), (0, tall - depth)))
    mod = jnp.pad(mod_w, ((0, 0), (0, tall - depth), (0, wide - local)))
    modes, key, cargo, cargo_shapes = split_riders(riders)
    whole = pl.BlockSpec(memory_space=pltpu.VMEM)
    away = pl.BlockSpec(memory_space=pl.ANY)
    columns = LATENTS * ranks
    low, out, *rest = pl.pallas_call(
        functools.partial(start_kernel, modes),
        out_shape=[
            jax.ShapeDtypeStruct(blocks.shape, F32),
            jax.ShapeDtypeStruct((columns, 8, wide), F32),
        ]
        + cargo_shapes,
        in_specs=[whole] * 2 + [away] * len(cargo),
        out_specs=[whole] * 2 + [away] * len(cargo),
        scratch_shapes=[
            pltpu.VMEM(blocks.shape, F32),
            pltpu.VMEM((rows, 8, wide), F32),
            pltpu.VMEM((rows, 8, wide), F32),
            pltpu.SemaphoreType.DMA((2, rows - 1)),
            pltpu.SemaphoreType.DMA((2, rows - 1)),
            pltpu.SemaphoreType.DMA((2, columns - 1)),
        ]
        + rider_scratch(modes),
        name="shift",
        compiler_params=comm_params(number_of("shift", key)),
    )(blocks, mod, *cargo)
    cond_rows = low[:, :LATENTS, :depth].reshape(rows * LATENTS, depth).astype(B16)
    own = lax.dynamic_index_in_dim(
        out[:, : layers * LATENTS].reshape(columns, layers, LATENTS, wide),
        lax.axis_index("lat"),
        axis=2,
        keepdims=False,
    )
    shift = jnp.transpose(own[:, :, :local], (1, 0, 2)).reshape(layers, columns * local)
    return cond_rows, shift, rest


def end_kernel(modes, *refs):
    refs = list(refs)
    take = lambda count: [refs.pop(0) for _ in range(count)]
    (value,) = take(1)
    sources = take(len(modes))
    (out,) = take(1)
    targets = take(len(modes))
    parts, pair, part_sems, pair_sems, out_sems = take(5)
    row, lat, rank = here()
    ranks = rank_count()
    others = row_peers()
    company = [device_at(row, lat, (rank + step) % ranks) for step in range(1, ranks)]
    greet(company + [lat_peer()] + [device for _, device in others])
    riding = start_riders(modes, sources, targets, *refs) if modes else []
    copies = []
    for index, device in enumerate(company):
        copy = remote(value, parts.at[index], part_sems, index, device)
        copy.start()
        copies.append(copy)
    for copy in copies:
        copy.wait()
    pair[lat] = value[...] + jnp.sum(parts[...], axis=0)
    copy = remote(pair.at[lat], pair.at[lat], pair_sems, 0, lat_peer())
    copy.start()
    copy.wait()
    out[row] = pair[...]
    copies = []
    for index, (_, device) in enumerate(others):
        copy = remote(pair, out.at[row], out_sems, index, device)
        copy.start()
        copies.append(copy)
    for copy in copies:
        copy.wait()
    for copy in riding:
        copy.wait()


def end_call(value, riders):
    rows, ranks = lax.axis_size("row"), rank_count()
    modes, key, cargo, cargo_shapes = split_riders(riders)
    whole = pl.BlockSpec(memory_space=pltpu.VMEM)
    away = pl.BlockSpec(memory_space=pl.ANY)
    return pl.pallas_call(
        functools.partial(end_kernel, modes),
        out_shape=[jax.ShapeDtypeStruct((rows, LATENTS) + value.shape, F32)]
        + cargo_shapes,
        in_specs=[whole] + [away] * len(cargo),
        out_specs=[whole] + [away] * len(cargo),
        scratch_shapes=[
            pltpu.VMEM((ranks - 1,) + value.shape, F32),
            pltpu.VMEM((LATENTS,) + value.shape, F32),
            pltpu.SemaphoreType.DMA((2, ranks - 1)),
            pltpu.SemaphoreType.DMA((2, 1)),
            pltpu.SemaphoreType.DMA((2, rows - 1)),
        ]
        + rider_scratch(modes),
        name="gains",
        compiler_params=comm_params(number_of("gains", key)),
    )(value, *cargo)


def first_body(index, span, total, ins, outs):
    resid, gain, shift = ins
    return (norm_stats(resid[span])[0] * gain[...] + shift[...]).astype(B16)


def middle_body(index, span, total, ins, outs):
    resid, gain = ins
    value = resid[span] + total
    outs[0][span] = value
    return (norm_stats(value)[0] * gain[...]).astype(B16)


def last_body(index, span, total, ins, outs):
    outs[0][span] = ins[0][span] + total
    return None


def spread_body(index, span, total, ins, outs):
    return ins[0][span].astype(B16)


def add_rows(out, index, value):
    value = jnp.sum(value, axis=0, keepdims=True)
    if index == 0:
        out[...] = value
    else:
        out[...] += value


def back_body(index, span, total, ins, outs):
    grad, resid, gain = ins
    normed, rstd = norm_stats(resid[span])
    value = grad[span] + norm_back(normed, rstd, total * gain[...])
    outs[0][span] = value
    add_rows(outs[1], index, total * normed)
    return value.astype(B16)


def back_last_body(index, span, total, ins, outs):
    back_body(index, span, total, ins, outs)
    add_rows(outs[2], index, total)
    return None


def first_tokens(resid, gain, shift, riders=()):
    return token_call("first", first_body, None, [resid, gain, shift], [], True, riders)


def middle_tokens(part, resid, gain, riders=()):
    ins = [resid, gain]
    return token_call("middle", middle_body, part, ins, [resid.shape], True, riders)


def last_tokens(part, resid, riders=()):
    return token_call("last", last_body, part, [resid], [resid.shape], False, riders)


def spread_tokens(grad, riders=(), shared=None):
    return token_call("spread", spread_body, None, [grad], [], True, riders, shared)


def back_tokens(part, grad, resid, gain, riders=()):
    shapes = [grad.shape, gain.shape]
    ins = [grad, resid, gain]
    return token_call("back", back_body, part, ins, shapes, True, riders)


def back_last_tokens(part, grad, resid, gain, riders=()):
    shapes = [grad.shape, gain.shape, gain.shape]
    ins = [grad, resid, gain]
    return token_call("back_last", back_last_body, part, ins, shapes, False, riders)


def dot(left, right, left_dim, right_dim):
    return lax.dot_general(
        left, right, (((left_dim,), (right_dim,)), ((), ())), preferred_element_type=F32
    )


def skip_kernel(resid_ref, skip_ref, gain_ref, weight_ref, low_ref, out_ref):
    tokens, width = resid_ref.shape
    parts, _, depth = weight_ref.shape
    step = tokens // CHUNKS
    for index in range(CHUNKS):
        span = pl.ds(index * step, step)
        joined = jnp.concatenate([resid_ref[span], skip_ref[span].astype(F32)], axis=1)
        low_ref[span] = (norm_stats(joined)[0] * gain_ref[...]).astype(B16)
    for part in range(parts):
        low = low_ref[:, part * depth : (part + 1) * depth]
        term = dot(low, weight_ref[part], 1, 1)
        if part == 0:
            out_ref[...] = term
        else:
            out_ref[...] += term


def skip_back_kernel(
    grad_ref,
    low_ref,
    resid_ref,
    skip_ref,
    gain_ref,
    weight_ref,
    weight_out,
    resid_out,
    skip_out,
    gain_out,
    norm_grad,
    leaving,
    grad_sibling,
    low_sibling,
    sems,
):
    tokens, width = resid_ref.shape
    parts, _, depth = weight_ref.shape
    blocks = LATENTS * rank_count()
    local = width // blocks
    step = tokens // CHUNKS
    sibling = peers_along("core")[2][0][1]
    core = lax.axis_index("core")
    greet([sibling])
    grad_low = grad_ref[...].astype(B16)
    even, odd = [], []
    for block in range(0, blocks, 2):
        even.append(grad_ref[:, block * local : (block + 1) * local])
        odd.append(grad_ref[:, (block + 1) * local : (block + 2) * local])
    even, odd = jnp.concatenate(even, axis=1), jnp.concatenate(odd, axis=1)
    leaving[...] = jnp.where(core == 0, odd, even).astype(B16)
    staying = jnp.where(core == 0, even, odd).astype(B16)
    copies = [
        remote(leaving, grad_sibling, sems, 0, sibling),
        remote(low_ref, low_sibling, sems, 1, sibling),
    ]
    for copy in copies:
        copy.start()
    for part in range(parts):
        columns = slice(part * depth, (part + 1) * depth)
        norm_grad[:, columns] = dot(grad_low, weight_ref[part], 1, 0)
    for index in range(CHUNKS):
        span = pl.ds(index * step, step)
        joined = jnp.concatenate([resid_ref[span], skip_ref[span].astype(F32)], axis=1)
        normed, rstd = norm_stats(joined)
        grad = norm_grad[span]
        add_rows(gain_out, index, grad * normed)
        value = norm_back(normed, rstd, grad * gain_ref[...])
        resid_out[span] = value[:, :width]
        skip_out[span] = value[:, width:]
    for copy in copies:
        copy.wait()
    mine_t, theirs_t = staying.T, grad_sibling[...].T
    for part in range(parts):
        columns = slice(part * depth, (part + 1) * depth)
        term = dot(mine_t, low_ref[:, columns], 1, 0)
        term = term + dot(theirs_t, low_sibling[:, columns], 1, 0)
        weight_out[part] = term.astype(B16)


def local_call(name, body, args, shapes, scratch=(), params=None):
    return pl.pallas_call(
        body,
        out_shape=shapes,
        in_specs=[pl.BlockSpec(memory_space=pltpu.VMEM)] * len(args),
        out_specs=[pl.BlockSpec(memory_space=pltpu.VMEM)] * len(shapes),
        scratch_shapes=list(scratch),
        name=name,
        compiler_params=params or pltpu.CompilerParams(vmem_limit_bytes=VMEM_LIMIT),
    )(*args)


def skip_forward(resid, skip, gain, weight):
    tokens, width = resid.shape
    shapes = [
        jax.ShapeDtypeStruct((tokens, 2 * width), B16),
        jax.ShapeDtypeStruct((tokens, width), F32),
    ]
    return local_call("skip", skip_kernel, [resid, skip, gain, weight], shapes)


def skip_backward(grad, low, resid, skip, gain, weight):
    tokens, width = resid.shape
    parts, _, depth = weight.shape
    half = width // 2
    shapes = [
        jax.ShapeDtypeStruct((parts, half, depth), B16),
        jax.ShapeDtypeStruct(resid.shape, F32),
        jax.ShapeDtypeStruct(resid.shape, F32),
        jax.ShapeDtypeStruct(gain.shape, F32),
    ]
    scratch = [
        pltpu.VMEM((tokens, 2 * width), F32),
        pltpu.VMEM((tokens, half), B16),
        pltpu.VMEM((tokens, half), B16),
        pltpu.VMEM((tokens, 2 * width), B16),
        pltpu.SemaphoreType.DMA((2, 2)),
    ]
    args = [grad, low, resid, skip, gain, weight]
    params = comm_params(number_of("skip_back", ()))
    return local_call("skip_back", skip_back_kernel, args, shapes, scratch, params)


def on_device(
    latent,
    skips,
    cond,
    text,
    skip_gain,
    attn_gain,
    ffn_gain,
    skip_w,
    mod_w,
    qkv_w,
    out_w,
    cq_w,
    ckv_w,
    cout_w,
    fc1_w,
    fc2_w,
    cotangent,
):
    rows = lax.axis_size("row")
    ranks = rank_count()
    row = lax.axis_index("row")
    lat = lax.axis_index("lat")
    rank = here()[2]
    width = latent.shape[1]
    depth = qkv_w.shape[2]
    local = qkv_w.shape[3]
    hidden_local = fc1_w.shape[2]
    layers = skip_w.shape[0]
    text_depth = ckv_w.shape[2]
    text_count = text.shape[1]
    tables = rotary_tables()


    def gather_both(pack, other, sizes):
        low, high = jnp.where(lat == 0, pack, other), jnp.where(lat == 0, other, pack)
        pieces, start = [], 0
        for size in sizes:
            pieces += [low[:, start : start + size], high[:, start : start + size]]
            start += size
        return lax.all_gather(jnp.concatenate(pieces, axis=1), "row", axis=0, tiled=True)

    attn_pack, cross_pack, text_pack, up_pack, down_pack = [], [], [], [], []
    attn_full, cross_full, text_full_w = [], [], []
    for layer in range(layers):
        attn_pack.append(
            jnp.concatenate(
                [qkv_w[layer, 0], qkv_w[layer, 1], qkv_w[layer, 2], out_w[layer].T], axis=1
            )
        )
        cross_pack.append(jnp.concatenate([cq_w[layer], cout_w[layer].T], axis=1))
        text_pack.append(jnp.concatenate([ckv_w[layer, 0], ckv_w[layer, 1]], axis=1))
        up_pack.append(fc1_w[layer])
        down_pack.append(fc2_w[layer].T)

    cond_rows, shift, others = start_call(
        cond, mod_w, [swap(attn_pack[0])]
    )
    attn_full.append(gather_both(attn_pack[0], others[0], [local] * 4))


    def stack(array):
        return [("gather", "lat", 0, None, array)]

    def gather_one(array):
        return [("gather", "b", 0, 0, array), ("gather", "a", 0, 1, array)]

    def gather_two(halves):
        return [("gather", "a", 0, None, halves[0]), ("gather", "b", 1, None, halves[1])]

    def whole(halves):
        return [half.reshape(width, -1) for half in halves]

    grad = cotangent.astype(F32)
    grad_all, cross_other, text_other, up_stack, skip_blocks = spread_tokens(
        grad, [swap(cross_pack[0]), swap(text_pack[0])] + stack(up_pack[0]), skip_w[0].T
    )
    skip_full = [skip_blocks.reshape(rows, width, -1)]
    down_stack = down_half = None

    def own_text(text):
        text_parts = lax.all_gather(text, ("lat", "chip", "core"), axis=0)
        text_own = lax.dynamic_index_in_dim(text_parts, lat, axis=1, keepdims=False)
        text_own = jnp.transpose(text_own, (1, 0, 2)).reshape(text_count, -1)
        return jnp.pad(text_own, ((0, -text_count % 128), (0, 0)))

    wide = LATENTS * local

    def thirds(stack, count):
        return [stack[index * wide : (index + 1) * wide] for index in range(count)]

    resid = latent.astype(F32)
    saved = []
    for layer in range(layers):
        keep = {}
        keep["skip_in"] = resid
        keep["skip_low"], resid_one = skip_forward(
            resid, skips[layer], skip_gain[layer : layer + 1], skip_full[layer]
        )
        keep["first"] = resid_one
        following = layer + 1 < layers
        if layer == 0:
            riders = gather_one(up_stack) + stack(down_pack[0])
        else:
            riders = [swap(cross_pack[layer]), swap(text_pack[layer])]
        first_all, *others = first_tokens(
            resid_one, attn_gain[layer, 0:1], shift[layer : layer + 1], riders
        )
        if layer == 0:
            up_half, down_stack = others[:2], others[2]
            text_own = own_text(lax.optimization_barrier((text, cross_other))[0])
        else:
            cross_other, text_other = others
        cross_full.append(gather_both(cross_pack[layer], cross_other, [local] * 2))
        text_full_w.append(gather_both(text_pack[layer], text_other, [local] * 2))
        keep["first_all"] = first_all
        weight = attn_full[layer]
        query, keys, values = thirds(dot(weight[:, : 3 * wide], first_all, 0, 1), 3)
        self_low, self_lse = attention(query, keys, values, tables, SEQ, True)
        keep["self"] = (query, keys, values, self_lse, self_low)
        out_t = weight[:, 3 * wide :]
        keep["out_t"] = out_t
        if following:
            skip_next, self_low = lax.optimization_barrier((skip_w[layer + 1].T, self_low))
            skip_full.append(
                lax.all_gather(skip_next, ("row", "lat", "chip", "core"), axis=0).reshape(
                    rows, width, -1
                )
            )
        riders = gather_two(up_half) + gather_one(down_stack)
        if following:
            riders.append(swap(attn_pack[layer + 1]))
        resid_two, third_all, *others = middle_tokens(
            (True, [self_low], [out_t]), resid_one, attn_gain[layer, 1:2], riders
        )
        up_w, down_half = whole(others[:2]), others[2:4]
        if following:
            attn_full.append(gather_both(attn_pack[layer + 1], others[4], [local] * 4))
        keep["third"] = resid_two
        keep["third_all"] = third_all
        weight = cross_full[layer]
        query_w, cout_t = weight[:, :wide], weight[:, wide:]
        keep["cross_w"] = (query_w, cout_t)
        cross_query = dot(query_w, third_all, 0, 1)
        text_keys, text_values = thirds(dot(text_full_w[layer], text_own, 0, 1), 2)
        cross_low, cross_lse = attention(
            cross_query, text_keys, text_values, tables, text_count, False
        )
        keep["cross"] = (cross_query, text_keys, text_values, cross_lse, cross_low)
        riders = gather_two(down_half) + (stack(up_pack[layer + 1]) if following else [])
        resid_three, second_all, *others = middle_tokens(
            (True, [cross_low], [cout_t]),
            resid_two,
            ffn_gain[layer : layer + 1],
            riders,
        )
        down_w = whole(others[:2])
        if following:
            up_stack = others[2]
        keep["second"] = resid_three
        keep["second_all"] = second_all
        hidden = [dot(second_all, up_w[part], 1, 0) for part in range(LATENTS)]
        act_low = [gelu_tanh(part).astype(B16) for part in hidden]
        keep["hidden"] = hidden
        keep["act"] = act_low
        keep["ffn_w"] = (up_w, down_w)
        term = (False, act_low, down_w)
        if following:
            riders = gather_one(up_stack) + stack(down_pack[layer + 1])
        if following:
            resid, *others = last_tokens(term, resid_three, riders)
        if following:
            up_half, down_stack = others[:2], others[2]
        saved.append(keep)

    final_term, final_resid = term, resid_three

    def sum_over_rows(parts, counts):
        pieces = []
        for part, count in zip(parts, counts):
            pieces += [
                part[:, index * local : (index + 1) * local].astype(B16)
                for index in range(LATENTS * count)
            ]
        packed = jnp.concatenate(pieces[0::2] + pieces[1::2], axis=1)
        summed = lax.psum_scatter(packed, "row", scatter_dimension=0, tiled=True)
        half = summed.shape[1] // 2
        low, high = summed[:, :half], summed[:, half:]
        return jnp.where(lat == 0, low, high), jnp.where(lat == 0, high, low)

    def finish(mine, other):
        total = mine.astype(F32) + other.astype(F32)
        return [
            total[:, start : start + local] for start in range(0, total.shape[1], local)
        ]

    fast = rows // 2
    slow_at, fast_at = row // fast, row % fast

    def by_rows(value):
        return value.astype(B16).reshape(2, fast, -1, value.shape[1])

    def pick(value, index, axis):
        return lax.dynamic_index_in_dim(value, index, axis=axis, keepdims=False).astype(F32)

    def scatter_one(halves):
        return [("scatter", "a", 0, None, halves[0]), ("scatter", "b", 1, None, halves[1])]

    def added_one(halves, arrived):
        low = pick(halves[0], slow_at, 0) + jnp.sum(arrived[0].astype(F32), axis=0)
        high = pick(halves[1], fast_at, 1) + jnp.sum(arrived[1].astype(F32), axis=0)
        return [low.astype(B16), high.astype(B16)]

    def chip_rider(value):
        return ("scatter", "chip", 1, None, value)

    def added_chips(value, arrived):
        total = pick(value, rank // 2, 1) + jnp.sum(arrived.astype(F32), axis=0)
        mine = jnp.where(lat == 0, total[0], total[1])
        return mine, jnp.where(lat == 0, total[1], total[0]).astype(B16)

    def scatter_two(halves):
        return [("scatter", "b", 0, None, halves[0]), ("scatter", "a", 0, None, halves[1])]

    def added_two(halves, arrived):
        low = pick(halves[0], fast_at, 0) + jnp.sum(arrived[0].astype(F32), axis=0)
        high = pick(halves[1], slow_at, 0) + jnp.sum(arrived[1].astype(F32), axis=0)
        mine = jnp.where(lat == 0, low, high)
        return mine, jnp.where(lat == 0, high, low).astype(B16)

    text_grad = jnp.zeros(text_own.shape, F32)
    weight_store = [None] * layers
    gain_store = [None] * layers
    skip_store = [None] * layers
    shift_store = [None] * layers
    waiting = None
    for layer in range(layers - 1, -1, -1):
        keep = saved[layer]
        up_w, down_w = keep["ffn_w"]
        if waiting is not None:
            grad_all, other = spread_tokens(grad, [swap(waiting["down"][1])])
            waiting["store"]["down"] = waiting["down"][0] + other.astype(F32)
        ups, downs, hidden_grads = [], [], []
        for part in range(LATENTS):
            act_grad = dot(grad_all, down_w[part], 1, 0)
            hidden_grad = (act_grad * gelu_grad(keep["hidden"][part])).astype(B16)
            downs.append(by_rows(dot(grad_all, keep["act"][part], 0, 0)))
            ups.append(by_rows(dot(keep["second_all"], hidden_grad, 0, 0)))
            hidden_grads.append(hidden_grad)
        riders = scatter_one(ups)
        if waiting is not None:
            riders.append(chip_rider(waiting["skip"]))
        names = ("attn", "cross", "text")
        if waiting is not None:
            riders += [swap(waiting[name][1]) for name in names]
        grad_three, gain_ffn, grad_all, *others = back_tokens(
            (False, hidden_grads, up_w), grad, keep["second"], ffn_gain[layer : layer + 1], riders
        )
        ups = added_one(ups, others[:2])
        if waiting is not None:
            waiting["skip"] = added_chips(waiting["skip"], others[2])
            for name, other in zip(names, others[3:]):
                waiting["store"][name] = finish(waiting[name][0], other)

        query_w, cout_t = keep["cross_w"]
        cross_query, text_keys, text_values, cross_lse, cross_low = keep["cross"]
        out_grad = dot(cout_t, grad_all, 0, 1).astype(B16)
        cout_grad = dot(grad_all, cross_low, 0, 1)
        query_grad, keys_grad, values_grad = attention_back(
            cross_query, text_keys, text_values, cross_lse, out_grad, tables, text_count, False
        )
        cq_grad = dot(keep["third_all"], query_grad, 0, 1)
        cross_sum = sum_over_rows([cq_grad, cout_grad], [1, 1])
        both = jnp.concatenate([keys_grad, values_grad], axis=0)
        text_sum = sum_over_rows([dot(text_own, both, 0, 1)], [2])
        text_grad = text_grad + dot(both, text_full_w[layer], 0, 1)
        riders = scatter_two(ups) + scatter_one(downs)
        if waiting is not None:
            riders.append(swap(waiting["skip"][1]))
        grad_two, gain_cross, grad_all, *others = back_tokens(
            (True, [query_grad], [query_w]),
            grad_three,
            keep["third"],
            attn_gain[layer, 1:2],
            riders,
        )
        up_mine, up_theirs = added_two(ups, others[:2])
        downs = added_one(downs, others[2:4])
        if waiting is not None:
            waiting["store"]["skip"] = waiting["skip"][0] + others[4].astype(F32)

        weight = attn_full[layer]
        query, keys, values, self_lse, self_low = keep["self"]
        out_grad = dot(keep["out_t"], grad_all, 0, 1).astype(B16)
        wout_grad = dot(grad_all, self_low, 0, 1)
        three = attention_back(query, keys, values, self_lse, out_grad, tables, SEQ, True)
        both = jnp.concatenate(three, axis=0)
        qkv_grad = dot(keep["first_all"], both, 0, 1)
        riders = scatter_two(downs) + [swap(up_theirs)]
        if layer == 0:
            blocks = text_grad[:text_count].astype(B16).reshape(text_count, LATENTS * ranks, -1)
            blocks = jnp.transpose(blocks, (1, 0, 2))
            blocks = lax.all_to_all(
                blocks, ("lat", "chip", "core"), split_axis=0, concat_axis=0, tiled=True
            )
            riders += [swap(cross_sum[1]), swap(text_sum[1])]
        grad_one, gain_self, shift_own, *others = back_last_tokens(
            (True, [both], [weight[:, : 3 * wide]]),
            grad_two,
            keep["first"],
            attn_gain[layer, 0:1],
            riders,
        )
        if layer == 0:
            grad_one, blocks = lax.optimization_barrier((grad_one, blocks))
            text_out = jnp.sum(
                blocks.astype(F32).reshape((LATENTS, ranks) + blocks.shape[1:]), axis=1
            )
        down_sum = added_two(downs, others[:2])
        up_grad = up_mine + others[2].astype(F32)
        early = others[3:]
        attn_sum = sum_over_rows([qkv_grad, wout_grad], [3, 1])

        packed, grad, skip_store[layer], gain_skip = skip_backward(
            grad_one,
            keep["skip_low"],
            keep["skip_in"],
            skips[layer],
            skip_gain[layer : layer + 1],
            skip_full[layer],
        )
        skip_sum = lax.psum_scatter(packed, "row", scatter_dimension=0, tiled=False)
        skip_sum = skip_sum.reshape(LATENTS, ranks // 2, local, -1)
        gain_store[layer] = (gain_skip[0], jnp.concatenate([gain_self, gain_cross]), gain_ffn[0])
        store = dict(up=up_grad)
        waiting = dict(attn=attn_sum, cross=cross_sum, text=text_sum, down=down_sum, store=store)
        waiting["skip"] = skip_sum
        weight_store[layer] = store
        shift_store[layer] = shift_own

    sizes = [gain_store[0][slot].size for slot in range(3)] + [width]
    flat = jnp.concatenate(
        [
            gain_store[layer][slot].reshape(-1)
            for slot in range(3)
            for layer in range(layers)
        ]
        + [shift_store[layer].reshape(-1) for layer in range(layers)]
    )
    flat = jnp.pad(flat, (0, -flat.size % 1024)).reshape(-1, 128)
    flat_all, down_other = end_call(flat, [swap(waiting["down"][1])])
    waiting["store"]["down"] = waiting["down"][0] + down_other.astype(F32)
    final_resid, flat_all = lax.optimization_barrier((final_resid, flat_all))
    riders = [chip_rider(waiting["skip"]), swap(waiting["attn"][1])]
    mixed, arrived, attn_other = last_tokens(final_term, final_resid, riders)
    mine, theirs = added_chips(waiting["skip"], arrived)
    other = lax.ppermute(theirs, "lat", [(0, 1), (1, 0)])
    waiting["store"]["skip"] = mine + other.astype(F32)
    for name, other in zip(names, [attn_other] + early):
        waiting["store"][name] = finish(waiting[name][0], other)
    flat_all = flat_all.reshape(rows * LATENTS, -1)
    totals = jnp.sum(flat_all, axis=0)
    gains, start = [], 0
    for slot in range(3):
        size = layers * sizes[slot]
        gains.append(
            totals[start : start + size].reshape((layers,) + gain_store[0][slot].shape)
        )
        start += size
    shift_grad = flat_all[:, start : start + layers * width].reshape(-1, layers, width)
    column = (lat * ranks + rank) * local
    shift_cols = lax.dynamic_slice_in_dim(shift_grad, column, local, axis=2).astype(B16)

    weight_store = [
        (
            store["skip"].T,
            dot(cond_rows, shift_cols[:, layer], 0, 0),
            jnp.stack(store["attn"][:3]),
            store["attn"][3].T,
            store["cross"][0],
            jnp.stack(store["text"]),
            store["cross"][1].T,
            store["up"],
            store["down"].T,
        )
        for layer, store in enumerate(weight_store)
    ]
    weight_outs = tuple(
        jnp.stack([weight_store[layer][slot] for layer in range(layers)]) for slot in range(9)
    )
    return (mixed, grad, jnp.stack(skip_store), text_out) + tuple(gains) + weight_outs


def solution(mesh):
    NUMBERS.clear()
    rows, columns = mesh.shape["row"], mesh.shape["col"]
    grid = Mesh(
        mesh.devices.reshape(rows, LATENTS, columns // (2 * LATENTS), 2),
        ("row", "lat", "chip", "core"),
    )
    col = ("lat", "chip", "core")
    tokens = ("row", "lat", "chip", "core")
    return jax.shard_map(
        on_device,
        mesh=grid,
        in_specs=(
            P(tokens, None),
            P(None, tokens, None),
            P("row", None),
            P("row", None, col),
            P(),
            P(),
            P(),
            P(None, "row", col),
            P(None, "row", col),
            P(None, None, "row", col),
            P(None, col, "row"),
            P(None, "row", col),
            P(None, None, "row", col),
            P(None, col, "row"),
            P(None, "row", col),
            P(None, col, "row"),
            P(tokens, None),
        ),
        out_specs=(
            P(tokens, None),
            P(tokens, None),
            P(None, tokens, None),
            P("row", None, col),
            P(),
            P(),
            P(),
            P(None, "row", col),
            P(None, "row", col),
            P(None, None, "row", col),
            P(None, col, "row"),
            P(None, "row", col),
            P(None, None, "row", col),
            P(None, col, "row"),
            P(None, "row", col),
            P(None, col, "row"),
        ),
        check_vma=False,
    )
```
